128 devices in a mesh: gx: 2 (over core), gy: 2 (over x_hi), gz: 32 (over z, y, x_lo).
Axes of the slice: x: 4 (x_hi: 2, x_lo: 2; x = x_hi * 2 + x_lo), y: 4, z: 4, core: 2. Of those that a mesh axis runs over, the one named last changes fastest.
Arguments:
- populations: float32 [512, 27, 4096], P(('gx', 'gy', 'gz')), may hold values from 0.8 to 1.2
- solid: float32 [512, 4096], P(('gx', 'gy', 'gz')), may hold values from 0 to 1
- block_list: int32 [128, 4], replicated, may hold values from -1 to 3, as said below
- targets: int32 [128, 4], replicated, may hold values from -1 to 511, as said below
Outputs:
- rebalanced: float32 [512, 27, 4096], P(('gx', 'gy', 'gz'))
The draws below stay inside these ranges and needn't reach their ends.
Inputs may be any that keep to these rules, and one draw needn't show every extreme that they name: `block_list`: each row lists the local block positions held in the 4 slots of one device, -1 for an empty slot, no position twice in a row. Every device holds between 2 and 4 blocks; among the devices with a common gx index one holds exactly 2 and another exactly 4. `targets`: an entry is d * 4 + s for the new device d and slot s of the block in that slot, -1 exactly where block_list is -1. A block keeps its slot or goes to a slot that block_list leaves empty on a device with the same gx index; no two blocks share a target; every device sends at most one block away and receives at most one; among the devices with a common gx index at least one block moves.
All inputs are finite; a program needn't handle non-finite values.
Results may differ from the reference program's by a relative error of at most 0.0003.
Values sent between devices are 32-bit elements; how exact they have to be, the bound alone decides.
A program may use at most 192 MiB of HBM per device.

```python
import jax
import jax.numpy as jnp
import numpy as np
from jax import lax

C = 16
RX = 2
RY = 2
RZ = 1
STEPS = 2
CELLS = 4096
BLOCKS = 512
N_GX = 2
N_GY = 2
N_GZ = 32


def layout_tables(key):
    base_key = jax.random.fold_in(key, 11)
    subkeys = jax.random.split(base_key, 6)
    plane_size = N_GY * N_GZ
    device_total = N_GX * plane_size
    places = RX * RY * RZ
    stretch_loads = jax.random.randint(subkeys[0], (N_GX, plane_size), 2, places + 1)
    light_pick = jax.random.randint(subkeys[1], (N_GX, 1), 0, plane_size)
    heavy_pick = (light_pick + jax.random.randint(subkeys[2], (N_GX, 1), 1, plane_size)) % plane_size
    column = jnp.arange(plane_size, dtype=jnp.int32)[None, :]
    stretch_loads = jnp.where(column == light_pick, 2, jnp.where(column == heavy_pick, places, stretch_loads)).astype(jnp.int32)
    flat_loads = stretch_loads.reshape(device_total)
    spread = jnp.arange(places, dtype=jnp.int32)[None, :]
    place_scores = jax.random.randint(subkeys[3], (device_total, places), 0, 1 << 20) * places + spread
    slot_scores = jax.random.randint(subkeys[4], (device_total, places), 0, 1 << 20) * places + spread
    place_order = jnp.argsort(place_scores, axis=1).astype(jnp.int32)
    slot_order = jnp.argsort(slot_scores, axis=1).astype(jnp.int32)
    listed = jnp.where(spread < flat_loads[:, None], place_order, -1).astype(jnp.int32)
    device_rows = jnp.arange(device_total, dtype=jnp.int32)[:, None]
    block_list = jnp.zeros((device_total, places), jnp.int32).at[device_rows, slot_order].set(listed)
    moved_to = jnp.where(block_list >= 0, device_rows * places + spread, -1).astype(jnp.int32)
    ranking = stretch_loads * ((1 << 20) * plane_size) + jax.random.randint(subkeys[5], (N_GX, plane_size), 0, 1 << 20) * plane_size + column
    load_order = jnp.argsort(ranking, axis=1).astype(jnp.int32)
    half_plane = plane_size // 2
    offsets = (jnp.arange(N_GX, dtype=jnp.int32) * plane_size)[:, None]
    light_dev = (load_order[:, :half_plane] + offsets).reshape(-1)
    heavy_dev = (load_order[:, ::-1][:, :half_plane] + offsets).reshape(-1)
    light_load = flat_loads[light_dev]
    heavy_load = flat_loads[heavy_dev]
    shifted = heavy_load > light_load + 1
    send_slot = slot_order[heavy_dev, heavy_load - 1]
    receive_slot = slot_order[light_dev, jnp.minimum(light_load, places - 1)]
    current = moved_to[heavy_dev, send_slot]
    moved_to = moved_to.at[heavy_dev, send_slot].set(jnp.where(shifted, light_dev * places + receive_slot, current).astype(jnp.int32))
    return (block_list, moved_to)


def draw_block_list(key, part):
    return layout_tables(key)[0]


def draw_targets(key, part):
    return layout_tables(key)[1]


def steps_of(key, shape, shards, low, high):
    def one(dim, shards_of):
        steps = jax.random.uniform(jax.random.fold_in(jax.random.fold_in(key, 6), dim), (shards_of,), jnp.float32, low / len(shards), high / len(shards))
        return jnp.repeat(jnp.exp(steps), shape[dim] // shards_of).reshape((-1,) + (1,) * (len(shape) - dim - 1))

    gain = one(*shards[0])
    for cut in shards[1:]:
        gain = gain * one(*cut)
    return gain


def setup_inputs(seed: int = 0) -> dict:
    splits = jax.random.split(jax.random.key(seed), 5)
    return {
        "populations": jnp.clip(0.8 + 0.40000004 * jax.random.uniform(splits[0], (BLOCKS, 27, CELLS), jnp.float32) ** steps_of(splits[0], (BLOCKS, 27, CELLS), ((0, 128),), -0.2, 0.2), 0.8, 1.2),
        "solid": jnp.clip(1.0 * jax.random.uniform(splits[1], (BLOCKS, CELLS), jnp.float32) ** steps_of(splits[1], (BLOCKS, CELLS), ((0, 128),), -0.2, 0.2), 0.0, 1.0),
        "block_list": draw_block_list(jax.random.fold_in(splits[4], 71), 0),
        "targets": draw_targets(jax.random.fold_in(splits[4], 71), 0),
    }


DIRECTIONS = [(first - 1, second - 1, third - 1) for first in range(3) for second in range(3) for third in range(3)]
LEVELS = [8.0 / 27.0, 2.0 / 27.0, 1.0 / 54.0, 1.0 / 216.0]
WEIGHT_TABLE = [LEVELS[abs(offset[0]) + abs(offset[1]) + abs(offset[2])] for offset in DIRECTIONS]
OMEGA = 0.8


def take_rows(group, chosen):
    return jnp.take(group, chosen, axis=0)


def to_dense(values, block_list, span_x, span_y, span_z):
    places = RX * RY * RZ
    slot_total = block_list.shape[1]
    matches = block_list[:, None, :] == jnp.arange(places, dtype=jnp.int32)[None, :, None]
    slot_of = jnp.sum(jnp.where(matches, jnp.arange(slot_total, dtype=jnp.int32)[None, None, :], 0), axis=2).astype(jnp.int32)
    occupied = jnp.any(matches, axis=2)
    per_device = values.reshape((block_list.shape[0], slot_total) + values.shape[1:])
    picked = jax.vmap(take_rows)(per_device, slot_of)
    picked = jnp.where(occupied[:, :, None, None], picked, jnp.zeros((), values.dtype))
    layers = values.shape[1]
    shaped = picked.reshape(span_x, span_y, span_z, RX, RY, RZ, layers, C, C, C)
    shaped = shaped.transpose(6, 0, 3, 7, 1, 4, 8, 2, 5, 9)
    return shaped.reshape(layers, span_x * RX * C, span_y * RY * C, span_z * RZ * C)


def from_dense(dense, block_list, span_x, span_y, span_z):
    layers = dense.shape[0]
    shaped = dense.reshape(layers, span_x, RX, C, span_y, RY, C, span_z, RZ, C)
    shaped = shaped.transpose(1, 4, 7, 2, 5, 8, 0, 3, 6, 9)
    per_place = shaped.reshape(span_x * span_y * span_z, RX * RY * RZ, layers, C * C * C)
    chosen = jnp.maximum(block_list, 0).astype(jnp.int32)
    picked = jax.vmap(take_rows)(per_place, chosen)
    picked = jnp.where(block_list[:, :, None, None] >= 0, picked, jnp.zeros((), dense.dtype))
    return picked.reshape(-1, layers, C * C * C)


def block_presence(block_list, count_x, count_y, count_z):
    places = RX * RY * RZ
    occupied = jnp.any(block_list[:, :, None] == jnp.arange(places, dtype=jnp.int32)[None, None, :], axis=1)
    shaped = occupied.reshape(count_x, count_y, count_z, RX, RY, RZ).transpose(0, 3, 1, 4, 2, 5)
    return shaped.reshape(count_x * RX, count_y * RY, count_z * RZ).astype(jnp.float32)


def collide(current, solid_frac, present):
    weights = jnp.asarray(np.array(WEIGHT_TABLE), dtype=current.dtype)
    velocity = jnp.asarray(np.array(DIRECTIONS).T, dtype=current.dtype)
    highest = lax.Precision.HIGHEST
    density = jnp.einsum("i,ixyz->xyz", weights, current, precision=highest)
    density = jnp.where(present > 0.5, density, jnp.ones((), current.dtype))
    momentum = jnp.einsum("ai,ixyz->axyz", velocity * weights[None, :], current, precision=highest)
    velocity_field = momentum / density[None]
    project = jnp.einsum("ai,axyz->ixyz", velocity, velocity_field, precision=highest)
    square = jnp.sum(velocity_field * velocity_field, axis=0)
    balance = density[None] * (1.0 + 3.0 * project + 4.5 * project * project - 1.5 * square[None])
    relaxed = current + OMEGA * (balance - current)
    return (1.0 - solid_frac)[None] * relaxed + solid_frac[None] * current[::-1]


def propagate(collided, padded, present_ext):
    span_x, span_y, span_z = collided.shape[1], collided.shape[2], collided.shape[3]
    pulled = []
    reached = []
    for direction in range(27):
        offset = DIRECTIONS[direction]
        start_x = 1 - offset[0]
        start_y = 1 - offset[1]
        start_z = 1 - offset[2]
        pulled.append(padded[direction, start_x:start_x + span_x, start_y:start_y + span_y, start_z:start_z + span_z])
        reached.append(present_ext[start_x:start_x + span_x, start_y:start_y + span_y, start_z:start_z + span_z])
    return jnp.where(jnp.stack(reached) > 0.5, jnp.stack(pulled), collided[::-1])


def reference(populations, solid, block_list, targets):
    current = to_dense(populations, block_list, N_GX, N_GY, N_GZ)
    solid_frac = to_dense(solid[:, None, :], block_list, N_GX, N_GY, N_GZ)[0]
    block_grid = block_presence(block_list, N_GX, N_GY, N_GZ)
    cells_on = jnp.repeat(jnp.repeat(jnp.repeat(block_grid, C, axis=0), C, axis=1), C, axis=2)
    present_ext = jnp.pad(cells_on, 1)
    for iteration in range(STEPS):
        collided = collide(current, solid_frac, cells_on)
        padded = jnp.pad(collided, ((0, 0), (1, 1), (1, 1), (1, 1)))
        current = jnp.where(cells_on[None] > 0.5, propagate(collided, padded, present_ext), jnp.zeros((), current.dtype))
    finished = from_dense(current, block_list, N_GX, N_GY, N_GZ)
    flat_targets = targets.reshape(-1)
    destination = jnp.where(flat_targets >= 0, flat_targets, BLOCKS).astype(jnp.int32)
    return jnp.zeros_like(finished).at[destination].set(finished, mode="drop")
```

```python
import jax
import jax.numpy as jnp
from jax import lax
from jax.experimental import pallas as pl
from jax.experimental.pallas import tpu as pltpu
from jax.sharding import PartitionSpec as P

STEPS = 2
GZ = 32
ROW = 64
PIECES = 54
ABSENT = -1.0e30
EDGE = -1.0e29
W0, W1, W2, W3 = 8.0 / 27.0, 2.0 / 27.0, 1.0 / 54.0, 1.0 / 216.0
OMEGA = 0.8
MESH = pl.DeviceIdType.MESH
F32 = jnp.float32


def velocity(i):
    return (i // 9 - 1, (i // 3) % 3 - 1, i % 3 - 1)


def crow(i, yh1, x8):
    return (i * 6 + yh1) * 48 + x8


def grow(i, yh, x):
    return (i * 4 + yh) * 32 + x


def lanes(shape=(8, 128)):
    return lax.broadcasted_iota(jnp.int32, shape, 1)


def roll(value, shift):
    shift = shift % 128
    return value if shift == 0 else pltpu.roll(value, shift, 1)


def collide_tile(load, n, store):
    s, d = {}, {}
    g13 = load(13)
    for j in range(14, 27):
        up, down = load(j), load(26 - j)
        s[j] = up + down
        d[j] = up - down
    level = {1: [], 2: [], 3: []}
    for j in range(14, 27):
        level[sum(abs(c) for c in velocity(j))].append(j)

    def total(values):
        values = list(values)
        while len(values) > 1:
            values = [values[k] + values[k + 1] if k + 1 < len(values) else values[k] for k in range(0, len(values), 2)]
        return values[0]

    rho = W0 * g13 + W1 * total(s[j] for j in level[1]) + W2 * total(s[j] for j in level[2]) + W3 * total(s[j] for j in level[3])
    momentum = []
    for axis in range(3):
        acc = None
        for lev, w in ((1, W1), (2, W2), (3, W3)):
            plus = [d[j] for j in level[lev] if velocity(j)[axis] > 0]
            minus = [d[j] for j in level[lev] if velocity(j)[axis] < 0]
            term = total(plus)
            if minus:
                term = term - total(minus)
            term = w * term
            acc = term if acc is None else acc + term
        momentum.append(acc)
    mx, my, mz = momentum
    rinv = 1.0 / rho
    fluid = 1.0 - n
    a = (1.0 - OMEGA) * fluid
    b = OMEGA * fluid
    p = 0.5 * (a + n)
    q = 0.5 * (a - n)
    e0 = b * (rho - 1.5 * rinv * (mx * mx + my * my + mz * mz))
    k = 4.5 * b * rinv
    b3 = 3.0 * b
    store(13, (a + n) * g13 + e0)
    for j in range(14, 27):
        cx, cy, cz = velocity(j)
        proj = None
        for c, m in ((cx, mx), (cy, my), (cz, mz)):
            if c:
                if proj is None:
                    proj = m if c > 0 else -m
                else:
                    proj = proj + m if c > 0 else proj - m
        even = p * s[j] + (e0 + k * (proj * proj))
        odd = q * d[j] + b3 * proj
        store(j, even + odd)
        store(26 - j, even - odd)


def kernel(
    pops_ref, solid_ref, list_ref, tgt_ref, tgtv_ref, out_ref,
    praw, dense, nsol, coll, zhalo, fin, leave, buf1, buf2, got, srcv, srcs,
    xs, ys, zs, xr, yr, xyr, zr, xzr, yzr, xyzr,
    load_sem, src_sem, send_sem, recv_sem, s1, r1, s2, r2,
):
    ix, iy, iz = lax.axis_index("gx"), lax.axis_index("gy"), lax.axis_index("gz")
    me = iy * GZ + iz
    device = ix * ROW + me
    ox, oy = 1 - ix, 1 - iy
    has_down = iz > 0
    has_up = iz < GZ - 1

    for s in range(4):
        pltpu.make_async_copy(pops_ref.at[s], praw.at[s], load_sem.at[s]).start()

    bar = pltpu.get_barrier_semaphore()

    def greet(k, c):
        t = lax.rem(me + k, ROW)
        pl.semaphore_signal(bar, inc=1, device_id=(ix, t // GZ, lax.rem(t, GZ)), device_id_type=MESH)
        return c

    pl.semaphore_signal(bar, inc=1, device_id=(ox, iy, iz), device_id_type=MESH)
    pl.semaphore_signal(bar, inc=1, device_id=(ox, oy, iz), device_id_type=MESH)

    @pl.when(has_down)
    def _():
        pl.semaphore_signal(bar, inc=1, device_id=(ox, iy, iz - 1), device_id_type=MESH)
        pl.semaphore_signal(bar, inc=1, device_id=(ox, oy, iz - 1), device_id_type=MESH)

    @pl.when(has_up)
    def _():
        pl.semaphore_signal(bar, inc=1, device_id=(ox, iy, iz + 1), device_id_type=MESH)
        pl.semaphore_signal(bar, inc=1, device_id=(ox, oy, iz + 1), device_id_type=MESH)

    lax.fori_loop(1, ROW, greet, 0)

    tg = tgtv_ref[...]
    rows4 = lax.broadcasted_iota(jnp.int32, (128, 4), 0)
    tdev = jnp.where(tg >= 0, lax.shift_right_arithmetic(tg, 2), -1)
    tdev = jnp.where(tdev == rows4, -1, tdev)
    best = None
    for d8 in range(16):
        part = tdev[8 * d8 : 8 * d8 + 8]
        rows = lax.broadcasted_iota(jnp.int32, (8, 128), 0) + 8 * d8
        for s in range(4):
            hit = jnp.where(part[:, s : s + 1] == lanes(), rows, -1)
            best = hit if best is None else jnp.maximum(best, hit)
    for shift in (4, 2, 1):
        best = jnp.maximum(best, pltpu.roll(best, shift, 0))
    srcv[...] = best
    src_copy = pltpu.make_async_copy(srcv, srcs, src_sem)
    src_copy.start()

    none = jnp.full((8, 128), ABSENT, F32)

    def clear_coll(i, c):
        for yh1 in (0, 5):
            for x in range(0, 48, 8):
                coll[pl.ds(crow(i, yh1, x), 8), :] = none
        for yh1 in range(1, 5):
            for x in (0, 40):
                coll[pl.ds(crow(i, yh1, x), 8), :] = none
        return c

    lax.fori_loop(0, 27, clear_coll, 0)

    def clear_z(i, c):
        for yh1 in (0, 5):
            for x in range(0, 48, 8):
                zhalo[pl.ds(crow(i, yh1, x), 8), :] = none
        for yh1 in range(1, 5):
            for x in (0, 40):
                zhalo[pl.ds(crow(i, yh1, x), 8), :] = none
        return c

    lax.fori_loop(0, 18, clear_z, 0)
    for side, missing in ((0, iz == 0), (1, iz == GZ - 1)):

        @pl.when(missing)
        def _():
            for step in range(STEPS):
                for m in range(9):
                    zr[step, side, m] = none
                for m in range(3):
                    xzr[step, side, m] = none
                    yzr[step, side, m] = none
                xyzr[step, side] = none

    for k in range(32):
        nsol[pl.ds((k % 2) * 16 + k // 2, 4, stride=32), :] = solid_ref[:, 128 * k : 128 * k + 128]

    for s in range(4):
        pltpu.make_async_copy(pops_ref.at[s], praw.at[s], load_sem.at[s]).wait()

    def unpack_block(s, c):
        def one(x, c2):
            for yhi in range(2):
                at = pl.multiple_of((2 * x + yhi) * 128, 128)
                for a in range(4):
                    n_dir = 8 if a < 3 else 3
                    dense[pl.ds((s * 32 + 8 * a) * 32 + yhi * 16 + x, n_dir, stride=32), :] = praw[
                        s, 8 * a : 8 * a + n_dir, pl.ds(at, 128)
                    ]
            return c2

        return lax.fori_loop(0, 16, one, c)

    lax.fori_loop(0, 4, unpack_block, 0)

    def slot_of(p):
        slot, there = 0, 0
        for s in range(4):
            match = list_ref[device, s] == p
            slot = jnp.where(match, s, slot)
            there = jnp.where(match, 1, there)
        return slot, there

    def collide(step):
        def tile(t, c):
            p, yhi, xh = t // 4, lax.rem(t // 2, 2), lax.rem(t, 2)
            slot, there = slot_of(p)
            yh = 2 * lax.rem(p, 2) + yhi
            x0 = 16 * (p // 2) + 8 * xh
            inside = jnp.full((8, 128), there, jnp.int32) > 0
            n = nsol[pl.ds(slot * 32 + yhi * 16 + xh * 8, 8), :]
            if step == 0:
                def load(i):
                    return dense[pl.ds((slot * 32 + i) * 32 + yhi * 16 + xh * 8, 8), :]
            else:
                def load(i):
                    return fin[pl.ds(grow(i, yh, x0), 8), :]

            def store(i, value):
                coll[pl.ds(pl.multiple_of(crow(i, yh + 1, 8 + x0), 8), 8), :] = jnp.where(inside, value, ABSENT)

            collide_tile(load, n, store)
            return c

        lax.fori_loop(0, 16, tile, 0)

    def messages(step):
        y_at = 2 * oy
        down, up = iz - 1, iz + 1
        table = [
            (None, xs.at[step], xr.at[step], (ox, iy, iz)),
            (None, ys.at[step], yr.at[step], (ix, oy, iz)),
            (None, xs.at[step, :, y_at], xyr.at[step], (ox, oy, iz)),
            (has_up, zs.at[step, 0], zr.at[step, 0], (ix, iy, up)),
            (has_down, zs.at[step, 1], zr.at[step, 1], (ix, iy, down)),
            (has_up, xs.at[step, 2], xzr.at[step, 0], (ox, iy, up)),
            (has_down, xs.at[step, 0], xzr.at[step, 1], (ox, iy, down)),
            (has_up, ys.at[step, 2], yzr.at[step, 0], (ix, oy, up)),
            (has_down, ys.at[step, 0], yzr.at[step, 1], (ix, oy, down)),
            (has_up, xs.at[step, 2, y_at], xyzr.at[step, 0], (ox, oy, up)),
            (has_down, xs.at[step, 0, y_at], xyzr.at[step, 1], (ox, oy, down)),
        ]
        def copy(m):
            _, src, dst, target = table[m]
            return pltpu.make_async_remote_copy(
                src_ref=src, dst_ref=dst, send_sem=send_sem.at[step, m], recv_sem=recv_sem.at[step, m],
                device_id=target, device_id_type=MESH,
            )

        return [row[0] for row in table], copy

    def guarded(condition, action):
        if condition is None:
            action()
        else:
            pl.when(condition)(action)

    def start(step, which):
        conditions, copy = messages(step)
        for m in which:
            guarded(conditions[m], lambda: copy(m).start())

    def arrive(step, which):
        _, copy = messages(step)
        for m in which:
            condition = None if m < 3 else has_down if m % 2 == 1 else has_up
            guarded(condition, lambda: copy(m).wait_recv())

    lane = lanes()

    def pack_and_send(step):
        row = jnp.where(ix == 0, 39, 8)

        def pack_x(m, c):
            i = 18 * ox + m
            xs[step, lax.rem(m, 3), m // 3, 0:4] = coll[pl.ds(crow(i, 1, row), 4, stride=48), :]
            return c

        lax.fori_loop(0, 9, pack_x, 0)

        def pack_y(m, c):
            i = 9 * (m // 3) + 6 * oy + lax.rem(m, 3)
            yh1 = jnp.where(iy == 0, 4, 1)
            acc = jnp.zeros((8, 128), F32)
            for xo in range(4):
                group = lax.rem(7 * oy - xo + 8, 8)
                value = coll[pl.ds(pl.multiple_of(crow(i, yh1, 8 + 8 * xo), 8), 8), :]
                acc = jnp.where(lax.shift_right_logical(lane, 4) == group, roll(value, -16 * xo), acc)
            ys[step, lax.rem(m, 3), m // 3] = acc
            return c

        lax.fori_loop(0, 9, pack_y, 0)
        start(step, (1, 7, 8, 0, 2, 5, 6, 9, 10))

        def pack_z(m, c):
            up, down = None, None
            for k in range(16):
                yh, xo = k // 4, k % 4
                high = coll[pl.ds(pl.multiple_of(crow(3 * m + 2, yh + 1, 8 + 8 * xo), 8), 8), :]
                low = coll[pl.ds(pl.multiple_of(crow(3 * m, yh + 1, 8 + 8 * xo), 8), 8), :]
                high, low = roll(high, -k), roll(low, k)
                z = lax.bitwise_and(lane, 15)
                up = high if up is None else jnp.where(z == 15 - k, high, up)
                down = low if down is None else jnp.where(z == k, low, down)
            zs[step, 0, m] = up
            zs[step, 1, m] = down
            return c

        lax.fori_loop(0, 9, pack_z, 0)
        start(step, (3, 4))

    def receive(step):
        rowx = jnp.where(ix == 0, 40, 7)
        edge = 5 * oy
        arrive(step, (0, 2))

        def take_x(m, c):
            i = 18 * ix + m
            coll[pl.ds(crow(i, 1, rowx), 4, stride=48), :] = xr[step, lax.rem(m, 3), m // 3, 0:4]
            return c

        lax.fori_loop(0, 9, take_x, 0)
        for cz in range(3):
            i = 18 * ix + 6 * iy + cz
            coll[pl.ds(crow(i, edge, rowx), 1), :] = xyr[step, cz, pl.ds(3 * iy, 1), :]
        arrive(step, (1,))

        def take_y(m, c):
            i = 9 * (m // 3) + 6 * iy + lax.rem(m, 3)
            value = yr[step, lax.rem(m, 3), m // 3]
            for xo in range(4):
                coll[pl.ds(pl.multiple_of(crow(i, edge, 8 + 8 * xo), 8), 8), :] = roll(value, 16 * xo)
            return c

        lax.fori_loop(0, 9, take_y, 0)
        arrive(step, (7, 8, 5, 6, 9, 10))
        for side in range(2):
            turn = -16 if side == 0 else 16
            for cx in range(3):
                m = 9 * side + 3 * cx + 2 * iy
                value = yzr[step, side, cx]
                for xo in range(4):
                    zhalo[pl.ds(pl.multiple_of(crow(m, edge, 8 + 8 * xo), 8), 8), :] = roll(value, turn + 16 * xo)
            for cy in range(3):
                m = 9 * side + 6 * ix + cy
                value = roll(xzr[step, side, cy], turn)
                zhalo[pl.ds(crow(m, 1, rowx), 4, stride=48), :] = value[0:4]
            value = roll(xyzr[step, side], turn)
            first, last = value[0:1], value[3:4]
            m = 9 * side + 6 * ix + 2 * iy
            zhalo[pl.ds(crow(m, edge, rowx), 1), :] = jnp.where(jnp.full((1, 128), iy, jnp.int32) > 0, last, first)
        arrive(step, (3, 4))

        def take_z(m, c):
            below, above = zr[step, 0, m], zr[step, 1, m]
            for k in range(16):
                yh, xo = k // 4, k % 4
                zhalo[pl.ds(pl.multiple_of(crow(m, yh + 1, 8 + 8 * xo), 8), 8), :] = roll(below, k - 16)
                zhalo[pl.ds(pl.multiple_of(crow(9 + m, yh + 1, 8 + 8 * xo), 8), 8), :] = roll(above, 16 - k)
            return c

        lax.fori_loop(0, 9, take_z, 0)

    def propagate_tile(yh, x0, store):
        z15 = lax.bitwise_and(lane, 15) == 15
        z0 = lax.bitwise_and(lane, 15) == 0
        for i in range(27):
            cx, cy, cz = velocity(i)
            here = 8 + x0 - cx
            value = coll[pl.ds(crow(i, yh + 1, here), 8), :]
            if cy:
                other = coll[pl.ds(crow(i, yh + 1 - cy, here), 8), :]
                value = jnp.where(lane >= 112 if cy > 0 else lane < 16, other, value)
            if cz:
                m = i // 3 + (0 if cz > 0 else 9)
                halo = zhalo[pl.ds(crow(m, yh + 1, here), 8), :]
                if cy:
                    other = zhalo[pl.ds(crow(m, yh + 1 - cy, here), 8), :]
                    if cz > 0:
                        at = 111 if cy > 0 else 127
                    else:
                        at = 0 if cy > 0 else 16
                    halo = jnp.where(lane == at, other, halo)
                value = jnp.where(z15 if cz > 0 else z0, halo, value)
            value = roll(value, 16 * cy + cz)
            if i != 13:
                back = coll[pl.ds(crow(26 - i, yh + 1, 8 + x0), 8), :]
                value = jnp.where(value > EDGE, value, back)
            store(i, value)

    def propagate():
        def tile(t, c):
            yh, x0 = t // 4, 8 * lax.rem(t, 4)

            def store(i, value):
                fin[pl.ds(pl.multiple_of(grow(i, yh, x0), 8), 8), :] = value

            propagate_tile(yh, x0, store)
            return c

        lax.fori_loop(0, 16, tile, 0)

    collide(0)
    pl.semaphore_wait(bar, ROW - 1 + 2 + 2 * jnp.where(has_down, 1, 0) + 2 * jnp.where(has_up, 1, 0))
    pack_and_send(0)
    receive(0)
    propagate()
    collide(1)
    pack_and_send(1)

    leaving = 0
    for s in range(4):
        target = tgt_ref[device, s]
        away = jnp.where(target >= 0, jnp.where(lax.shift_right_arithmetic(target, 2) == device, 0, 1), 0)
        leaving = jnp.where(away == 1, jnp.clip(list_ref[device, s], 0, 3), leaving)
    receive(1)

    def leave_tile(t, c):
        yhi, xh = t // 2, lax.rem(t, 2)
        yh = 2 * lax.rem(leaving, 2) + yhi
        x0 = 16 * (leaving // 2) + 8 * xh

        def store(i, value):
            leave[2 * i + yhi, pl.ds(pl.multiple_of(8 * xh, 8), 8), :] = value

        propagate_tile(yh, x0, store)
        return c

    lax.fori_loop(0, 4, leave_tile, 0)

    def spread(k, c):
        t = lax.rem(me + k, ROW)

        @pl.when(t < PIECES)
        def _():
            pltpu.make_async_remote_copy(
                src_ref=leave.at[t], dst_ref=buf1.at[me], send_sem=s1, recv_sem=r1,
                device_id=(ix, t // GZ, lax.rem(t, GZ)), device_id_type=MESH,
            ).start()

        return c

    lax.fori_loop(1, ROW, spread, 0)

    propagate()

    def keep_slot(s, c):
        pos, kept = 0, 0
        for t in range(4):
            match = tgt_ref[device, t] == device * 4 + s
            pos = jnp.where(match, jnp.clip(list_ref[device, t], 0, 3), pos)
            kept = jnp.where(match, 1, kept)
        base = 2 * lax.rem(pos, 2) * 32 + 16 * (pos // 2)
        there = jnp.full((8, 128), kept, jnp.int32) > 0

        def one(x, c2):
            for yhi in range(2):
                at = pl.multiple_of((2 * x + yhi) * 128, 128)
                for a in range(4):
                    n_dir = 8 if a < 3 else 3
                    value = fin[pl.ds(8 * a * 128 + base + yhi * 32 + x, n_dir, stride=128), :]
                    out_ref[s, 8 * a : 8 * a + n_dir, pl.ds(at, 128)] = jnp.where(there[:n_dir], value, 0.0)
            return c2

        return lax.fori_loop(0, 16, one, c)

    lax.fori_loop(0, 4, keep_slot, 0)
    src_copy.wait()

    @pl.when(me < PIECES)
    def _():
        buf1[me] = leave[me]
        pltpu.make_async_copy(buf1.at[pl.ds(0, ROW - 1)], buf1.at[pl.ds(0, ROW - 1)], r1).wait()

        def forward(k, c):
            t = lax.rem(me + k, ROW)
            source = srcs[0, ix * ROW + t]
            buf2[t] = buf1[jnp.clip(source - ix * ROW, 0, ROW - 1)]
            pltpu.make_async_remote_copy(
                src_ref=buf2.at[t], dst_ref=got.at[me], send_sem=s2, recv_sem=r2,
                device_id=(ix, t // GZ, lax.rem(t, GZ)), device_id_type=MESH,
            ).start()
            return c

        lax.fori_loop(1, ROW, forward, 0)
        got[me] = buf1[jnp.clip(srcs[0, device] - ix * ROW, 0, ROW - 1)]
        pltpu.make_async_copy(got.at[pl.ds(0, PIECES - 1)], got.at[pl.ds(0, PIECES - 1)], r2).wait()
        pltpu.make_async_copy(buf2.at[pl.ds(0, ROW - 1)], buf2.at[pl.ds(0, ROW - 1)], s2).wait()
        pltpu.make_async_copy(leave.at[pl.ds(0, PIECES - 1)], leave.at[pl.ds(0, PIECES - 1)], s1).wait()

    @pl.when(me >= PIECES)
    def _():
        pltpu.make_async_copy(got.at[pl.ds(0, PIECES)], got.at[pl.ds(0, PIECES)], r2).wait()
        pltpu.make_async_copy(leave.at[pl.ds(0, PIECES)], leave.at[pl.ds(0, PIECES)], s1).wait()

    source = srcs[0, device]
    new_slot = -1
    for t in range(4):
        target = tgt_ref[jnp.clip(source, 0, 127), t]
        mine = jnp.where(target >= 0, jnp.where(lax.shift_right_arithmetic(target, 2) == device, 1, 0), 0)
        new_slot = jnp.where(mine == 1, lax.bitwise_and(target, 3), new_slot)
    new_slot = jnp.where(source >= 0, new_slot, -1)

    def place(x, c):
        for yhi in range(2):
            at = pl.multiple_of((2 * x + yhi) * 128, 128)
            for a in range(4):
                n_dir = 8 if a < 3 else 3
                value = got_flat(got, a, yhi, x, n_dir)
                for s in range(4):
                    hit = jnp.full((8, 128), new_slot, jnp.int32) == s
                    old = out_ref[s, 8 * a : 8 * a + n_dir, pl.ds(at, 128)]
                    out_ref[s, 8 * a : 8 * a + n_dir, pl.ds(at, 128)] = jnp.where(hit[:n_dir], value, old)
        return c

    lax.fori_loop(0, 16, place, 0)
    for step in range(STEPS):
        conditions, copy = messages(step)
        for m, condition in enumerate(conditions):
            guarded(condition, lambda: copy(m).wait_send())


def got_flat(got, a, yhi, x, n_dir):
    flat = got.reshape(PIECES * 16, 128)
    return flat[pl.ds((8 * a * 2 + yhi) * 16 + x, n_dir, stride=32), :]


def body(populations, solid, block_list, targets):
    vmem = pltpu.VMEM
    tile = (8, 128)
    return pl.pallas_call(
        kernel,
        out_shape=jax.ShapeDtypeStruct((4, 27, 4096), F32),
        in_specs=[
            pl.BlockSpec(memory_space=pl.ANY),
            pl.BlockSpec(memory_space=pltpu.VMEM),
            pl.BlockSpec(memory_space=pltpu.SMEM),
            pl.BlockSpec(memory_space=pltpu.SMEM),
            pl.BlockSpec(memory_space=pltpu.VMEM),
        ],
        out_specs=pl.BlockSpec(memory_space=pltpu.VMEM),
        scratch_shapes=[
            vmem((4, 27, 4096), F32),
            vmem((4 * 32 * 32, 128), F32),
            vmem((4 * 32, 128), F32),
            vmem((27 * 6 * 48, 128), F32),
            vmem((18 * 6 * 48, 128), F32),
            vmem((27 * 4 * 32, 128), F32),
            vmem((PIECES, 16, 128), F32),
            vmem((ROW, 16, 128), F32),
            vmem((ROW, 16, 128), F32),
            vmem((PIECES, 16, 128), F32),
            vmem(tile, jnp.int32),
            pltpu.SMEM(tile, jnp.int32),
            vmem((2, 3, 3) + tile, F32),
            vmem((2, 3, 3) + tile, F32),
            vmem((2, 2, 9) + tile, F32),
            vmem((2, 3, 3) + tile, F32),
            vmem((2, 3, 3) + tile, F32),
            vmem((2, 3) + tile, F32),
            vmem((2, 2, 9) + tile, F32),
            vmem((2, 2, 3) + tile, F32),
            vmem((2, 2, 3) + tile, F32),
            vmem((2, 2) + tile, F32),
            pltpu.SemaphoreType.DMA((4,)),
            pltpu.SemaphoreType.DMA,
            pltpu.SemaphoreType.DMA((STEPS, 11)),
            pltpu.SemaphoreType.DMA((STEPS, 11)),
            pltpu.SemaphoreType.DMA,
            pltpu.SemaphoreType.DMA,
            pltpu.SemaphoreType.DMA,
            pltpu.SemaphoreType.DMA,
        ],
        compiler_params=pltpu.CompilerParams(
            collective_id=0, has_side_effects=True, vmem_limit_bytes=40 * 1024 * 1024
        ),
        name="lattice",
    )(populations, solid, block_list, targets, targets)


def solution(mesh):
    in_specs = (P(("gx", "gy", "gz"), None, None), P(("gx", "gy", "gz"), None), P(), P())
    out_specs = P(("gx", "gy", "gz"), None, None)
    return jax.shard_map(body, mesh=mesh, in_specs=in_specs, out_specs=out_specs, check_vma=False)
```

```python
import jax
import jax.numpy as jnp
from jax import lax
from jax.experimental import pallas as pl
from jax.experimental.pallas import tpu as pltpu
from jax.sharding import PartitionSpec as P

STEPS = 2
GZ = 32
ROW = 64
PIECES = 54
ABSENT = -1.0e30
EDGE = -1.0e29
W0, W1, W2, W3 = 8.0 / 27.0, 2.0 / 27.0, 1.0 / 54.0, 1.0 / 216.0
OMEGA = 0.8
MESH = pl.DeviceIdType.MESH
F32 = jnp.float32


def velocity(i):
    return (i // 9 - 1, (i // 3) % 3 - 1, i % 3 - 1)


def crow(i, yh1, x8):
    return (i * 6 + yh1) * 48 + x8


def grow(i, yh, x):
    return (i * 4 + yh) * 32 + x


def lanes(shape=(8, 128)):
    return lax.broadcasted_iota(jnp.int32, shape, 1)


def roll(value, shift):
    shift = shift % 128
    return value if shift == 0 else pltpu.roll(value, shift, 1)


def collide_tile(load, n, store):
    s, d = {}, {}
    g13 = load(13)
    for j in range(14, 27):
        up, down = load(j), load(26 - j)
        s[j] = up + down
        d[j] = up - down
    level = {1: [], 2: [], 3: []}
    for j in range(14, 27):
        level[sum(abs(c) for c in velocity(j))].append(j)

    def total(values):
        values = list(values)
        while len(values) > 1:
            values = [values[k] + values[k + 1] if k + 1 < len(values) else values[k] for k in range(0, len(values), 2)]
        return values[0]

    rho = W0 * g13 + W1 * total(s[j] for j in level[1]) + W2 * total(s[j] for j in level[2]) + W3 * total(s[j] for j in level[3])
    momentum = []
    for axis in range(3):
        acc = None
        for lev, w in ((1, W1), (2, W2), (3, W3)):
            plus = [d[j] for j in level[lev] if velocity(j)[axis] > 0]
            minus = [d[j] for j in level[lev] if velocity(j)[axis] < 0]
            term = total(plus)
            if minus:
                term = term - total(minus)
            term = w * term
            acc = term if acc is None else acc + term
        momentum.append(acc)
    mx, my, mz = momentum
    rinv = 1.0 / rho
    fluid = 1.0 - n
    a = (1.0 - OMEGA) * fluid
    b = OMEGA * fluid
    p = 0.5 * (a + n)
    q = 0.5 * (a - n)
    e0 = b * (rho - 1.5 * rinv * (mx * mx + my * my + mz * mz))
    k = 4.5 * b * rinv
    b3 = 3.0 * b
    store(13, (a + n) * g13 + e0)
    for j in range(14, 27):
        cx, cy, cz = velocity(j)
        proj = None
        for c, m in ((cx, mx), (cy, my), (cz, mz)):
            if c:
                if proj is None:
                    proj = m if c > 0 else -m
                else:
                    proj = proj + m if c > 0 else proj - m
        even = p * s[j] + (e0 + k * (proj * proj))
        odd = q * d[j] + b3 * proj
        store(j, even + odd)
        store(26 - j, even - odd)


def kernel(
    pops_in, solid_in, list_in, tgt_in, out_ref,
    solid_ref, list_ref, tgt_ref, tgtv_ref, praw, coll, zhalo, fin, leave, buf1, buf2, got, srcv, srcs,
    xs, ys, zs, xr, yr, xyr, zr, xzr, yzr, xyzr,
    load_sem, src_sem, know_sem, send_sem, recv_sem, s1, r1, s2, r2,
):
    ix, iy, iz = lax.axis_index("gx"), lax.axis_index("gy"), lax.axis_index("gz")
    me = iy * GZ + iz
    device = ix * ROW + me
    ox, oy = 1 - ix, 1 - iy
    has_down = iz > 0
    has_up = iz < GZ - 1

    pairs = ((tgt_in, tgtv_ref), (tgt_in, tgt_ref), (list_in, list_ref), (solid_in, solid_ref), (pops_in, praw))
    loads = [pltpu.make_async_copy(src, dst, load_sem.at[k]) for k, (src, dst) in enumerate(pairs)]
    for load in loads:
        load.start()

    bar = pltpu.get_barrier_semaphore()

    def greet(*target):
        pl.semaphore_signal(bar, inc=1, device_id=target, device_id_type=MESH)

    @pl.when(has_down)
    def _():
        for x in (ix, ox):
            for y in (iy, oy):
                greet(x, y, iz - 1)

    @pl.when(has_up)
    def _():
        for x in (ix, ox):
            for y in (iy, oy):
                greet(x, y, iz + 1)

    greet(ix, oy, iz)
    greet(ox, oy, iz)
    greet(ox, iy, iz)
    for bit in (2, 4, 8, 16):
        greet(ix, iy, lax.bitwise_xor(iz, bit))

    partners = [(ix, iy, lax.bitwise_xor(iz, 1 << r)) for r in range(5)] + [(ix, oy, iz)]

    def know_signal(r):
        pl.semaphore_signal(know_sem.at[r], inc=1, device_id=partners[r], device_id_type=MESH)

    def know_wait(r):
        pl.semaphore_wait(know_sem.at[r], 1)

    lane = lanes()

    none = jnp.full((8, 128), ABSENT, F32)

    def clear_coll(i, c):
        for yh1 in (0, 5):
            for x in range(0, 48, 8):
                coll[pl.ds(crow(i, yh1, x), 8), :] = none
        for yh1 in range(1, 5):
            for x in (0, 40):
                coll[pl.ds(crow(i, yh1, x), 8), :] = none
        return c

    lax.fori_loop(0, 27, clear_coll, 0)

    def clear_z(i, c):
        for yh1 in (0, 5):
            for x in range(0, 48, 8):
                zhalo[pl.ds(crow(i, yh1, x), 8), :] = none
        for yh1 in range(1, 5):
            for x in (0, 40):
                zhalo[pl.ds(crow(i, yh1, x), 8), :] = none
        return c

    lax.fori_loop(0, 18, clear_z, 0)
    for side, missing in ((0, iz == 0), (1, iz == GZ - 1)):

        @pl.when(missing)
        def _():
            for step in range(STEPS):
                for m in range(9):
                    zr[step, side, m] = none
                for m in range(3):
                    xzr[step, side, m] = none
                    yzr[step, side, m] = none
                xyzr[step, side] = none

    loads[0].wait()
    tg = tgtv_ref[...]
    sender = lanes((4, 128))
    tdev = jnp.where(tg >= 0, lax.shift_right_arithmetic(tg, 2), -1)
    tdev = jnp.where(tdev == sender, -1, tdev) - ix * ROW
    table = jnp.full((8, 128), -1, jnp.int32)
    for t8 in range(8):
        rows = lax.broadcasted_iota(jnp.int32, (8, 128), 0) + 8 * t8
        best = jnp.full((8, 128), -1, jnp.int32)
        for s in range(4):
            best = jnp.where(tdev[s : s + 1] == rows, lane, best)
        for shift in (64, 32, 16, 8, 4, 2, 1):
            best = jnp.maximum(best, pltpu.roll(best, shift, 1))
        table = jnp.where(lane == t8, best, table)
    srcv[...] = table
    src_copy = pltpu.make_async_copy(srcv, srcs, src_sem)
    src_copy.start()

    def raw_row(i, slot, yhi, x):
        return (i * 32 + 2 * x + yhi) * 4 + slot

    def slot_of(p):
        slot, there = 0, 0
        for s in range(4):
            match = list_ref[s, device] == p
            slot = jnp.where(match, s, slot)
            there = jnp.where(match, 1, there)
        return slot, there

    def collide(step):
        def tile(t, c):
            p, yhi, xh = t // 4, lax.rem(t // 2, 2), lax.rem(t, 2)
            slot, there = slot_of(p)
            yh = 2 * lax.rem(p, 2) + yhi
            x0 = 16 * (p // 2) + 8 * xh
            inside = jnp.full((8, 128), there, jnp.int32) > 0
            n = solid_ref[pl.ds(raw_row(0, slot, yhi, 8 * xh), 8, stride=8), :]
            if step == 0:
                def load(i):
                    return praw[pl.ds(raw_row(i, slot, yhi, 8 * xh), 8, stride=8), :]
            else:
                def load(i):
                    return fin[pl.ds(grow(i, yh, x0), 8), :]

            def store(i, value):
                coll[pl.ds(pl.multiple_of(crow(i, yh + 1, 8 + x0), 8), 8), :] = jnp.where(inside, value, ABSENT)

            collide_tile(load, n, store)
            return c

        lax.fori_loop(0, 16, tile, 0)

    def messages(step):
        y_at = 2 * oy
        down, up = iz - 1, iz + 1
        table = [
            (None, xs.at[step], xr.at[step], (ox, iy, iz)),
            (None, ys.at[step], yr.at[step], (ix, oy, iz)),
            (None, xs.at[step, :, y_at], xyr.at[step], (ox, oy, iz)),
            (has_up, zs.at[step, 0], zr.at[step, 0], (ix, iy, up)),
            (has_down, zs.at[step, 1], zr.at[step, 1], (ix, iy, down)),
            (has_up, xs.at[step, 2], xzr.at[step, 0], (ox, iy, up)),
            (has_down, xs.at[step, 0], xzr.at[step, 1], (ox, iy, down)),
            (has_up, ys.at[step, 2], yzr.at[step, 0], (ix, oy, up)),
            (has_down, ys.at[step, 0], yzr.at[step, 1], (ix, oy, down)),
            (has_up, xs.at[step, 2, y_at], xyzr.at[step, 0], (ox, oy, up)),
            (has_down, xs.at[step, 0, y_at], xyzr.at[step, 1], (ox, oy, down)),
        ]
        def copy(m):
            _, src, dst, target = table[m]
            return pltpu.make_async_remote_copy(
                src_ref=src, dst_ref=dst, send_sem=send_sem.at[step, m], recv_sem=recv_sem.at[step, m],
                device_id=target, device_id_type=MESH,
            )

        return [row[0] for row in table], copy

    def guarded(condition, action):
        if condition is None:
            action()
        else:
            pl.when(condition)(action)

    def start(step, which):
        conditions, copy = messages(step)
        for m in which:
            guarded(conditions[m], lambda: copy(m).start())

    def arrive(step, which):
        _, copy = messages(step)
        for m in which:
            condition = None if m < 3 else has_down if m % 2 == 1 else has_up
            guarded(condition, lambda: copy(m).wait_recv())

    def pack_and_send(step):
        row = jnp.where(ix == 0, 39, 8)

        def pack_x(m, c):
            i = 18 * ox + m
            xs[step, lax.rem(m, 3), m // 3, 0:4] = coll[pl.ds(crow(i, 1, row), 4, stride=48), :]
            return c

        def pack_y(m, c):
            i = 9 * (m // 3) + 6 * oy + lax.rem(m, 3)
            yh1 = jnp.where(iy == 0, 4, 1)
            acc = jnp.zeros((8, 128), F32)
            for xo in range(4):
                group = lax.rem(7 * oy - xo + 8, 8)
                value = coll[pl.ds(pl.multiple_of(crow(i, yh1, 8 + 8 * xo), 8), 8), :]
                acc = jnp.where(lax.shift_right_logical(lane, 4) == group, roll(value, -16 * xo), acc)
            ys[step, lax.rem(m, 3), m // 3] = acc
            return c

        lax.fori_loop(0, 9, pack_y, 0, unroll=True)
        start(step, (7, 8, 1))
        lax.fori_loop(0, 9, pack_x, 0, unroll=True)
        start(step, (9, 10, 2, 5, 6, 0))

        def pack_z(m, c):
            up, down = None, None
            for k in range(16):
                yh, xo = k // 4, k % 4
                high = coll[pl.ds(pl.multiple_of(crow(3 * m + 2, yh + 1, 8 + 8 * xo), 8), 8), :]
                low = coll[pl.ds(pl.multiple_of(crow(3 * m, yh + 1, 8 + 8 * xo), 8), 8), :]
                high, low = roll(high, -k), roll(low, k)
                z = lax.bitwise_and(lane, 15)
                up = high if up is None else jnp.where(z == 15 - k, high, up)
                down = low if down is None else jnp.where(z == k, low, down)
            zs[step, 0, m] = up
            zs[step, 1, m] = down
            return c

        lax.fori_loop(0, 9, pack_z, 0, unroll=3)
        start(step, (3, 4))

    def receive(step):
        rowx = jnp.where(ix == 0, 40, 7)
        edge = 5 * oy
        arrive(step, (0, 2))

        def take_x(m, c):
            i = 18 * ix + m
            coll[pl.ds(crow(i, 1, rowx), 4, stride=48), :] = xr[step, lax.rem(m, 3), m // 3, 0:4]
            return c

        lax.fori_loop(0, 9, take_x, 0, unroll=True)
        for cz in range(3):
            i = 18 * ix + 6 * iy + cz
            coll[pl.ds(crow(i, edge, rowx), 1), :] = xyr[step, cz, pl.ds(3 * iy, 1), :]
        arrive(step, (3, 4))

        def take_z(m, c):
            below, above = zr[step, 0, m], zr[step, 1, m]
            for k in range(16):
                yh, xo = k // 4, k % 4
                zhalo[pl.ds(pl.multiple_of(crow(m, yh + 1, 8 + 8 * xo), 8), 8), :] = roll(below, k - 16)
                zhalo[pl.ds(pl.multiple_of(crow(9 + m, yh + 1, 8 + 8 * xo), 8), 8), :] = roll(above, 16 - k)
            return c

        lax.fori_loop(0, 9, take_z, 0, unroll=3)
        arrive(step, (1,))

        def take_y(m, c):
            i = 9 * (m // 3) + 6 * iy + lax.rem(m, 3)
            value = yr[step, lax.rem(m, 3), m // 3]
            for xo in range(4):
                coll[pl.ds(pl.multiple_of(crow(i, edge, 8 + 8 * xo), 8), 8), :] = roll(value, 16 * xo)
            return c

        lax.fori_loop(0, 9, take_y, 0, unroll=True)
        arrive(step, (7, 8, 5, 6, 9, 10))
        for side in range(2):
            turn = -16 if side == 0 else 16
            for cx in range(3):
                m = 9 * side + 3 * cx + 2 * iy
                value = yzr[step, side, cx]
                for xo in range(4):
                    zhalo[pl.ds(pl.multiple_of(crow(m, edge, 8 + 8 * xo), 8), 8), :] = roll(value, turn + 16 * xo)
            for cy in range(3):
                m = 9 * side + 6 * ix + cy
                value = roll(xzr[step, side, cy], turn)
                zhalo[pl.ds(crow(m, 1, rowx), 4, stride=48), :] = value[0:4]
            value = roll(xyzr[step, side], turn)
            first, last = value[0:1], value[3:4]
            m = 9 * side + 6 * ix + 2 * iy
            zhalo[pl.ds(crow(m, edge, rowx), 1), :] = jnp.where(jnp.full((1, 128), iy, jnp.int32) > 0, last, first)

    def propagate_tile(yh, x0, store):
        z15 = lax.bitwise_and(lane, 15) == 15
        z0 = lax.bitwise_and(lane, 15) == 0
        for i in range(27):
            cx, cy, cz = velocity(i)
            here = 8 + x0 - cx
            value = coll[pl.ds(crow(i, yh + 1, here), 8), :]
            if cy:
                other = coll[pl.ds(crow(i, yh + 1 - cy, here), 8), :]
                value = jnp.where(lane >= 112 if cy > 0 else lane < 16, other, value)
            if cz:
                m = i // 3 + (0 if cz > 0 else 9)
                halo = zhalo[pl.ds(crow(m, yh + 1, here), 8), :]
                if cy:
                    other = zhalo[pl.ds(crow(m, yh + 1 - cy, here), 8), :]
                    if cz > 0:
                        at = 111 if cy > 0 else 127
                    else:
                        at = 0 if cy > 0 else 16
                    halo = jnp.where(lane == at, other, halo)
                value = jnp.where(z15 if cz > 0 else z0, halo, value)
            value = roll(value, 16 * cy + cz)
            if i != 13:
                back = coll[pl.ds(crow(26 - i, yh + 1, 8 + x0), 8), :]
                value = jnp.where(value > EDGE, value, back)
            store(i, value)

    def propagate():
        def tile(t, c):
            yh, x0 = t // 4, 8 * lax.rem(t, 4)

            def store(i, value):
                fin[pl.ds(pl.multiple_of(grow(i, yh, x0), 8), 8), :] = value

            propagate_tile(yh, x0, store)
            return c

        lax.fori_loop(0, 16, tile, 0)

    for load in loads[1:]:
        load.wait()
    collide(0)
    pl.semaphore_wait(bar, 7 + 4 * jnp.where(has_down, 1, 0) + 4 * jnp.where(has_up, 1, 0))
    know_signal(0)
    pack_and_send(0)
    know_wait(0)
    know_signal(1)
    receive(0)
    know_wait(1)
    know_signal(2)
    propagate()
    know_wait(2)
    know_signal(3)
    collide(1)
    know_wait(3)
    know_signal(4)
    pack_and_send(1)
    know_wait(4)
    know_signal(5)

    leaving = 0
    for s in range(4):
        target = tgt_ref[s, device]
        away = jnp.where(target >= 0, jnp.where(lax.shift_right_arithmetic(target, 2) == device, 0, 1), 0)
        leaving = jnp.where(away == 1, jnp.clip(list_ref[s, device], 0, 3), leaving)
    receive(1)

    def leave_tile(t, c):
        yhi, xh = t // 2, lax.rem(t, 2)
        yh = 2 * lax.rem(leaving, 2) + yhi
        x0 = 16 * (leaving // 2) + 8 * xh

        def store(i, value):
            leave[2 * i + yhi, pl.ds(pl.multiple_of(8 * xh, 8), 8), :] = value

        propagate_tile(yh, x0, store)
        return c

    lax.fori_loop(0, 4, leave_tile, 0)

    def piece_of(t):
        return t - (t + ix) // 6, lax.rem(t + ix, 6) != 5

    know_wait(5)

    def spread(k, c):
        t = lax.bitwise_xor(me, ROW - k)
        piece, used = piece_of(t)

        @pl.when(used)
        def _():
            pltpu.make_async_remote_copy(
                src_ref=leave.at[piece], dst_ref=buf1.at[me], send_sem=s1, recv_sem=r1,
                device_id=(ix, t // GZ, lax.rem(t, GZ)), device_id_type=MESH,
            ).start()

        return c

    lax.fori_loop(1, ROW, spread, 0)

    def keep_tile(t, c):
        s, yhi, xh = t // 4, lax.rem(t // 2, 2), lax.rem(t, 2)
        pos, kept = 0, 0
        for k in range(4):
            match = tgt_ref[k, device] == device * 4 + s
            pos = jnp.where(match, jnp.clip(list_ref[k, device], 0, 3), pos)
            kept = jnp.where(match, 1, kept)
        there = jnp.full((8, 128), kept, jnp.int32) > 0

        def store(i, value):
            out_ref[pl.ds(raw_row(i, s, yhi, 8 * xh), 8, stride=8), :] = jnp.where(there, value, 0.0)

        propagate_tile(2 * lax.rem(pos, 2) + yhi, 16 * (pos // 2) + 8 * xh, store)
        return c

    lax.fori_loop(0, 16, keep_tile, 0)
    src_copy.wait()

    own, passes = piece_of(me)

    @pl.when(passes)
    def _():
        buf1[me] = leave[own]
        pltpu.make_async_copy(buf1.at[pl.ds(0, ROW - 1)], buf1.at[pl.ds(0, ROW - 1)], r1).wait()

        def forward(k, c):
            t = lax.bitwise_xor(me, ROW - k)
            source = srcs[lax.rem(t, 8), t // 8]
            buf2[t] = buf1[jnp.clip(source - ix * ROW, 0, ROW - 1)]
            pltpu.make_async_remote_copy(
                src_ref=buf2.at[t], dst_ref=got.at[own], send_sem=s2, recv_sem=r2,
                device_id=(ix, t // GZ, lax.rem(t, GZ)), device_id_type=MESH,
            ).start()
            return c

        lax.fori_loop(1, ROW, forward, 0)
        got[own] = buf1[jnp.clip(srcs[lax.rem(me, 8), me // 8] - ix * ROW, 0, ROW - 1)]
        pltpu.make_async_copy(got.at[pl.ds(0, PIECES - 1)], got.at[pl.ds(0, PIECES - 1)], r2).wait()
        pltpu.make_async_copy(buf2.at[pl.ds(0, ROW - 1)], buf2.at[pl.ds(0, ROW - 1)], s2).wait()
        pltpu.make_async_copy(leave.at[pl.ds(0, PIECES - 1)], leave.at[pl.ds(0, PIECES - 1)], s1).wait()

    @pl.when(jnp.logical_not(passes))
    def _():
        pltpu.make_async_copy(got.at[pl.ds(0, PIECES)], got.at[pl.ds(0, PIECES)], r2).wait()
        pltpu.make_async_copy(leave.at[pl.ds(0, PIECES)], leave.at[pl.ds(0, PIECES)], s1).wait()

    source = srcs[lax.rem(me, 8), me // 8]
    new_slot = -1
    for t in range(4):
        target = tgt_ref[t, jnp.clip(source, 0, 127)]
        mine = jnp.where(target >= 0, jnp.where(lax.shift_right_arithmetic(target, 2) == device, 1, 0), 0)
        new_slot = jnp.where(mine == 1, lax.bitwise_and(target, 3), new_slot)
    new_slot = jnp.where(source >= 0, new_slot, -1)

    def place(j, c):
        i, yhi = j // 2, lax.rem(j, 2)
        for xh in range(2):
            value = got[j, 8 * xh : 8 * xh + 8]
            for s in range(4):
                at = pl.ds(raw_row(i, s, yhi, 8 * xh), 8, stride=8)
                hit = jnp.full((8, 128), new_slot, jnp.int32) == s
                out_ref[at, :] = jnp.where(hit, value, out_ref[at, :])
        return c

    lax.fori_loop(0, PIECES, place, 0)
    for step in range(STEPS):
        conditions, copy = messages(step)
        for m, condition in enumerate(conditions):
            guarded(condition, lambda: copy(m).wait_send())


def body(populations, solid, block_list, targets):
    vmem = pltpu.VMEM
    tile = (8, 128)
    rows = populations.reshape(4, 27, 32, 128).transpose(1, 2, 0, 3).reshape(27 * 32 * 4, 128)
    cells = solid.reshape(4, 32, 128).transpose(1, 0, 2).reshape(32 * 4, 128)
    out = pl.pallas_call(
        kernel,
        out_shape=jax.ShapeDtypeStruct((27 * 32 * 4, 128), F32),
        in_specs=[pl.BlockSpec(memory_space=pl.ANY)] * 4,
        out_specs=pl.BlockSpec(memory_space=pltpu.VMEM),
        scratch_shapes=[
            vmem((128, 128), F32),
            pltpu.SMEM((4, 128), jnp.int32),
            pltpu.SMEM((4, 128), jnp.int32),
            vmem((4, 128), jnp.int32),
            vmem((27 * 32 * 4, 128), F32),
            vmem((27 * 6 * 48, 128), F32),
            vmem((18 * 6 * 48, 128), F32),
            vmem((27 * 4 * 32, 128), F32),
            vmem((PIECES, 16, 128), F32),
            vmem((ROW, 16, 128), F32),
            vmem((ROW, 16, 128), F32),
            vmem((PIECES, 16, 128), F32),
            vmem(tile, jnp.int32),
            pltpu.SMEM(tile, jnp.int32),
            vmem((2, 3, 3) + tile, F32),
            vmem((2, 3, 3) + tile, F32),
            vmem((2, 2, 9) + tile, F32),
            vmem((2, 3, 3) + tile, F32),
            vmem((2, 3, 3) + tile, F32),
            vmem((2, 3) + tile, F32),
            vmem((2, 2, 9) + tile, F32),
            vmem((2, 2, 3) + tile, F32),
            vmem((2, 2, 3) + tile, F32),
            vmem((2, 2) + tile, F32),
            pltpu.SemaphoreType.DMA((5,)),
            pltpu.SemaphoreType.DMA,
            pltpu.SemaphoreType.REGULAR((6,)),
            pltpu.SemaphoreType.DMA((STEPS, 11)),
            pltpu.SemaphoreType.DMA((STEPS, 11)),
            pltpu.SemaphoreType.DMA,
            pltpu.SemaphoreType.DMA,
            pltpu.SemaphoreType.DMA,
            pltpu.SemaphoreType.DMA,
        ],
        compiler_params=pltpu.CompilerParams(
            collective_id=0, has_side_effects=True, vmem_limit_bytes=58 * 1024 * 1024
        ),
        name="lattice",
    )(rows, cells, block_list.T, targets.T)
    return out.reshape(27, 32, 4, 128).transpose(2, 0, 1, 3).reshape(4, 27, 4096)


def solution(mesh):
    in_specs = (P(("gx", "gy", "gz"), None, None), P(("gx", "gy", "gz"), None), P(), P())
    out_specs = P(("gx", "gy", "gz"), None, None)
    return jax.shard_map(body, mesh=mesh, in_specs=in_specs, out_specs=out_specs, check_vma=False)
```

```python
import jax
import jax.numpy as jnp
from jax import lax
from jax.experimental import pallas as pl
from jax.experimental.pallas import tpu as pltpu
from jax.sharding import PartitionSpec as P

STEPS = 2
GZ = 32
ROW = 64
PIECES = 54
ABSENT = -1.0e30
EDGE = -1.0e29
W0, W1, W2, W3 = 8.0 / 27.0, 2.0 / 27.0, 1.0 / 54.0, 1.0 / 216.0
OMEGA = 0.8
MESH = pl.DeviceIdType.MESH
F32 = jnp.float32


def velocity(i):
    return (i // 9 - 1, (i // 3) % 3 - 1, i % 3 - 1)


def crow(i, yh1, x8):
    return (i * 6 + yh1) * 48 + x8


def grow(i, yh, x):
    return (i * 4 + yh) * 32 + x


DIRS = range(27)
FACES_X = [(i, yhi) for i in DIRS if velocity(i)[0] for yhi in range(2)]
FACES_Y = [(i, xh) for i in DIRS if velocity(i)[1] for xh in range(2)]
FACES_Z = [(i, yhi, xh) for i in DIRS if velocity(i)[2] for yhi in range(2) for xh in range(2)]
EDGE_PIECES = 8


def lanes(shape=(8, 128)):
    return lax.broadcasted_iota(jnp.int32, shape, 1)


def roll(value, shift):
    shift = shift % 128
    return value if shift == 0 else pltpu.roll(value, shift, 1)


def collide_tile(load, n, store):
    s, d = {}, {}
    g13 = load(13)
    for j in range(14, 27):
        up, down = load(j), load(26 - j)
        s[j] = up + down
        d[j] = up - down
    level = {1: [], 2: [], 3: []}
    for j in range(14, 27):
        level[sum(abs(c) for c in velocity(j))].append(j)

    def total(values):
        values = list(values)
        while len(values) > 1:
            values = [values[k] + values[k + 1] if k + 1 < len(values) else values[k] for k in range(0, len(values), 2)]
        return values[0]

    rho = W0 * g13 + W1 * total(s[j] for j in level[1]) + W2 * total(s[j] for j in level[2]) + W3 * total(s[j] for j in level[3])
    momentum = []
    for axis in range(3):
        acc = None
        for lev, w in ((1, W1), (2, W2), (3, W3)):
            plus = [d[j] for j in level[lev] if velocity(j)[axis] > 0]
            minus = [d[j] for j in level[lev] if velocity(j)[axis] < 0]
            term = total(plus)
            if minus:
                term = term - total(minus)
            term = w * term
            acc = term if acc is None else acc + term
        momentum.append(acc)
    mx, my, mz = momentum
    rinv = 1.0 / rho
    fluid = 1.0 - n
    a = (1.0 - OMEGA) * fluid
    b = OMEGA * fluid
    p = 0.5 * (a + n)
    q = 0.5 * (a - n)
    e0 = b * (rho - 1.5 * rinv * (mx * mx + my * my + mz * mz))
    k = 4.5 * b * rinv
    b3 = 3.0 * b
    store(13, (a + n) * g13 + e0)
    for j in range(14, 27):
        cx, cy, cz = velocity(j)
        proj = None
        for c, m in ((cx, mx), (cy, my), (cz, mz)):
            if c:
                if proj is None:
                    proj = m if c > 0 else -m
                else:
                    proj = proj + m if c > 0 else proj - m
        even = p * s[j] + (e0 + k * (proj * proj))
        odd = q * d[j] + b3 * proj
        store(j, even + odd)
        store(26 - j, even - odd)


def kernel(
    pops_in, solid_in, list_in, tgt_in, kept_out, got, edge_got,
    solid_ref, list_ref, tgt_ref, tgtv_ref, praw, coll, zhalo, fin, kept, leave, leave2, bnd, buf1, buf2, srcv, srcs,
    xs, ys, zs, es, xr, yr, zr, er,
    load_sem, src_sem, know_sem, send_sem, recv_sem, s1, r1, s2, r2, s3, r3, s4, r4,
):
    ix, iy, iz = lax.axis_index("gx"), lax.axis_index("gy"), lax.axis_index("gz")
    me = iy * GZ + iz
    device = ix * ROW + me
    ox, oy = 1 - ix, 1 - iy
    has_down = iz > 0
    has_up = iz < GZ - 1

    pairs = ((tgt_in, tgtv_ref), (tgt_in, tgt_ref), (list_in, list_ref), (solid_in, solid_ref), (pops_in, praw))
    loads = [pltpu.make_async_copy(src, dst, load_sem.at[k]) for k, (src, dst) in enumerate(pairs)]
    for load in loads:
        load.start()

    bar = pltpu.get_barrier_semaphore()

    def greet(*target):
        pl.semaphore_signal(bar, inc=1, device_id=target, device_id_type=MESH)

    @pl.when(has_down)
    def _():
        for x in (ix, ox):
            for y in (iy, oy):
                greet(x, y, iz - 1)

    @pl.when(has_up)
    def _():
        for x in (ix, ox):
            for y in (iy, oy):
                greet(x, y, iz + 1)

    greet(ix, oy, iz)
    greet(ox, oy, iz)
    greet(ox, iy, iz)

    def flipped(bits):
        return (ix, iy, lax.bitwise_xor(iz, bits))

    rounds = [
        [flipped(1), flipped(2), flipped(3)],
        [flipped(4), flipped(8), flipped(12)],
        [(ix, oy, iz), flipped(16), (ix, oy, lax.bitwise_xor(iz, 16))],
    ]
    for bits in (2, 3, 4, 8, 12, 16):
        greet(*flipped(bits))
    greet(*rounds[2][2])

    def know_signal(r):
        for target in rounds[r]:
            pl.semaphore_signal(know_sem.at[r], inc=1, device_id=target, device_id_type=MESH)

    def know_wait(r):
        pl.semaphore_wait(know_sem.at[r], 3)

    lane = lanes()

    none = jnp.full((8, 128), ABSENT, F32)

    def clear_coll(i, c):
        for yh1 in (0, 5):
            for x in range(0, 48, 8):
                coll[pl.ds(crow(i, yh1, x), 8), :] = none
        for yh1 in range(1, 5):
            for x in (0, 40):
                coll[pl.ds(crow(i, yh1, x), 8), :] = none
        return c

    lax.fori_loop(0, 27, clear_coll, 0)

    def clear_z(i, c):
        for yh1 in (0, 5):
            for x in range(0, 48, 8):
                zhalo[pl.ds(crow(i, yh1, x), 8), :] = none
        for yh1 in range(1, 5):
            for x in (0, 40):
                zhalo[pl.ds(crow(i, yh1, x), 8), :] = none
        return c

    lax.fori_loop(0, 18, clear_z, 0)
    for side, missing in ((0, iz == 0), (1, iz == GZ - 1)):

        @pl.when(missing)
        def _():
            for step in range(STEPS):
                for m in range(9):
                    zr[step, side, m] = none
                for m in (1, 3, 5):
                    er[step, m + side] = none

    loads[0].wait()
    tg = tgtv_ref[...]
    sender = lanes((4, 128))
    tdev = jnp.where(tg >= 0, lax.shift_right_arithmetic(tg, 2), -1)
    tdev = jnp.where(tdev == sender, -1, tdev) - ix * ROW
    table = jnp.full((8, 128), -1, jnp.int32)
    for t8 in range(8):
        rows = lax.broadcasted_iota(jnp.int32, (8, 128), 0) + 8 * t8
        best = jnp.full((8, 128), -1, jnp.int32)
        for s in range(4):
            best = jnp.where(tdev[s : s + 1] == rows, lane, best)
        for shift in (64, 32, 16, 8, 4, 2, 1):
            best = jnp.maximum(best, pltpu.roll(best, shift, 1))
        table = jnp.where(lane == t8, best, table)
    srcv[...] = table
    src_copy = pltpu.make_async_copy(srcv, srcs, src_sem)
    src_copy.start()

    def raw_row(i, slot, yhi, x):
        return (i * 32 + 2 * x + yhi) * 4 + slot

    def slot_of(p):
        slot, there = 0, 0
        for s in range(4):
            match = list_ref[s, device] == p
            slot = jnp.where(match, s, slot)
            there = jnp.where(match, 1, there)
        return slot, there

    def collide(step):
        def tile(t, c):
            p, yhi, xh = t // 4, lax.rem(t // 2, 2), lax.rem(t, 2)
            slot, there = slot_of(p)
            yh = 2 * lax.rem(p, 2) + yhi
            x0 = 16 * (p // 2) + 8 * xh
            inside = jnp.full((8, 128), there, jnp.int32) > 0
            n = solid_ref[pl.ds(raw_row(0, slot, yhi, 8 * xh), 8, stride=8), :]
            if step == 0:
                def load(i):
                    return praw[pl.ds(raw_row(i, slot, yhi, 8 * xh), 8, stride=8), :]
            else:
                def load(i):
                    return fin[pl.ds(grow(i, yh, x0), 8), :]

            def store(i, value):
                coll[pl.ds(pl.multiple_of(crow(i, yh + 1, 8 + x0), 8), 8), :] = jnp.where(inside, value, ABSENT)

            collide_tile(load, n, store)
            return c

        lax.fori_loop(0, 16, tile, 0)

    def messages(step):
        down, up = iz - 1, iz + 1
        edges, far = es.at[step], er.at[step]
        table = [
            (None, xs.at[step], xr.at[step], (ox, iy, iz)),
            (None, ys.at[step], yr.at[step], (ix, oy, iz)),
            (None, edges.at[0], far.at[0], (ox, oy, iz)),
            (has_up, zs.at[step, 0], zr.at[step, 0], (ix, iy, up)),
            (has_down, zs.at[step, 1], zr.at[step, 1], (ix, iy, down)),
            (has_up, edges.at[1], far.at[1], (ox, iy, up)),
            (has_down, edges.at[2], far.at[2], (ox, iy, down)),
            (has_up, edges.at[3], far.at[3], (ix, oy, up)),
            (has_down, edges.at[4], far.at[4], (ix, oy, down)),
            (has_up, edges.at[5], far.at[5], (ox, oy, up)),
            (has_down, edges.at[6], far.at[6], (ox, oy, down)),
        ]

        def copy(m):
            _, src, dst, target = table[m]
            return pltpu.make_async_remote_copy(
                src_ref=src, dst_ref=dst, send_sem=send_sem.at[step, m], recv_sem=recv_sem.at[step, m],
                device_id=target, device_id_type=MESH,
            )

        return [row[0] for row in table], copy

    def guarded(condition, action):
        if condition is None:
            action()
        else:
            pl.when(condition)(action)

    def start(step, which):
        conditions, copy = messages(step)
        for m in which:
            guarded(conditions[m], lambda: copy(m).start())

    def arrive(step, which):
        _, copy = messages(step)
        for m in which:
            condition = None if m < 3 else has_down if m % 2 == 1 else has_up
            guarded(condition, lambda: copy(m).wait_recv())

    def pack_and_send(step):
        row = jnp.where(ix == 0, 39, 8)
        yh1 = 1 + 3 * oy
        z = lax.bitwise_and(lane, 15)
        group = lax.shift_right_logical(lane, 4)
        slots = [group == lax.rem(7 * oy - xo + 8, 8) for xo in range(4)]
        own_half = jnp.logical_or(jnp.logical_or(slots[0], slots[1]), jnp.logical_or(slots[2], slots[3]))

        halves = []
        for d in range(9):
            cz, cx = d // 3, d % 3
            i = 9 * cx + 6 * oy + cz
            acc = None
            for xo in range(4):
                value = roll(coll[pl.ds(pl.multiple_of(crow(i, yh1, 8 + 8 * xo), 8), 8), :], -16 * xo)
                acc = value if acc is None else jnp.where(slots[xo], value, acc)
            halves.append(acc)

        def merge(values, step_of, home):
            acc = values[0]
            for k in (1, 2):
                acc = jnp.where(z == home + k * step_of, roll(values[k], k * step_of), acc)
            return acc

        es[step, 3] = merge(halves[6:9], -1, 15)
        es[step, 4] = merge(halves[0:3], 1, 0)
        start(step, (7, 8))
        for v in range(5):
            tile = halves[2 * v]
            if v < 4:
                tile = jnp.where(own_half, tile, roll(halves[2 * v + 1], -64))
            ys[step, v] = tile
        start(step, (1,))

        for cz in range(3):
            es[step, 0, cz : cz + 1] = coll[pl.ds(crow(18 * ox + 6 * oy + cz, yh1, row), 1), :]
        for side in range(2):
            es[step, 5 + side, 0:1] = coll[pl.ds(crow(18 * ox + 6 * oy + 2 - 2 * side, yh1, row), 1), :]
        start(step, (9, 10, 2))
        for cz in range(3):
            for cy in range(3):
                xs[step, cz, cy, 0:4] = coll[pl.ds(crow(18 * ox + 3 * cy + cz, 1, row), 4, stride=48), :]
        es[step, 1] = merge([xs[step, 2, cy] for cy in range(3)], -1, 15)
        es[step, 2] = merge([xs[step, 0, cy] for cy in range(3)], 1, 0)
        start(step, (5, 6))

        def pack_z(m, c):
            up, down = None, None
            for k in range(16):
                yh, xo = k // 4, k % 4
                high = coll[pl.ds(pl.multiple_of(crow(3 * m + 2, yh + 1, 8 + 8 * xo), 8), 8), :]
                low = coll[pl.ds(pl.multiple_of(crow(3 * m, yh + 1, 8 + 8 * xo), 8), 8), :]
                high, low = roll(high, -k), roll(low, k)
                z = lax.bitwise_and(lane, 15)
                up = high if up is None else jnp.where(z == 15 - k, high, up)
                down = low if down is None else jnp.where(z == k, low, down)
            zs[step, 0, m] = up
            zs[step, 1, m] = down
            return c

        lax.fori_loop(0, 9, pack_z, 0, unroll=3)
        start(step, (3, 4))
        start(step, (0,))

    def receive(step):
        rowx = jnp.where(ix == 0, 40, 7)
        edge = 5 * oy
        arrive(step, (0,))
        for cz in range(3):
            for cy in range(3):
                coll[pl.ds(crow(18 * ix + 3 * cy + cz, 1, rowx), 4, stride=48), :] = xr[step, cz, cy, 0:4]

        def take_z(m, c):
            below, above = zr[step, 0, m], zr[step, 1, m]
            for k in range(16):
                yh, xo = k // 4, k % 4
                zhalo[pl.ds(pl.multiple_of(crow(m, yh + 1, 8 + 8 * xo), 8), 8), :] = roll(below, k - 16)
                zhalo[pl.ds(pl.multiple_of(crow(9 + m, yh + 1, 8 + 8 * xo), 8), 8), :] = roll(above, 16 - k)
            return c

        if step == 0:
            know_wait(0)
            know_signal(1)
        arrive(step, (3, 4))
        lax.fori_loop(0, 9, take_z, 0, unroll=3)
        arrive(step, (1,))
        for d in range(9):
            cz, cx = d // 3, d % 3
            i = 9 * cx + 6 * iy + cz
            value = yr[step, d // 2]
            for xo in range(4):
                coll[pl.ds(pl.multiple_of(crow(i, edge, 8 + 8 * xo), 8), 8), :] = roll(value, 16 * xo + 64 * (d % 2))
        arrive(step, (2,))
        for cz in range(3):
            coll[pl.ds(crow(18 * ix + 6 * iy + cz, edge, rowx), 1), :] = er[step, 0, cz : cz + 1]
        arrive(step, (5, 6, 7, 8, 9, 10))
        for side in range(2):
            sign = 1 - 2 * side
            value = er[step, 3 + side]
            for cx in range(3):
                m = 9 * side + 3 * cx + 2 * iy
                for xo in range(4):
                    zhalo[pl.ds(pl.multiple_of(crow(m, edge, 8 + 8 * xo), 8), 8), :] = roll(
                        value, sign * (cx - 16) + 16 * xo
                    )
            value = er[step, 1 + side]
            for cy in range(3):
                m = 9 * side + 6 * ix + cy
                zhalo[pl.ds(crow(m, 1, rowx), 4, stride=48), :] = roll(value, sign * (cy - 16))[0:4]
            m = 9 * side + 6 * ix + 2 * iy
            zhalo[pl.ds(crow(m, edge, rowx), 1), :] = roll(er[step, 5 + side], -16 * sign)[0:1]

    def propagate_tile(yh, x0, store):
        z15 = lax.bitwise_and(lane, 15) == 15
        z0 = lax.bitwise_and(lane, 15) == 0
        for i in range(27):
            cx, cy, cz = velocity(i)
            here = 8 + x0 - cx
            value = coll[pl.ds(crow(i, yh + 1, here), 8), :]
            if cy:
                other = coll[pl.ds(crow(i, yh + 1 - cy, here), 8), :]
                value = jnp.where(lane >= 112 if cy > 0 else lane < 16, other, value)
            if cz:
                m = i // 3 + (0 if cz > 0 else 9)
                halo = zhalo[pl.ds(crow(m, yh + 1, here), 8), :]
                if cy:
                    other = zhalo[pl.ds(crow(m, yh + 1 - cy, here), 8), :]
                    if cz > 0:
                        at = 111 if cy > 0 else 127
                    else:
                        at = 0 if cy > 0 else 16
                    halo = jnp.where(lane == at, other, halo)
                value = jnp.where(z15 if cz > 0 else z0, halo, value)
            value = roll(value, 16 * cy + cz)
            if i != 13:
                back = coll[pl.ds(crow(26 - i, yh + 1, 8 + x0), 8), :]
                value = jnp.where(value > EDGE, value, back)
            store(i, value)

    def propagate():
        def tile(t, c):
            yh, x0 = t // 4, 8 * lax.rem(t, 4)

            def store(i, value):
                fin[pl.ds(pl.multiple_of(grow(i, yh, x0), 8), 8), :] = value

            propagate_tile(yh, x0, store)
            return c

        lax.fori_loop(0, 16, tile, 0)

    for load in loads[1:]:
        load.wait()
    collide(0)
    pl.semaphore_wait(bar, 10 + 4 * jnp.where(has_down, 1, 0) + 4 * jnp.where(has_up, 1, 0))
    know_signal(0)
    pack_and_send(0)
    receive(0)
    know_wait(1)
    know_signal(2)
    propagate()
    collide(1)
    pack_and_send(1)

    leaving = 0
    for s in range(4):
        target = tgt_ref[s, device]
        away = jnp.where(target >= 0, jnp.where(lax.shift_right_arithmetic(target, 2) == device, 0, 1), 0)
        leaving = jnp.where(away == 1, jnp.clip(list_ref[s, device], 0, 3), leaving)

    def leave_to(buffer):
        def tile(t, c):
            yhi, xh = t // 2, lax.rem(t, 2)
            yh = 2 * lax.rem(leaving, 2) + yhi
            x0 = 16 * (leaving // 2) + 8 * xh

            def store(i, value):
                buffer[2 * i + yhi, pl.ds(pl.multiple_of(8 * xh, 8), 8), :] = value

            propagate_tile(yh, x0, store)
            return c

        lax.fori_loop(0, 4, tile, 0)

    leave_to(leave)
    know_wait(2)

    def piece_of(t):
        return t - (t + ix) // 6, lax.rem(t + ix, 6) != 5

    def spread(k, c):
        t = lax.bitwise_xor(me, ROW - k)
        piece, used = piece_of(t)

        @pl.when(used)
        def _():
            pltpu.make_async_remote_copy(
                src_ref=leave.at[piece], dst_ref=buf1.at[me], send_sem=s1, recv_sem=r1,
                device_id=(ix, t // GZ, lax.rem(t, GZ)), device_id_type=MESH,
            ).start()

        return c

    lax.fori_loop(1, ROW, spread, 0)
    receive(1)

    leave_to(leave2)
    group = lax.shift_right_logical(lane, 4)
    z = lax.bitwise_and(lane, 15)

    def put(tile, value):
        bnd[tile // 2, 8 * (tile % 2) : 8 * (tile % 2) + 8] = value

    for q, (i, yhi) in enumerate(FACES_X):
        x = 0 if velocity(i)[0] > 0 else 15
        bnd[q // 16, q % 16 : q % 16 + 1] = leave2[2 * i + yhi, x : x + 1]
    for tile in range(5):
        acc = None
        for slot, (i, xh) in enumerate(FACES_Y[8 * tile : 8 * tile + 8]):
            home, yhi = (0, 0) if velocity(i)[1] > 0 else (7, 1)
            value = roll(leave2[2 * i + yhi, 8 * xh : 8 * xh + 8], 16 * (slot - home))
            acc = value if acc is None else jnp.where(group == slot, value, acc)
        put(5 + tile, acc)
    for tile in range(5):
        acc = None
        for slot, (i, yhi, xh) in enumerate(FACES_Z[16 * tile : 16 * tile + 16]):
            home = 0 if velocity(i)[2] > 0 else 15
            value = roll(leave2[2 * i + yhi, 8 * xh : 8 * xh + 8], slot - home)
            acc = value if acc is None else jnp.where(z == slot, value, acc)
        put(10 + tile, acc)
    put(15, acc)

    def edge_spread(b, c):
        t = 6 * b + 5 - ix

        @pl.when(t != me)
        def _():
            pltpu.make_async_remote_copy(
                src_ref=bnd.at[b], dst_ref=buf1.at[me], send_sem=s3, recv_sem=r3,
                device_id=(ix, t // GZ, lax.rem(t, GZ)), device_id_type=MESH,
            ).start()

        return c

    lax.fori_loop(0, EDGE_PIECES, edge_spread, 0)

    def keep_tile(t, c):
        s, yhi, xh = t // 4, lax.rem(t // 2, 2), lax.rem(t, 2)
        pos, stays = 0, 0
        for k in range(4):
            match = tgt_ref[k, device] == device * 4 + s
            pos = jnp.where(match, jnp.clip(list_ref[k, device], 0, 3), pos)
            stays = jnp.where(match, 1, stays)
        there = jnp.full((8, 128), stays, jnp.int32) > 0

        def store(i, value):
            kept[pl.ds(raw_row(i, s, yhi, 8 * xh), 8, stride=8), :] = jnp.where(there, value, 0.0)

        propagate_tile(2 * lax.rem(pos, 2) + yhi, 16 * (pos // 2) + 8 * xh, store)
        return c

    lax.fori_loop(0, 16, keep_tile, 0)
    keep_copy = pltpu.make_async_copy(kept, kept_out, load_sem.at[0])
    keep_copy.start()
    src_copy.wait()
    own, passes = piece_of(me)
    own_edge = (me + ix) // 6
    relays = jnp.logical_and(jnp.logical_not(passes), own_edge < EDGE_PIECES)

    def count(buffer, n, sem):
        pltpu.make_async_copy(buffer.at[pl.ds(0, n)], buffer.at[pl.ds(0, n)], sem).wait()

    def relay(dst, send, recv):
        def forward(k, c):
            t = lax.bitwise_xor(me, ROW - k)
            source = srcs[lax.rem(t, 8), t // 8]
            buf2[t] = buf1[jnp.clip(source - ix * ROW, 0, ROW - 1)]
            pltpu.make_async_remote_copy(
                src_ref=buf2.at[t], dst_ref=dst, send_sem=send, recv_sem=recv,
                device_id=(ix, t // GZ, lax.rem(t, GZ)), device_id_type=MESH,
            ).start()
            return c

        lax.fori_loop(1, ROW, forward, 0)
        buf2[me] = buf1[jnp.clip(srcs[lax.rem(me, 8), me // 8] - ix * ROW, 0, ROW - 1)]
        mine = pltpu.make_async_copy(buf2.at[me], dst, load_sem.at[1])
        mine.start()
        mine.wait()

    @pl.when(passes)
    def _():
        buf1[me] = leave[own]
        count(buf1, ROW - 1, r1)
        relay(got.at[own], s2, r2)
        count(got, PIECES - 1, r2)
        count(got, EDGE_PIECES, r4)
        count(buf2, ROW - 1, s2)
        count(leave, PIECES - 1, s1)
        count(leave, EDGE_PIECES, s3)

    @pl.when(relays)
    def _():
        buf1[me] = bnd[own_edge]
        count(buf1, ROW - 1, r3)
        relay(edge_got.at[own_edge], s4, r4)
        count(got, PIECES, r2)
        count(got, EDGE_PIECES - 1, r4)
        count(buf2, ROW - 1, s4)
        count(leave, PIECES, s1)
        count(leave, EDGE_PIECES - 1, s3)

    @pl.when(jnp.logical_not(jnp.logical_or(passes, relays)))
    def _():
        count(got, PIECES, r2)
        count(got, EDGE_PIECES, r4)
        count(leave, PIECES, s1)
        count(leave, EDGE_PIECES, s3)

    keep_copy.wait()
    for step in range(STEPS):
        conditions, copy = messages(step)
        for m, condition in enumerate(conditions):
            guarded(condition, lambda: copy(m).wait_send())


def finish_kernel(kept_in, got_in, edge_in, tgt_ref, out_ref, rows, got, edge, sem, out_sem):
    parts = 3
    size = 3456 // parts
    device = (lax.axis_index("gx") * 2 + lax.axis_index("gy")) * GZ + lax.axis_index("gz")
    a = pltpu.make_async_copy(edge_in, edge, sem.at[0])
    b = pltpu.make_async_copy(got_in, got, sem.at[1])
    a.start()
    b.start()
    reads = [
        pltpu.make_async_copy(kept_in.at[pl.ds(k * size, size)], rows.at[pl.ds(k * size, size)], sem.at[2 + k])
        for k in range(parts)
    ]
    writes = [
        pltpu.make_async_copy(rows.at[pl.ds(k * size, size)], out_ref.at[pl.ds(k * size, size)], out_sem.at[k])
        for k in range(parts)
    ]
    for read in reads:
        read.start()
    tg = tgt_ref[...]
    comes = jnp.logical_and(lax.shift_right_arithmetic(tg, 2) == device, lanes((4, 128)) != device)
    slot = jnp.max(jnp.where(comes, lax.bitwise_and(tg, 3), -1).astype(F32)).astype(jnp.int32)
    at_slot = jnp.clip(slot, 0, 3)
    a.wait()
    b.wait()
    lane = lanes()
    group = lax.shift_right_logical(lane, 4)
    z = lax.bitwise_and(lane, 15)
    sub = lax.broadcasted_iota(jnp.int32, (8, 128), 0)

    def face(tile):
        return edge[tile // 2, 8 * (tile % 2) : 8 * (tile % 2) + 8]

    for k in range(parts):
        reads[k].wait()

        @pl.when(slot >= 0)
        def _():
            for i in range(9 * k, 9 * k + 9):
                cx, cy, cz = velocity(i)
                for yhi in range(2):
                    for xh in range(2):
                        value = got[2 * i + yhi, 8 * xh : 8 * xh + 8]
                        if cz:
                            q = FACES_Z.index((i, yhi, xh))
                            home = 0 if cz > 0 else 15
                            value = jnp.where(z == home, roll(face(10 + q // 16), home - q % 16), value)
                        if cy and yhi == (0 if cy > 0 else 1):
                            q = FACES_Y.index((i, xh))
                            home = 0 if cy > 0 else 7
                            value = jnp.where(group == home, roll(face(5 + q // 8), 16 * (home - q % 8)), value)
                        if cx and xh == (0 if cx > 0 else 1):
                            q = FACES_X.index((i, yhi))
                            line = jnp.broadcast_to(edge[q // 16, q % 16 : q % 16 + 1], (8, 128))
                            value = jnp.where(sub == (0 if cx > 0 else 7), line, value)
                        rows[pl.ds((i * 32 + 16 * xh + yhi) * 4 + at_slot, 8, stride=8), :] = value

        writes[k].start()
    for write in writes:
        write.wait()


def body(populations, solid, block_list, targets):
    vmem = pltpu.VMEM
    tile = (8, 128)
    rows = populations.reshape(4, 27, 32, 128).transpose(1, 2, 0, 3).reshape(27 * 32 * 4, 128)
    cells = solid.reshape(4, 32, 128).transpose(1, 0, 2).reshape(32 * 4, 128)
    kept, got, edge = pl.pallas_call(
        kernel,
        out_shape=[
            jax.ShapeDtypeStruct((27 * 32 * 4, 128), F32),
            jax.ShapeDtypeStruct((PIECES, 16, 128), F32),
            jax.ShapeDtypeStruct((EDGE_PIECES, 16, 128), F32),
        ],
        in_specs=[pl.BlockSpec(memory_space=pl.ANY)] * 4,
        out_specs=[pl.BlockSpec(memory_space=pl.ANY)] * 3,
        scratch_shapes=[
            vmem((128, 128), F32),
            pltpu.SMEM((4, 128), jnp.int32),
            pltpu.SMEM((4, 128), jnp.int32),
            vmem((4, 128), jnp.int32),
            vmem((27 * 32 * 4, 128), F32),
            vmem((27 * 6 * 48, 128), F32),
            vmem((18 * 6 * 48, 128), F32),
            vmem((27 * 4 * 32, 128), F32),
            vmem((27 * 4 * 32, 128), F32),
            vmem((PIECES, 16, 128), F32),
            vmem((PIECES, 16, 128), F32),
            vmem((EDGE_PIECES, 16, 128), F32),
            vmem((ROW, 16, 128), F32),
            vmem((ROW, 16, 128), F32),
            vmem(tile, jnp.int32),
            pltpu.SMEM(tile, jnp.int32),
            vmem((2, 3, 3) + tile, F32),
            vmem((2, 5) + tile, F32),
            vmem((2, 2, 9) + tile, F32),
            vmem((2, 7) + tile, F32),
            vmem((2, 3, 3) + tile, F32),
            vmem((2, 5) + tile, F32),
            vmem((2, 2, 9) + tile, F32),
            vmem((2, 7) + tile, F32),
            pltpu.SemaphoreType.DMA((5,)),
            pltpu.SemaphoreType.DMA,
            pltpu.SemaphoreType.REGULAR((3,)),
            pltpu.SemaphoreType.DMA((STEPS, 11)),
            pltpu.SemaphoreType.DMA((STEPS, 11)),
            pltpu.SemaphoreType.DMA,
            pltpu.SemaphoreType.DMA,
            pltpu.SemaphoreType.DMA,
            pltpu.SemaphoreType.DMA,
            pltpu.SemaphoreType.DMA,
            pltpu.SemaphoreType.DMA,
            pltpu.SemaphoreType.DMA,
            pltpu.SemaphoreType.DMA,
        ],
        compiler_params=pltpu.CompilerParams(
            collective_id=0, has_side_effects=True, vmem_limit_bytes=58 * 1024 * 1024
        ),
        name="lattice",
    )(rows, cells, block_list.T, targets.T)
    out = pl.pallas_call(
        finish_kernel,
        out_shape=jax.ShapeDtypeStruct((27 * 32 * 4, 128), F32),
        in_specs=[pl.BlockSpec(memory_space=pl.ANY)] * 3 + [pl.BlockSpec(memory_space=pltpu.VMEM)],
        out_specs=pl.BlockSpec(memory_space=pl.ANY),
        scratch_shapes=[
            vmem((27 * 32 * 4, 128), F32),
            vmem((PIECES, 16, 128), F32),
            vmem((EDGE_PIECES, 16, 128), F32),
            pltpu.SemaphoreType.DMA((5,)),
            pltpu.SemaphoreType.DMA((3,)),
        ],
        compiler_params=pltpu.CompilerParams(vmem_limit_bytes=58 * 1024 * 1024),
        name="finish",
    )(kept, got, edge, targets.T)
    return out.reshape(27, 32, 4, 128).transpose(2, 0, 1, 3).reshape(4, 27, 4096)


def solution(mesh):
    in_specs = (P(("gx", "gy", "gz"), None, None), P(("gx", "gy", "gz"), None), P(), P())
    out_specs = P(("gx", "gy", "gz"), None, None)
    return jax.shard_map(body, mesh=mesh, in_specs=in_specs, out_specs=out_specs, check_vma=False)
```

```python
import jax
import jax.numpy as jnp
from jax import lax
from jax.experimental import pallas as pl
from jax.experimental.pallas import tpu as pltpu
from jax.sharding import PartitionSpec as P

STEPS = 2
GZ = 32
ROW = 64
PIECES = 54
ABSENT = -1.0e30
EDGE = -1.0e29
W0, W1, W2, W3 = 8.0 / 27.0, 2.0 / 27.0, 1.0 / 54.0, 1.0 / 216.0
OMEGA = 0.8
MESH = pl.DeviceIdType.MESH
F32 = jnp.float32


def velocity(i):
    return (i // 9 - 1, (i // 3) % 3 - 1, i % 3 - 1)


def crow(i, yh1, x8):
    return (i * 6 + yh1) * 48 + x8


def grow(i, yh, x):
    return (i * 4 + yh) * 32 + x


DIRS = range(27)
FACES_X = [(i, yhi) for i in DIRS if velocity(i)[0] for yhi in range(2)]
FACES_Y = [(i, xh) for i in DIRS if velocity(i)[1] for xh in range(2)]
FACES_Z = [(i, yhi, xh) for i in DIRS if velocity(i)[2] for yhi in range(2) for xh in range(2)]
EDGE_PIECES = 8


def lanes(shape=(8, 128)):
    return lax.broadcasted_iota(jnp.int32, shape, 1)


def roll(value, shift):
    shift = shift % 128
    return value if shift == 0 else pltpu.roll(value, shift, 1)


def collide_tile(load, n, store):
    s, d = {}, {}
    g13 = load(13)
    for j in range(14, 27):
        up, down = load(j), load(26 - j)
        s[j] = up + down
        d[j] = up - down
    level = {1: [], 2: [], 3: []}
    for j in range(14, 27):
        level[sum(abs(c) for c in velocity(j))].append(j)

    def total(values):
        values = list(values)
        while len(values) > 1:
            values = [values[k] + values[k + 1] if k + 1 < len(values) else values[k] for k in range(0, len(values), 2)]
        return values[0]

    rho = W0 * g13 + W1 * total(s[j] for j in level[1]) + W2 * total(s[j] for j in level[2]) + W3 * total(s[j] for j in level[3])
    momentum = []
    for axis in range(3):
        acc = None
        for lev, w in ((1, W1), (2, W2), (3, W3)):
            plus = [d[j] for j in level[lev] if velocity(j)[axis] > 0]
            minus = [d[j] for j in level[lev] if velocity(j)[axis] < 0]
            term = total(plus)
            if minus:
                term = term - total(minus)
            term = w * term
            acc = term if acc is None else acc + term
        momentum.append(acc)
    mx, my, mz = momentum
    rinv = 1.0 / rho
    fluid = 1.0 - n
    a = (1.0 - OMEGA) * fluid
    b = OMEGA * fluid
    p = 0.5 * (a + n)
    q = 0.5 * (a - n)
    e0 = b * (rho - 1.5 * rinv * (mx * mx + my * my + mz * mz))
    k = 4.5 * b * rinv
    b3 = 3.0 * b
    store(13, (a + n) * g13 + e0)
    for j in range(14, 27):
        cx, cy, cz = velocity(j)
        proj = None
        for c, m in ((cx, mx), (cy, my), (cz, mz)):
            if c:
                if proj is None:
                    proj = m if c > 0 else -m
                else:
                    proj = proj + m if c > 0 else proj - m
        even = p * s[j] + (e0 + k * (proj * proj))
        odd = q * d[j] + b3 * proj
        store(j, even + odd)
        store(26 - j, even - odd)


def kernel(
    pops_in, solid_in, list_in, tgt_in, kept_out, got, edge_got,
    solid_ref, list_ref, tgt_ref, tgtv_ref, praw, coll, zhalo, fin, kept, leave, leave2, bnd, buf1, buf2, srcv, srcs,
    xs, ys, zs, es, xr, yr, zr, er,
    load_sem, src_sem, know_sem, send_sem, recv_sem, s1, r1, s2, r2, s3, r3, s4, r4,
):
    ix, iy, iz = lax.axis_index("gx"), lax.axis_index("gy"), lax.axis_index("gz")
    me = iy * GZ + iz
    device = ix * ROW + me
    ox, oy = 1 - ix, 1 - iy
    has_down = iz > 0
    has_up = iz < GZ - 1

    pairs = ((tgt_in, tgtv_ref), (tgt_in, tgt_ref), (list_in, list_ref), (solid_in, solid_ref), (pops_in, praw))
    loads = [pltpu.make_async_copy(src, dst, load_sem.at[k]) for k, (src, dst) in enumerate(pairs)]
    for load in loads:
        load.start()

    bar = pltpu.get_barrier_semaphore()

    def greet(*target):
        pl.semaphore_signal(bar, inc=1, device_id=target, device_id_type=MESH)

    @pl.when(has_down)
    def _():
        for x in (ix, ox):
            for y in (iy, oy):
                greet(x, y, iz - 1)

    @pl.when(has_up)
    def _():
        for x in (ix, ox):
            for y in (iy, oy):
                greet(x, y, iz + 1)

    greet(ix, oy, iz)
    greet(ox, oy, iz)
    greet(ox, iy, iz)

    def flipped(bits):
        return (ix, iy, lax.bitwise_xor(iz, bits))

    rounds = [
        [flipped(1), flipped(2), flipped(3)],
        [flipped(4), flipped(8), flipped(12)],
        [(ix, oy, iz), flipped(16), (ix, oy, lax.bitwise_xor(iz, 16))],
    ]
    for bits in (2, 3, 4, 8, 12, 16):
        greet(*flipped(bits))
    greet(*rounds[2][2])

    def know_signal(r):
        for target in rounds[r]:
            pl.semaphore_signal(know_sem.at[r], inc=1, device_id=target, device_id_type=MESH)

    def know_wait(r):
        pl.semaphore_wait(know_sem.at[r], 3)

    lane = lanes()

    none = jnp.full((8, 128), ABSENT, F32)

    def clear_coll(i, c):
        for yh1 in (0, 5):
            for x in range(0, 48, 8):
                coll[pl.ds(crow(i, yh1, x), 8), :] = none
        for yh1 in range(1, 5):
            for x in (0, 40):
                coll[pl.ds(crow(i, yh1, x), 8), :] = none
        return c

    lax.fori_loop(0, 27, clear_coll, 0)

    def clear_z(i, c):
        for yh1 in (0, 5):
            for x in range(0, 48, 8):
                zhalo[pl.ds(crow(i, yh1, x), 8), :] = none
        for yh1 in range(1, 5):
            for x in (0, 40):
                zhalo[pl.ds(crow(i, yh1, x), 8), :] = none
        return c

    lax.fori_loop(0, 18, clear_z, 0)
    for side, missing in ((0, iz == 0), (1, iz == GZ - 1)):

        @pl.when(missing)
        def _():
            for step in range(STEPS):
                for m in range(9):
                    zr[step, side, m] = none
                for m in (1, 3, 5):
                    er[step, m + side] = none

    loads[0].wait()
    tg = tgtv_ref[...]
    sender = lanes((4, 128))
    tdev = jnp.where(tg >= 0, lax.shift_right_arithmetic(tg, 2), -1)
    tdev = jnp.where(tdev == sender, -1, tdev) - ix * ROW
    table = jnp.full((8, 128), -1, jnp.int32)
    for t8 in range(8):
        rows = lax.broadcasted_iota(jnp.int32, (8, 128), 0) + 8 * t8
        best = jnp.full((8, 128), -1, jnp.int32)
        for s in range(4):
            best = jnp.where(tdev[s : s + 1] == rows, lane, best)
        for shift in (64, 32, 16, 8, 4, 2, 1):
            best = jnp.maximum(best, pltpu.roll(best, shift, 1))
        table = jnp.where(lane == t8, best, table)
    srcv[...] = table
    src_copy = pltpu.make_async_copy(srcv, srcs, src_sem)
    src_copy.start()

    def raw_row(i, slot, yhi, x):
        return (i * 32 + 2 * x + yhi) * 4 + slot

    def slot_of(p):
        slot, there = 0, 0
        for s in range(4):
            match = list_ref[s, device] == p
            slot = jnp.where(match, s, slot)
            there = jnp.where(match, 1, there)
        return slot, there

    def collide(step):
        def tile(t, c):
            p, yhi, xh = t // 4, lax.rem(t // 2, 2), lax.rem(t, 2)
            slot, there = slot_of(p)
            yh = 2 * lax.rem(p, 2) + yhi
            x0 = 16 * (p // 2) + 8 * xh
            inside = jnp.full((8, 128), there, jnp.int32) > 0
            n = solid_ref[pl.ds(raw_row(0, slot, yhi, 8 * xh), 8, stride=8), :]
            if step == 0:
                def load(i):
                    return praw[pl.ds(raw_row(i, slot, yhi, 8 * xh), 8, stride=8), :]
            else:
                def load(i):
                    return fin[pl.ds(grow(i, yh, x0), 8), :]

            def store(i, value):
                coll[pl.ds(pl.multiple_of(crow(i, yh + 1, 8 + x0), 8), 8), :] = jnp.where(inside, value, ABSENT)

            collide_tile(load, n, store)
            return c

        lax.fori_loop(0, 16, tile, 0, unroll=2)

    def messages(step):
        down, up = iz - 1, iz + 1
        edges, far = es.at[step], er.at[step]
        table = [
            (None, xs.at[step], xr.at[step], (ox, iy, iz)),
            (None, ys.at[step], yr.at[step], (ix, oy, iz)),
            (None, edges.at[0], far.at[0], (ox, oy, iz)),
            (has_up, zs.at[step, 0], zr.at[step, 0], (ix, iy, up)),
            (has_down, zs.at[step, 1], zr.at[step, 1], (ix, iy, down)),
            (has_up, edges.at[1], far.at[1], (ox, iy, up)),
            (has_down, edges.at[2], far.at[2], (ox, iy, down)),
            (has_up, edges.at[3], far.at[3], (ix, oy, up)),
            (has_down, edges.at[4], far.at[4], (ix, oy, down)),
            (has_up, edges.at[5], far.at[5], (ox, oy, up)),
            (has_down, edges.at[6], far.at[6], (ox, oy, down)),
        ]

        def copy(m):
            _, src, dst, target = table[m]
            return pltpu.make_async_remote_copy(
                src_ref=src, dst_ref=dst, send_sem=send_sem.at[step, m], recv_sem=recv_sem.at[step, m],
                device_id=target, device_id_type=MESH,
            )

        return [row[0] for row in table], copy

    def guarded(condition, action):
        if condition is None:
            action()
        else:
            pl.when(condition)(action)

    def start(step, which):
        conditions, copy = messages(step)
        for m in which:
            guarded(conditions[m], lambda: copy(m).start())

    def arrive(step, which):
        _, copy = messages(step)
        for m in which:
            condition = None if m < 3 else has_down if m % 2 == 1 else has_up
            guarded(condition, lambda: copy(m).wait_recv())

    def pack_and_send(step):
        row = jnp.where(ix == 0, 39, 8)
        yh1 = 1 + 3 * oy
        z = lax.bitwise_and(lane, 15)
        group = lax.shift_right_logical(lane, 4)
        slots = [group == lax.rem(7 * oy - xo + 8, 8) for xo in range(4)]
        own_half = jnp.logical_or(jnp.logical_or(slots[0], slots[1]), jnp.logical_or(slots[2], slots[3]))

        halves = []
        for d in range(9):
            cz, cx = d // 3, d % 3
            i = 9 * cx + 6 * oy + cz
            acc = None
            for xo in range(4):
                value = roll(coll[pl.ds(pl.multiple_of(crow(i, yh1, 8 + 8 * xo), 8), 8), :], -16 * xo)
                acc = value if acc is None else jnp.where(slots[xo], value, acc)
            halves.append(acc)

        def merge(values, step_of, home):
            acc = values[0]
            for k in (1, 2):
                acc = jnp.where(z == home + k * step_of, roll(values[k], k * step_of), acc)
            return acc

        es[step, 3] = merge(halves[6:9], -1, 15)
        es[step, 4] = merge(halves[0:3], 1, 0)
        start(step, (7, 8))
        for v in range(5):
            tile = halves[2 * v]
            if v < 4:
                tile = jnp.where(own_half, tile, roll(halves[2 * v + 1], -64))
            ys[step, v] = tile
        start(step, (1,))

        for cz in range(3):
            es[step, 0, cz : cz + 1] = coll[pl.ds(crow(18 * ox + 6 * oy + cz, yh1, row), 1), :]
        for side in range(2):
            es[step, 5 + side, 0:1] = coll[pl.ds(crow(18 * ox + 6 * oy + 2 - 2 * side, yh1, row), 1), :]
        start(step, (9, 10, 2))
        for cz in range(3):
            for cy in range(3):
                xs[step, cz, cy, 0:4] = coll[pl.ds(crow(18 * ox + 3 * cy + cz, 1, row), 4, stride=48), :]
        es[step, 1] = merge([xs[step, 2, cy] for cy in range(3)], -1, 15)
        es[step, 2] = merge([xs[step, 0, cy] for cy in range(3)], 1, 0)
        start(step, (5, 6))

        def pack_z(m, c):
            up, down = None, None
            for k in range(16):
                yh, xo = k // 4, k % 4
                high = coll[pl.ds(pl.multiple_of(crow(3 * m + 2, yh + 1, 8 + 8 * xo), 8), 8), :]
                low = coll[pl.ds(pl.multiple_of(crow(3 * m, yh + 1, 8 + 8 * xo), 8), 8), :]
                high, low = roll(high, -k), roll(low, k)
                z = lax.bitwise_and(lane, 15)
                up = high if up is None else jnp.where(z == 15 - k, high, up)
                down = low if down is None else jnp.where(z == k, low, down)
            zs[step, 0, m] = up
            zs[step, 1, m] = down
            return c

        lax.fori_loop(0, 9, pack_z, 0, unroll=3)
        start(step, (3, 4))
        start(step, (0,))

    def receive(step):
        rowx = jnp.where(ix == 0, 40, 7)
        edge = 5 * oy
        arrive(step, (0,))
        for cz in range(3):
            for cy in range(3):
                coll[pl.ds(crow(18 * ix + 3 * cy + cz, 1, rowx), 4, stride=48), :] = xr[step, cz, cy, 0:4]

        def take_z(m, c):
            below, above = zr[step, 0, m], zr[step, 1, m]
            for k in range(16):
                yh, xo = k // 4, k % 4
                zhalo[pl.ds(pl.multiple_of(crow(m, yh + 1, 8 + 8 * xo), 8), 8), :] = roll(below, k - 16)
                zhalo[pl.ds(pl.multiple_of(crow(9 + m, yh + 1, 8 + 8 * xo), 8), 8), :] = roll(above, 16 - k)
            return c

        if step == 0:
            know_wait(0)
            know_signal(1)
        arrive(step, (3, 4))
        lax.fori_loop(0, 9, take_z, 0, unroll=3)
        arrive(step, (1,))
        for d in range(9):
            cz, cx = d // 3, d % 3
            i = 9 * cx + 6 * iy + cz
            value = yr[step, d // 2]
            for xo in range(4):
                coll[pl.ds(pl.multiple_of(crow(i, edge, 8 + 8 * xo), 8), 8), :] = roll(value, 16 * xo + 64 * (d % 2))
        arrive(step, (2,))
        for cz in range(3):
            coll[pl.ds(crow(18 * ix + 6 * iy + cz, edge, rowx), 1), :] = er[step, 0, cz : cz + 1]
        arrive(step, (5, 6, 7, 8, 9, 10))
        for side in range(2):
            sign = 1 - 2 * side
            value = er[step, 3 + side]
            for cx in range(3):
                m = 9 * side + 3 * cx + 2 * iy
                for xo in range(4):
                    zhalo[pl.ds(pl.multiple_of(crow(m, edge, 8 + 8 * xo), 8), 8), :] = roll(
                        value, sign * (cx - 16) + 16 * xo
                    )
            value = er[step, 1 + side]
            for cy in range(3):
                m = 9 * side + 6 * ix + cy
                zhalo[pl.ds(crow(m, 1, rowx), 4, stride=48), :] = roll(value, sign * (cy - 16))[0:4]
            m = 9 * side + 6 * ix + 2 * iy
            zhalo[pl.ds(crow(m, edge, rowx), 1), :] = roll(er[step, 5 + side], -16 * sign)[0:1]

    def propagate_tile(yh, x0, store):
        z15 = lax.bitwise_and(lane, 15) == 15
        z0 = lax.bitwise_and(lane, 15) == 0
        for i in range(27):
            cx, cy, cz = velocity(i)
            here = 8 + x0 - cx
            value = coll[pl.ds(crow(i, yh + 1, here), 8), :]
            if cy:
                other = coll[pl.ds(crow(i, yh + 1 - cy, here), 8), :]
                value = jnp.where(lane >= 112 if cy > 0 else lane < 16, other, value)
            if cz:
                m = i // 3 + (0 if cz > 0 else 9)
                halo = zhalo[pl.ds(crow(m, yh + 1, here), 8), :]
                if cy:
                    other = zhalo[pl.ds(crow(m, yh + 1 - cy, here), 8), :]
                    if cz > 0:
                        at = 111 if cy > 0 else 127
                    else:
                        at = 0 if cy > 0 else 16
                    halo = jnp.where(lane == at, other, halo)
                value = jnp.where(z15 if cz > 0 else z0, halo, value)
            value = roll(value, 16 * cy + cz)
            if i != 13:
                back = coll[pl.ds(crow(26 - i, yh + 1, 8 + x0), 8), :]
                value = jnp.where(value > EDGE, value, back)
            store(i, value)

    def propagate():
        def tile(t, c):
            yh, x0 = t // 4, 8 * lax.rem(t, 4)

            def store(i, value):
                fin[pl.ds(pl.multiple_of(grow(i, yh, x0), 8), 8), :] = value

            propagate_tile(yh, x0, store)
            return c

        lax.fori_loop(0, 16, tile, 0, unroll=2)

    for load in loads[1:]:
        load.wait()
    collide(0)
    pl.semaphore_wait(bar, 10 + 4 * jnp.where(has_down, 1, 0) + 4 * jnp.where(has_up, 1, 0))
    know_signal(0)
    pack_and_send(0)
    receive(0)
    know_wait(1)
    know_signal(2)
    propagate()
    collide(1)
    pack_and_send(1)

    leaving = 0
    for s in range(4):
        target = tgt_ref[s, device]
        away = jnp.where(target >= 0, jnp.where(lax.shift_right_arithmetic(target, 2) == device, 0, 1), 0)
        leaving = jnp.where(away == 1, jnp.clip(list_ref[s, device], 0, 3), leaving)

    def leave_to(buffer):
        def tile(t, c):
            yhi, xh = t // 2, lax.rem(t, 2)
            yh = 2 * lax.rem(leaving, 2) + yhi
            x0 = 16 * (leaving // 2) + 8 * xh

            def store(i, value):
                buffer[2 * i + yhi, pl.ds(pl.multiple_of(8 * xh, 8), 8), :] = value

            propagate_tile(yh, x0, store)
            return c

        lax.fori_loop(0, 4, tile, 0, unroll=2)

    leave_to(leave)
    know_wait(2)

    def piece_of(t):
        return t - (t + ix) // 6, lax.rem(t + ix, 6) != 5

    def spread(k, c):
        t = lax.bitwise_xor(me, ROW - k)
        piece, used = piece_of(t)

        @pl.when(used)
        def _():
            pltpu.make_async_remote_copy(
                src_ref=leave.at[piece], dst_ref=buf1.at[me], send_sem=s1, recv_sem=r1,
                device_id=(ix, t // GZ, lax.rem(t, GZ)), device_id_type=MESH,
            ).start()

        return c

    lax.fori_loop(1, ROW, spread, 0)
    receive(1)

    leave_to(leave2)
    group = lax.shift_right_logical(lane, 4)
    z = lax.bitwise_and(lane, 15)

    def put(tile, value):
        bnd[tile // 2, 8 * (tile % 2) : 8 * (tile % 2) + 8] = value

    for q, (i, yhi) in enumerate(FACES_X):
        x = 0 if velocity(i)[0] > 0 else 15
        bnd[q // 16, q % 16 : q % 16 + 1] = leave2[2 * i + yhi, x : x + 1]
    for tile in range(5):
        acc = None
        for slot, (i, xh) in enumerate(FACES_Y[8 * tile : 8 * tile + 8]):
            home, yhi = (0, 0) if velocity(i)[1] > 0 else (7, 1)
            value = roll(leave2[2 * i + yhi, 8 * xh : 8 * xh + 8], 16 * (slot - home))
            acc = value if acc is None else jnp.where(group == slot, value, acc)
        put(5 + tile, acc)
    for tile in range(5):
        acc = None
        for slot, (i, yhi, xh) in enumerate(FACES_Z[16 * tile : 16 * tile + 16]):
            home = 0 if velocity(i)[2] > 0 else 15
            value = roll(leave2[2 * i + yhi, 8 * xh : 8 * xh + 8], slot - home)
            acc = value if acc is None else jnp.where(z == slot, value, acc)
        put(10 + tile, acc)
    put(15, acc)

    def edge_spread(b, c):
        t = 6 * b + 5 - ix

        @pl.when(t != me)
        def _():
            pltpu.make_async_remote_copy(
                src_ref=bnd.at[b], dst_ref=buf1.at[me], send_sem=s3, recv_sem=r3,
                device_id=(ix, t // GZ, lax.rem(t, GZ)), device_id_type=MESH,
            ).start()

        return c

    lax.fori_loop(0, EDGE_PIECES, edge_spread, 0)

    def keep_tile(t, c):
        s, yhi, xh = t // 4, lax.rem(t // 2, 2), lax.rem(t, 2)
        pos, stays = 0, 0
        for k in range(4):
            match = tgt_ref[k, device] == device * 4 + s
            pos = jnp.where(match, jnp.clip(list_ref[k, device], 0, 3), pos)
            stays = jnp.where(match, 1, stays)
        there = jnp.full((8, 128), stays, jnp.int32) > 0

        def store(i, value):
            kept[pl.ds(raw_row(i, s, yhi, 8 * xh), 8, stride=8), :] = jnp.where(there, value, 0.0)

        propagate_tile(2 * lax.rem(pos, 2) + yhi, 16 * (pos // 2) + 8 * xh, store)
        return c

    lax.fori_loop(0, 16, keep_tile, 0)
    keep_copy = pltpu.make_async_copy(kept, kept_out, load_sem.at[0])
    keep_copy.start()
    src_copy.wait()
    own, passes = piece_of(me)
    own_edge = (me + ix) // 6
    relays = jnp.logical_and(jnp.logical_not(passes), own_edge < EDGE_PIECES)

    def count(buffer, n, sem):
        pltpu.make_async_copy(buffer.at[pl.ds(0, n)], buffer.at[pl.ds(0, n)], sem).wait()

    def relay(dst, send, recv):
        def forward(k, c):
            t = lax.bitwise_xor(me, ROW - k)
            source = srcs[lax.rem(t, 8), t // 8]
            buf2[t] = buf1[jnp.clip(source - ix * ROW, 0, ROW - 1)]
            pltpu.make_async_remote_copy(
                src_ref=buf2.at[t], dst_ref=dst, send_sem=send, recv_sem=recv,
                device_id=(ix, t // GZ, lax.rem(t, GZ)), device_id_type=MESH,
            ).start()
            return c

        lax.fori_loop(1, ROW, forward, 0)
        buf2[me] = buf1[jnp.clip(srcs[lax.rem(me, 8), me // 8] - ix * ROW, 0, ROW - 1)]
        mine = pltpu.make_async_copy(buf2.at[me], dst, load_sem.at[1])
        mine.start()
        mine.wait()

    @pl.when(passes)
    def _():
        buf1[me] = leave[own]
        count(buf1, ROW - 1, r1)
        relay(got.at[own], s2, r2)
        count(got, PIECES - 1, r2)
        count(got, EDGE_PIECES, r4)
        count(buf2, ROW - 1, s2)
        count(leave, PIECES - 1, s1)
        count(leave, EDGE_PIECES, s3)

    @pl.when(relays)
    def _():
        buf1[me] = bnd[own_edge]
        count(buf1, ROW - 1, r3)
        relay(edge_got.at[own_edge], s4, r4)
        count(got, PIECES, r2)
        count(got, EDGE_PIECES - 1, r4)
        count(buf2, ROW - 1, s4)
        count(leave, PIECES, s1)
        count(leave, EDGE_PIECES - 1, s3)

    @pl.when(jnp.logical_not(jnp.logical_or(passes, relays)))
    def _():
        count(got, PIECES, r2)
        count(got, EDGE_PIECES, r4)
        count(leave, PIECES, s1)
        count(leave, EDGE_PIECES, s3)

    keep_copy.wait()
    for step in range(STEPS):
        conditions, copy = messages(step)
        for m, condition in enumerate(conditions):
            guarded(condition, lambda: copy(m).wait_send())


def finish_kernel(kept_in, got_in, edge_in, tgt_ref, out_ref, rows, got, edge, sem, out_sem):
    parts = 3
    size = 3456 // parts
    device = (lax.axis_index("gx") * 2 + lax.axis_index("gy")) * GZ + lax.axis_index("gz")
    a = pltpu.make_async_copy(edge_in, edge, sem.at[0])
    b = pltpu.make_async_copy(got_in, got, sem.at[1])
    a.start()
    b.start()
    reads = [
        pltpu.make_async_copy(kept_in.at[pl.ds(k * size, size)], rows.at[pl.ds(k * size, size)], sem.at[2 + k])
        for k in range(parts)
    ]
    writes = [
        pltpu.make_async_copy(rows.at[pl.ds(k * size, size)], out_ref.at[pl.ds(k * size, size)], out_sem.at[k])
        for k in range(parts)
    ]
    for read in reads:
        read.start()
    tg = tgt_ref[...]
    comes = jnp.logical_and(lax.shift_right_arithmetic(tg, 2) == device, lanes((4, 128)) != device)
    slot = jnp.max(jnp.where(comes, lax.bitwise_and(tg, 3), -1).astype(F32)).astype(jnp.int32)
    at_slot = jnp.clip(slot, 0, 3)
    a.wait()
    b.wait()
    lane = lanes()
    group = lax.shift_right_logical(lane, 4)
    z = lax.bitwise_and(lane, 15)
    sub = lax.broadcasted_iota(jnp.int32, (8, 128), 0)

    def face(tile):
        return edge[tile // 2, 8 * (tile % 2) : 8 * (tile % 2) + 8]

    for k in range(parts):
        reads[k].wait()

        @pl.when(slot >= 0)
        def _():
            for i in range(9 * k, 9 * k + 9):
                cx, cy, cz = velocity(i)
                for yhi in range(2):
                    for xh in range(2):
                        value = got[2 * i + yhi, 8 * xh : 8 * xh + 8]
                        if cz:
                            q = FACES_Z.index((i, yhi, xh))
                            home = 0 if cz > 0 else 15
                            value = jnp.where(z == home, roll(face(10 + q // 16), home - q % 16), value)
                        if cy and yhi == (0 if cy > 0 else 1):
                            q = FACES_Y.index((i, xh))
                            home = 0 if cy > 0 else 7
                            value = jnp.where(group == home, roll(face(5 + q // 8), 16 * (home - q % 8)), value)
                        if cx and xh == (0 if cx > 0 else 1):
                            q = FACES_X.index((i, yhi))
                            line = jnp.broadcast_to(edge[q // 16, q % 16 : q % 16 + 1], (8, 128))
                            value = jnp.where(sub == (0 if cx > 0 else 7), line, value)
                        rows[pl.ds((i * 32 + 16 * xh + yhi) * 4 + at_slot, 8, stride=8), :] = value

        writes[k].start()
    for write in writes:
        write.wait()


def body(populations, solid, block_list, targets):
    vmem = pltpu.VMEM
    tile = (8, 128)
    rows = populations.reshape(4, 27, 32, 128).transpose(1, 2, 0, 3).reshape(27 * 32 * 4, 128)
    cells = solid.reshape(4, 32, 128).transpose(1, 0, 2).reshape(32 * 4, 128)
    kept, got, edge = pl.pallas_call(
        kernel,
        out_shape=[
            jax.ShapeDtypeStruct((27 * 32 * 4, 128), F32),
            jax.ShapeDtypeStruct((PIECES, 16, 128), F32),
            jax.ShapeDtypeStruct((EDGE_PIECES, 16, 128), F32),
        ],
        in_specs=[pl.BlockSpec(memory_space=pl.ANY)] * 4,
        out_specs=[pl.BlockSpec(memory_space=pl.ANY)] * 3,
        scratch_shapes=[
            vmem((128, 128), F32),
            pltpu.SMEM((4, 128), jnp.int32),
            pltpu.SMEM((4, 128), jnp.int32),
            vmem((4, 128), jnp.int32),
            vmem((27 * 32 * 4, 128), F32),
            vmem((27 * 6 * 48, 128), F32),
            vmem((18 * 6 * 48, 128), F32),
            vmem((27 * 4 * 32, 128), F32),
            vmem((27 * 4 * 32, 128), F32),
            vmem((PIECES, 16, 128), F32),
            vmem((PIECES, 16, 128), F32),
            vmem((EDGE_PIECES, 16, 128), F32),
            vmem((ROW, 16, 128), F32),
            vmem((ROW, 16, 128), F32),
            vmem(tile, jnp.int32),
            pltpu.SMEM(tile, jnp.int32),
            vmem((2, 3, 3) + tile, F32),
            vmem((2, 5) + tile, F32),
            vmem((2, 2, 9) + tile, F32),
            vmem((2, 7) + tile, F32),
            vmem((2, 3, 3) + tile, F32),
            vmem((2, 5) + tile, F32),
            vmem((2, 2, 9) + tile, F32),
            vmem((2, 7) + tile, F32),
            pltpu.SemaphoreType.DMA((5,)),
            pltpu.SemaphoreType.DMA,
            pltpu.SemaphoreType.REGULAR((3,)),
            pltpu.SemaphoreType.DMA((STEPS, 11)),
            pltpu.SemaphoreType.DMA((STEPS, 11)),
            pltpu.SemaphoreType.DMA,
            pltpu.SemaphoreType.DMA,
            pltpu.SemaphoreType.DMA,
            pltpu.SemaphoreType.DMA,
            pltpu.SemaphoreType.DMA,
            pltpu.SemaphoreType.DMA,
            pltpu.SemaphoreType.DMA,
            pltpu.SemaphoreType.DMA,
        ],
        compiler_params=pltpu.CompilerParams(
            collective_id=0, has_side_effects=True, vmem_limit_bytes=58 * 1024 * 1024
        ),
        name="lattice",
    )(rows, cells, block_list.T, targets.T)
    out = pl.pallas_call(
        finish_kernel,
        out_shape=jax.ShapeDtypeStruct((27 * 32 * 4, 128), F32),
        in_specs=[pl.BlockSpec(memory_space=pl.ANY)] * 3 + [pl.BlockSpec(memory_space=pltpu.VMEM)],
        out_specs=pl.BlockSpec(memory_space=pl.ANY),
        scratch_shapes=[
            vmem((27 * 32 * 4, 128), F32),
            vmem((PIECES, 16, 128), F32),
            vmem((EDGE_PIECES, 16, 128), F32),
            pltpu.SemaphoreType.DMA((5,)),
            pltpu.SemaphoreType.DMA((3,)),
        ],
        compiler_params=pltpu.CompilerParams(vmem_limit_bytes=58 * 1024 * 1024),
        name="finish",
    )(kept, got, edge, targets.T)
    return out.reshape(27, 32, 4, 128).transpose(2, 0, 1, 3).reshape(4, 27, 4096)


def solution(mesh):
    in_specs = (P(("gx", "gy", "gz"), None, None), P(("gx", "gy", "gz"), None), P(), P())
    out_specs = P(("gx", "gy", "gz"), None, None)
    return jax.shard_map(body, mesh=mesh, in_specs=in_specs, out_specs=out_specs, check_vma=False)
```

```python
import jax
import jax.numpy as jnp
from jax import lax
from jax.experimental import pallas as pl
from jax.experimental.pallas import tpu as pltpu
from jax.sharding import PartitionSpec as P

STEPS = 2
GZ = 32
ROW = 64
PIECES = 54
ABSENT = -1.0e30
EDGE = -1.0e29
W0, W1, W2, W3 = 8.0 / 27.0, 2.0 / 27.0, 1.0 / 54.0, 1.0 / 216.0
OMEGA = 0.8
MESH = pl.DeviceIdType.MESH
F32 = jnp.float32


def velocity(i):
    return (i // 9 - 1, (i // 3) % 3 - 1, i % 3 - 1)


def crow(i, yh1, x8):
    return (i * 6 + yh1) * 48 + x8


def grow(i, yh, x):
    return (i * 4 + yh) * 32 + x


DIRS = range(27)
FACES_X = [(i, yhi) for i in DIRS if velocity(i)[0] for yhi in range(2)]
FACES_Y = [(i, xh) for i in DIRS if velocity(i)[1] for xh in range(2)]
FACES_Z = [(i, yhi, xh) for i in DIRS if velocity(i)[2] for yhi in range(2) for xh in range(2)]
EDGE_PIECES = 8


def lanes(shape=(8, 128)):
    return lax.broadcasted_iota(jnp.int32, shape, 1)


def roll(value, shift):
    shift = shift % 128
    return value if shift == 0 else pltpu.roll(value, shift, 1)


def collide_tile(load, n, store):
    s, d = {}, {}
    g13 = load(13)
    for j in range(14, 27):
        up, down = load(j), load(26 - j)
        s[j] = up + down
        d[j] = up - down
    level = {1: [], 2: [], 3: []}
    for j in range(14, 27):
        level[sum(abs(c) for c in velocity(j))].append(j)

    def total(values):
        values = list(values)
        while len(values) > 1:
            values = [values[k] + values[k + 1] if k + 1 < len(values) else values[k] for k in range(0, len(values), 2)]
        return values[0]

    rho = W0 * g13 + W1 * total(s[j] for j in level[1]) + W2 * total(s[j] for j in level[2]) + W3 * total(s[j] for j in level[3])
    momentum = []
    for axis in range(3):
        acc = None
        for lev, w in ((1, W1), (2, W2), (3, W3)):
            plus = [d[j] for j in level[lev] if velocity(j)[axis] > 0]
            minus = [d[j] for j in level[lev] if velocity(j)[axis] < 0]
            term = total(plus)
            if minus:
                term = term - total(minus)
            term = w * term
            acc = term if acc is None else acc + term
        momentum.append(acc)
    mx, my, mz = momentum
    rinv = 1.0 / rho
    fluid = 1.0 - n
    a = (1.0 - OMEGA) * fluid
    b = OMEGA * fluid
    p = 0.5 * (a + n)
    q = 0.5 * (a - n)
    e0 = b * (rho - 1.5 * rinv * (mx * mx + my * my + mz * mz))
    k = 4.5 * b * rinv
    b3 = 3.0 * b
    store(13, (a + n) * g13 + e0)
    for j in range(14, 27):
        cx, cy, cz = velocity(j)
        proj = None
        for c, m in ((cx, mx), (cy, my), (cz, mz)):
            if c:
                if proj is None:
                    proj = m if c > 0 else -m
                else:
                    proj = proj + m if c > 0 else proj - m
        even = p * s[j] + (e0 + k * (proj * proj))
        odd = q * d[j] + b3 * proj
        store(j, even + odd)
        store(26 - j, even - odd)


def kernel(
    pops_in, solid_in, list_in, tgt_in, kept_out, got, edge_got,
    solid_ref, list_ref, tgt_ref, tgtv_ref, praw, coll, zhalo, fin, kept, leave, leave2, bnd, buf1, buf2, srcv, srcs,
    xs, ys, zs, es, xr, yr, zr, er,
    load_sem, src_sem, know_sem, send_sem, recv_sem, s1, r1, s2, r2, s3, r3, s4, r4,
):
    ix, iy, iz = lax.axis_index("gx"), lax.axis_index("gy"), lax.axis_index("gz")
    me = iy * GZ + iz
    device = ix * ROW + me
    ox, oy = 1 - ix, 1 - iy
    has_down = iz > 0
    has_up = iz < GZ - 1

    pairs = ((tgt_in, tgtv_ref), (tgt_in, tgt_ref), (list_in, list_ref), (solid_in, solid_ref), (pops_in, praw))
    loads = [pltpu.make_async_copy(src, dst, load_sem.at[k]) for k, (src, dst) in enumerate(pairs)]
    for load in loads:
        load.start()

    bar = pltpu.get_barrier_semaphore()

    def greet(*target):
        pl.semaphore_signal(bar, inc=1, device_id=target, device_id_type=MESH)

    @pl.when(has_down)
    def _():
        for x in (ix, ox):
            for y in (iy, oy):
                greet(x, y, iz - 1)

    @pl.when(has_up)
    def _():
        for x in (ix, ox):
            for y in (iy, oy):
                greet(x, y, iz + 1)

    greet(ix, oy, iz)
    greet(ox, oy, iz)
    greet(ox, iy, iz)

    def flipped(bits):
        return (ix, iy, lax.bitwise_xor(iz, bits))

    rounds = [
        [flipped(1), flipped(2), flipped(3)],
        [flipped(4), flipped(8), flipped(12)],
        [(ix, oy, iz), flipped(16), (ix, oy, lax.bitwise_xor(iz, 16))],
    ]
    for bits in (2, 3, 4, 8, 12, 16):
        greet(*flipped(bits))
    greet(*rounds[2][2])

    def know_signal(r):
        for target in rounds[r]:
            pl.semaphore_signal(know_sem.at[r], inc=1, device_id=target, device_id_type=MESH)

    def know_wait(r):
        pl.semaphore_wait(know_sem.at[r], 3)

    lane = lanes()

    none = jnp.full((8, 128), ABSENT, F32)

    def clear_coll(i, c):
        for yh1 in (0, 5):
            for x in range(0, 48, 8):
                coll[pl.ds(crow(i, yh1, x), 8), :] = none
        for yh1 in range(1, 5):
            for x in (0, 40):
                coll[pl.ds(crow(i, yh1, x), 8), :] = none
        return c

    lax.fori_loop(0, 27, clear_coll, 0)

    def clear_z(i, c):
        for yh1 in (0, 5):
            for x in range(0, 48, 8):
                zhalo[pl.ds(crow(i, yh1, x), 8), :] = none
        for yh1 in range(1, 5):
            for x in (0, 40):
                zhalo[pl.ds(crow(i, yh1, x), 8), :] = none
        return c

    lax.fori_loop(0, 18, clear_z, 0)
    for side, missing in ((0, iz == 0), (1, iz == GZ - 1)):

        @pl.when(missing)
        def _():
            for step in range(STEPS):
                for m in range(9):
                    zr[step, side, m] = none
                for m in (1, 3, 5):
                    er[step, m + side] = none

    loads[0].wait()
    tg = tgtv_ref[...]
    sender = lanes((4, 128))
    tdev = jnp.where(tg >= 0, lax.shift_right_arithmetic(tg, 2), -1)
    tdev = jnp.where(tdev == sender, -1, tdev) - ix * ROW
    table = jnp.full((8, 128), -1, jnp.int32)
    for t8 in range(8):
        rows = lax.broadcasted_iota(jnp.int32, (8, 128), 0) + 8 * t8
        best = jnp.full((8, 128), -1, jnp.int32)
        for s in range(4):
            best = jnp.where(tdev[s : s + 1] == rows, lane, best)
        for shift in (64, 32, 16, 8, 4, 2, 1):
            best = jnp.maximum(best, pltpu.roll(best, shift, 1))
        table = jnp.where(lane == t8, best, table)
    srcv[...] = table
    src_copy = pltpu.make_async_copy(srcv, srcs, src_sem)
    src_copy.start()

    def raw_row(i, slot, yhi, x):
        return (i * 32 + 2 * x + yhi) * 4 + slot

    def slot_of(p):
        slot, there = 0, 0
        for s in range(4):
            match = list_ref[s, device] == p
            slot = jnp.where(match, s, slot)
            there = jnp.where(match, 1, there)
        return slot, there

    def collide(step):
        def tile(t, c):
            p, yhi, xh = t // 4, lax.rem(t // 2, 2), lax.rem(t, 2)
            slot, there = slot_of(p)
            yh = 2 * lax.rem(p, 2) + yhi
            x0 = 16 * (p // 2) + 8 * xh
            inside = jnp.full((8, 128), there, jnp.int32) > 0
            n = solid_ref[pl.ds(raw_row(0, slot, yhi, 8 * xh), 8, stride=8), :]
            if step == 0:
                def load(i):
                    return praw[pl.ds(raw_row(i, slot, yhi, 8 * xh), 8, stride=8), :]
            else:
                def load(i):
                    return fin[pl.ds(grow(i, yh, x0), 8), :]

            def store(i, value):
                coll[pl.ds(pl.multiple_of(crow(i, yh + 1, 8 + x0), 8), 8), :] = jnp.where(inside, value, ABSENT)

            collide_tile(load, n, store)
            return c

        lax.fori_loop(0, 16, tile, 0, unroll=2)

    def messages(step):
        down, up = iz - 1, iz + 1
        edges, far = es.at[step], er.at[step]
        table = [
            (None, xs.at[step], xr.at[step], (ox, iy, iz)),
            (None, ys.at[step], yr.at[step], (ix, oy, iz)),
            (None, edges.at[0], far.at[0], (ox, oy, iz)),
            (has_up, zs.at[step, 0], zr.at[step, 0], (ix, iy, up)),
            (has_down, zs.at[step, 1], zr.at[step, 1], (ix, iy, down)),
            (has_up, edges.at[1], far.at[1], (ox, iy, up)),
            (has_down, edges.at[2], far.at[2], (ox, iy, down)),
            (has_up, edges.at[3], far.at[3], (ix, oy, up)),
            (has_down, edges.at[4], far.at[4], (ix, oy, down)),
            (has_up, edges.at[5], far.at[5], (ox, oy, up)),
            (has_down, edges.at[6], far.at[6], (ox, oy, down)),
        ]

        def copy(m):
            _, src, dst, target = table[m]
            return pltpu.make_async_remote_copy(
                src_ref=src, dst_ref=dst, send_sem=send_sem.at[step, m], recv_sem=recv_sem.at[step, m],
                device_id=target, device_id_type=MESH,
            )

        return [row[0] for row in table], copy

    def guarded(condition, action):
        if condition is None:
            action()
        else:
            pl.when(condition)(action)

    def start(step, which):
        conditions, copy = messages(step)
        for m in which:
            guarded(conditions[m], lambda: copy(m).start())

    def arrive(step, which):
        _, copy = messages(step)
        for m in which:
            condition = None if m < 3 else has_down if m % 2 == 1 else has_up
            guarded(condition, lambda: copy(m).wait_recv())

    def pack_and_send(step):
        row = jnp.where(ix == 0, 39, 8)
        yh1 = 1 + 3 * oy
        z = lax.bitwise_and(lane, 15)
        group = lax.shift_right_logical(lane, 4)
        slots = [group == lax.rem(7 * oy - xo + 8, 8) for xo in range(4)]
        own_half = jnp.logical_or(jnp.logical_or(slots[0], slots[1]), jnp.logical_or(slots[2], slots[3]))

        halves = []
        for d in range(9):
            cz, cx = d // 3, d % 3
            i = 9 * cx + 6 * oy + cz
            acc = None
            for xo in range(4):
                value = roll(coll[pl.ds(pl.multiple_of(crow(i, yh1, 8 + 8 * xo), 8), 8), :], -16 * xo)
                acc = value if acc is None else jnp.where(slots[xo], value, acc)
            halves.append(acc)

        def merge(values, step_of, home):
            acc = values[0]
            for k in (1, 2):
                acc = jnp.where(z == home + k * step_of, roll(values[k], k * step_of), acc)
            return acc

        es[step, 3] = merge(halves[6:9], -1, 15)
        es[step, 4] = merge(halves[0:3], 1, 0)
        start(step, (7, 8))
        for v in range(5):
            tile = halves[2 * v]
            if v < 4:
                tile = jnp.where(own_half, tile, roll(halves[2 * v + 1], -64))
            ys[step, v] = tile
        start(step, (1,))

        for cz in range(3):
            es[step, 0, cz : cz + 1] = coll[pl.ds(crow(18 * ox + 6 * oy + cz, yh1, row), 1), :]
        for side in range(2):
            es[step, 5 + side, 0:1] = coll[pl.ds(crow(18 * ox + 6 * oy + 2 - 2 * side, yh1, row), 1), :]
        start(step, (9, 10, 2))
        for cz in range(3):
            for cy in range(3):
                xs[step, cz, cy, 0:4] = coll[pl.ds(crow(18 * ox + 3 * cy + cz, 1, row), 4, stride=48), :]
        es[step, 1] = merge([xs[step, 2, cy] for cy in range(3)], -1, 15)
        es[step, 2] = merge([xs[step, 0, cy] for cy in range(3)], 1, 0)
        start(step, (5, 6))

        def pack_z(m, c):
            up, down = None, None
            for k in range(16):
                yh, xo = k // 4, k % 4
                high = coll[pl.ds(pl.multiple_of(crow(3 * m + 2, yh + 1, 8 + 8 * xo), 8), 8), :]
                low = coll[pl.ds(pl.multiple_of(crow(3 * m, yh + 1, 8 + 8 * xo), 8), 8), :]
                high, low = roll(high, -k), roll(low, k)
                z = lax.bitwise_and(lane, 15)
                up = high if up is None else jnp.where(z == 15 - k, high, up)
                down = low if down is None else jnp.where(z == k, low, down)
            zs[step, 0, m] = up
            zs[step, 1, m] = down
            return c

        lax.fori_loop(0, 9, pack_z, 0, unroll=3)
        start(step, (3, 4))
        start(step, (0,))

    def receive(step):
        rowx = jnp.where(ix == 0, 40, 7)
        edge = 5 * oy
        arrive(step, (0,))
        for cz in range(3):
            for cy in range(3):
                coll[pl.ds(crow(18 * ix + 3 * cy + cz, 1, rowx), 4, stride=48), :] = xr[step, cz, cy, 0:4]

        def take_z(m, c):
            below, above = zr[step, 0, m], zr[step, 1, m]
            for k in range(16):
                yh, xo = k // 4, k % 4
                zhalo[pl.ds(pl.multiple_of(crow(m, yh + 1, 8 + 8 * xo), 8), 8), :] = roll(below, k - 16)
                zhalo[pl.ds(pl.multiple_of(crow(9 + m, yh + 1, 8 + 8 * xo), 8), 8), :] = roll(above, 16 - k)
            return c

        if step == 0:
            know_wait(0)
            know_signal(1)
        arrive(step, (3, 4))
        lax.fori_loop(0, 9, take_z, 0, unroll=3)
        arrive(step, (1,))
        for d in range(9):
            cz, cx = d // 3, d % 3
            i = 9 * cx + 6 * iy + cz
            value = yr[step, d // 2]
            for xo in range(4):
                coll[pl.ds(pl.multiple_of(crow(i, edge, 8 + 8 * xo), 8), 8), :] = roll(value, 16 * xo + 64 * (d % 2))
        arrive(step, (2,))
        for cz in range(3):
            coll[pl.ds(crow(18 * ix + 6 * iy + cz, edge, rowx), 1), :] = er[step, 0, cz : cz + 1]
        arrive(step, (5, 6, 7, 8, 9, 10))
        for side in range(2):
            sign = 1 - 2 * side
            value = er[step, 3 + side]
            for cx in range(3):
                m = 9 * side + 3 * cx + 2 * iy
                for xo in range(4):
                    zhalo[pl.ds(pl.multiple_of(crow(m, edge, 8 + 8 * xo), 8), 8), :] = roll(
                        value, sign * (cx - 16) + 16 * xo
                    )
            value = er[step, 1 + side]
            for cy in range(3):
                m = 9 * side + 6 * ix + cy
                zhalo[pl.ds(crow(m, 1, rowx), 4, stride=48), :] = roll(value, sign * (cy - 16))[0:4]
            m = 9 * side + 6 * ix + 2 * iy
            zhalo[pl.ds(crow(m, edge, rowx), 1), :] = roll(er[step, 5 + side], -16 * sign)[0:1]

    def propagate_tile(yh, x0, store):
        z15 = lax.bitwise_and(lane, 15) == 15
        z0 = lax.bitwise_and(lane, 15) == 0
        for i in range(27):
            cx, cy, cz = velocity(i)
            here = 8 + x0 - cx
            value = coll[pl.ds(crow(i, yh + 1, here), 8), :]
            if cy:
                other = coll[pl.ds(crow(i, yh + 1 - cy, here), 8), :]
                value = jnp.where(lane >= 112 if cy > 0 else lane < 16, other, value)
            if cz:
                m = i // 3 + (0 if cz > 0 else 9)
                halo = zhalo[pl.ds(crow(m, yh + 1, here), 8), :]
                if cy:
                    other = zhalo[pl.ds(crow(m, yh + 1 - cy, here), 8), :]
                    if cz > 0:
                        at = 111 if cy > 0 else 127
                    else:
                        at = 0 if cy > 0 else 16
                    halo = jnp.where(lane == at, other, halo)
                value = jnp.where(z15 if cz > 0 else z0, halo, value)
            value = roll(value, 16 * cy + cz)
            if i != 13:
                back = coll[pl.ds(crow(26 - i, yh + 1, 8 + x0), 8), :]
                value = jnp.where(value > EDGE, value, back)
            store(i, value)

    def propagate():
        def tile(t, c):
            yh, x0 = t // 4, 8 * lax.rem(t, 4)

            def store(i, value):
                fin[pl.ds(pl.multiple_of(grow(i, yh, x0), 8), 8), :] = value

            propagate_tile(yh, x0, store)
            return c

        lax.fori_loop(0, 16, tile, 0, unroll=2)

    for load in loads[1:]:
        load.wait()
    collide(0)
    pl.semaphore_wait(bar, 10 + 4 * jnp.where(has_down, 1, 0) + 4 * jnp.where(has_up, 1, 0))
    know_signal(0)
    pack_and_send(0)
    receive(0)
    know_wait(1)
    know_signal(2)
    propagate()
    collide(1)
    pack_and_send(1)

    leaving = 0
    for s in range(4):
        target = tgt_ref[s, device]
        away = jnp.where(target >= 0, jnp.where(lax.shift_right_arithmetic(target, 2) == device, 0, 1), 0)
        leaving = jnp.where(away == 1, jnp.clip(list_ref[s, device], 0, 3), leaving)

    def leave_to(buffer):
        def tile(t, c):
            yhi, xh = t // 2, lax.rem(t, 2)
            yh = 2 * lax.rem(leaving, 2) + yhi
            x0 = 16 * (leaving // 2) + 8 * xh

            def store(i, value):
                buffer[2 * i + yhi, pl.ds(pl.multiple_of(8 * xh, 8), 8), :] = value

            propagate_tile(yh, x0, store)
            return c

        lax.fori_loop(0, 4, tile, 0, unroll=2)

    leave_to(leave)
    know_wait(2)

    def piece_of(t):
        return t - (t + ix) // 6, lax.rem(t + ix, 6) != 5

    def spread(k, c):
        t = lax.bitwise_xor(me, ROW - k)
        piece, used = piece_of(t)

        @pl.when(used)
        def _():
            pltpu.make_async_remote_copy(
                src_ref=leave.at[piece], dst_ref=buf1.at[me], send_sem=s1, recv_sem=r1,
                device_id=(ix, t // GZ, lax.rem(t, GZ)), device_id_type=MESH,
            ).start()

        return c

    lax.fori_loop(1, ROW, spread, 0)
    receive(1)

    leave_to(leave2)
    group = lax.shift_right_logical(lane, 4)
    z = lax.bitwise_and(lane, 15)

    def put(tile, value):
        bnd[tile // 2, 8 * (tile % 2) : 8 * (tile % 2) + 8] = value

    for q, (i, yhi) in enumerate(FACES_X):
        x = 0 if velocity(i)[0] > 0 else 15
        bnd[q // 16, q % 16 : q % 16 + 1] = leave2[2 * i + yhi, x : x + 1]
    for tile in range(5):
        acc = None
        for slot, (i, xh) in enumerate(FACES_Y[8 * tile : 8 * tile + 8]):
            home, yhi = (0, 0) if velocity(i)[1] > 0 else (7, 1)
            value = roll(leave2[2 * i + yhi, 8 * xh : 8 * xh + 8], 16 * (slot - home))
            acc = value if acc is None else jnp.where(group == slot, value, acc)
        put(5 + tile, acc)
    for tile in range(5):
        acc = None
        for slot, (i, yhi, xh) in enumerate(FACES_Z[16 * tile : 16 * tile + 16]):
            home = 0 if velocity(i)[2] > 0 else 15
            value = roll(leave2[2 * i + yhi, 8 * xh : 8 * xh + 8], slot - home)
            acc = value if acc is None else jnp.where(z == slot, value, acc)
        put(10 + tile, acc)
    put(15, acc)

    def edge_spread(b, c):
        t = 6 * b + 5 - ix

        @pl.when(t != me)
        def _():
            pltpu.make_async_remote_copy(
                src_ref=bnd.at[b], dst_ref=buf1.at[me], send_sem=s3, recv_sem=r3,
                device_id=(ix, t // GZ, lax.rem(t, GZ)), device_id_type=MESH,
            ).start()

        return c

    lax.fori_loop(0, EDGE_PIECES, edge_spread, 0)

    def keep_tile(t, c):
        s, yhi, xh = t // 4, lax.rem(t // 2, 2), lax.rem(t, 2)
        pos, stays = 0, 0
        for k in range(4):
            match = tgt_ref[k, device] == device * 4 + s
            pos = jnp.where(match, jnp.clip(list_ref[k, device], 0, 3), pos)
            stays = jnp.where(match, 1, stays)
        there = jnp.full((8, 128), stays, jnp.int32) > 0

        def store(i, value):
            kept[pl.ds(raw_row(i, s, yhi, 8 * xh), 8, stride=8), :] = jnp.where(there, value, 0.0)

        propagate_tile(2 * lax.rem(pos, 2) + yhi, 16 * (pos // 2) + 8 * xh, store)
        return c

    lax.fori_loop(0, 16, keep_tile, 0)
    keep_copy = pltpu.make_async_copy(kept, kept_out, load_sem.at[0])
    keep_copy.start()
    src_copy.wait()
    own, passes = piece_of(me)
    own_edge = (me + ix) // 6
    relays = jnp.logical_and(jnp.logical_not(passes), own_edge < EDGE_PIECES)

    def count(buffer, n, sem):
        pltpu.make_async_copy(buffer.at[pl.ds(0, n)], buffer.at[pl.ds(0, n)], sem).wait()

    def relay(dst, send, recv):
        def forward(k, c):
            t = lax.bitwise_xor(me, ROW - k)
            source = srcs[lax.rem(t, 8), t // 8]
            buf2[t] = buf1[jnp.clip(source - ix * ROW, 0, ROW - 1)]
            pltpu.make_async_remote_copy(
                src_ref=buf2.at[t], dst_ref=dst, send_sem=send, recv_sem=recv,
                device_id=(ix, t // GZ, lax.rem(t, GZ)), device_id_type=MESH,
            ).start()
            return c

        lax.fori_loop(1, ROW, forward, 0)
        buf2[me] = buf1[jnp.clip(srcs[lax.rem(me, 8), me // 8] - ix * ROW, 0, ROW - 1)]
        mine = pltpu.make_async_copy(buf2.at[me], dst, load_sem.at[1])
        mine.start()
        mine.wait()

    @pl.when(passes)
    def _():
        buf1[me] = leave[own]
        count(buf1, ROW - 1, r1)
        relay(got.at[own], s2, r2)
        count(got, PIECES - 1, r2)
        count(got, EDGE_PIECES, r4)
        count(buf2, ROW - 1, s2)
        count(leave, PIECES - 1, s1)
        count(leave, EDGE_PIECES, s3)

    @pl.when(relays)
    def _():
        buf1[me] = bnd[own_edge]
        count(buf1, ROW - 1, r3)
        relay(edge_got.at[own_edge], s4, r4)
        count(got, PIECES, r2)
        count(got, EDGE_PIECES - 1, r4)
        count(buf2, ROW - 1, s4)
        count(leave, PIECES, s1)
        count(leave, EDGE_PIECES - 1, s3)

    @pl.when(jnp.logical_not(jnp.logical_or(passes, relays)))
    def _():
        count(got, PIECES, r2)
        count(got, EDGE_PIECES, r4)
        count(leave, PIECES, s1)
        count(leave, EDGE_PIECES, s3)

    keep_copy.wait()
    for step in range(STEPS):
        conditions, copy = messages(step)
        for m, condition in enumerate(conditions):
            guarded(condition, lambda: copy(m).wait_send())


def finish_kernel(kept_in, got_in, edge_in, tgt_in, out_ref, rows, got, edge, tgt_ref, sem, out_sem):
    parts = 3
    size = 3456 // parts
    device = (lax.axis_index("gx") * 2 + lax.axis_index("gy")) * GZ + lax.axis_index("gz")
    table = pltpu.make_async_copy(tgt_in, tgt_ref, sem.at[5])
    table.start()
    a = pltpu.make_async_copy(edge_in, edge, sem.at[0])
    b = pltpu.make_async_copy(got_in, got, sem.at[1])
    a.start()
    b.start()
    reads = [
        pltpu.make_async_copy(kept_in.at[pl.ds(k * size, size)], rows.at[pl.ds(k * size, size)], sem.at[2 + k])
        for k in range(parts)
    ]
    writes = [
        pltpu.make_async_copy(rows.at[pl.ds(k * size, size)], out_ref.at[pl.ds(k * size, size)], out_sem.at[k])
        for k in range(parts)
    ]
    for read in reads:
        read.start()
    table.wait()
    tg = tgt_ref[...]
    comes = jnp.logical_and(lax.shift_right_arithmetic(tg, 2) == device, lanes((4, 128)) != device)
    slot = jnp.max(jnp.where(comes, lax.bitwise_and(tg, 3), -1).astype(F32)).astype(jnp.int32)
    at_slot = jnp.clip(slot, 0, 3)
    a.wait()
    b.wait()
    lane = lanes()
    group = lax.shift_right_logical(lane, 4)
    z = lax.bitwise_and(lane, 15)
    sub = lax.broadcasted_iota(jnp.int32, (8, 128), 0)

    def face(tile):
        return edge[tile // 2, 8 * (tile % 2) : 8 * (tile % 2) + 8]

    for k in range(parts):
        reads[k].wait()

        @pl.when(slot >= 0)
        def _():
            for i in range(9 * k, 9 * k + 9):
                cx, cy, cz = velocity(i)
                for yhi in range(2):
                    for xh in range(2):
                        value = got[2 * i + yhi, 8 * xh : 8 * xh + 8]
                        if cz:
                            q = FACES_Z.index((i, yhi, xh))
                            home = 0 if cz > 0 else 15
                            value = jnp.where(z == home, roll(face(10 + q // 16), home - q % 16), value)
                        if cy and yhi == (0 if cy > 0 else 1):
                            q = FACES_Y.index((i, xh))
                            home = 0 if cy > 0 else 7
                            value = jnp.where(group == home, roll(face(5 + q // 8), 16 * (home - q % 8)), value)
                        if cx and xh == (0 if cx > 0 else 1):
                            q = FACES_X.index((i, yhi))
                            line = jnp.broadcast_to(edge[q // 16, q % 16 : q % 16 + 1], (8, 128))
                            value = jnp.where(sub == (0 if cx > 0 else 7), line, value)
                        rows[pl.ds((i * 32 + 16 * xh + yhi) * 4 + at_slot, 8, stride=8), :] = value

        writes[k].start()
    for write in writes:
        write.wait()


def body(populations, solid, block_list, targets):
    vmem = pltpu.VMEM
    tile = (8, 128)
    rows = populations.reshape(4, 27, 32, 128).transpose(1, 2, 0, 3).reshape(27 * 32 * 4, 128)
    cells = solid.reshape(4, 32, 128).transpose(1, 0, 2).reshape(32 * 4, 128)
    kept, got, edge = pl.pallas_call(
        kernel,
        out_shape=[
            jax.ShapeDtypeStruct((27 * 32 * 4, 128), F32),
            jax.ShapeDtypeStruct((PIECES, 16, 128), F32),
            jax.ShapeDtypeStruct((EDGE_PIECES, 16, 128), F32),
        ],
        in_specs=[pl.BlockSpec(memory_space=pl.ANY)] * 4,
        out_specs=[pl.BlockSpec(memory_space=pl.ANY)] * 3,
        scratch_shapes=[
            vmem((128, 128), F32),
            pltpu.SMEM((4, 128), jnp.int32),
            pltpu.SMEM((4, 128), jnp.int32),
            vmem((4, 128), jnp.int32),
            vmem((27 * 32 * 4, 128), F32),
            vmem((27 * 6 * 48, 128), F32),
            vmem((18 * 6 * 48, 128), F32),
            vmem((27 * 4 * 32, 128), F32),
            vmem((27 * 4 * 32, 128), F32),
            vmem((PIECES, 16, 128), F32),
            vmem((PIECES, 16, 128), F32),
            vmem((EDGE_PIECES, 16, 128), F32),
            vmem((ROW, 16, 128), F32),
            vmem((ROW, 16, 128), F32),
            vmem(tile, jnp.int32),
            pltpu.SMEM(tile, jnp.int32),
            vmem((2, 3, 3) + tile, F32),
            vmem((2, 5) + tile, F32),
            vmem((2, 2, 9) + tile, F32),
            vmem((2, 7) + tile, F32),
            vmem((2, 3, 3) + tile, F32),
            vmem((2, 5) + tile, F32),
            vmem((2, 2, 9) + tile, F32),
            vmem((2, 7) + tile, F32),
            pltpu.SemaphoreType.DMA((5,)),
            pltpu.SemaphoreType.DMA,
            pltpu.SemaphoreType.REGULAR((3,)),
            pltpu.SemaphoreType.DMA((STEPS, 11)),
            pltpu.SemaphoreType.DMA((STEPS, 11)),
            pltpu.SemaphoreType.DMA,
            pltpu.SemaphoreType.DMA,
            pltpu.SemaphoreType.DMA,
            pltpu.SemaphoreType.DMA,
            pltpu.SemaphoreType.DMA,
            pltpu.SemaphoreType.DMA,
            pltpu.SemaphoreType.DMA,
            pltpu.SemaphoreType.DMA,
        ],
        compiler_params=pltpu.CompilerParams(
            collective_id=0, has_side_effects=True, vmem_limit_bytes=58 * 1024 * 1024
        ),
        name="lattice",
    )(rows, cells, block_list.T, targets.T)
    out = pl.pallas_call(
        finish_kernel,
        out_shape=jax.ShapeDtypeStruct((27 * 32 * 4, 128), F32),
        in_specs=[pl.BlockSpec(memory_space=pl.ANY)] * 4,
        out_specs=pl.BlockSpec(memory_space=pl.ANY),
        scratch_shapes=[
            vmem((27 * 32 * 4, 128), F32),
            vmem((PIECES, 16, 128), F32),
            vmem((EDGE_PIECES, 16, 128), F32),
            vmem((4, 128), jnp.int32),
            pltpu.SemaphoreType.DMA((6,)),
            pltpu.SemaphoreType.DMA((3,)),
        ],
        compiler_params=pltpu.CompilerParams(vmem_limit_bytes=58 * 1024 * 1024),
        name="finish",
    )(kept, got, edge, targets.T)
    return out.reshape(27, 32, 4, 128).transpose(2, 0, 1, 3).reshape(4, 27, 4096)


def solution(mesh):
    in_specs = (P(("gx", "gy", "gz"), None, None), P(("gx", "gy", "gz"), None), P(), P())
    out_specs = P(("gx", "gy", "gz"), None, None)
    return jax.shard_map(body, mesh=mesh, in_specs=in_specs, out_specs=out_specs, check_vma=False)
```

```python
import jax
import jax.numpy as jnp
from jax import lax
from jax.experimental import pallas as pl
from jax.experimental.pallas import tpu as pltpu
from jax.sharding import PartitionSpec as P

STEPS = 2
GZ = 32
ROW = 64
PIECES = 54
ABSENT = -1.0e30
EDGE = -1.0e29
W0, W1, W2, W3 = 8.0 / 27.0, 2.0 / 27.0, 1.0 / 54.0, 1.0 / 216.0
OMEGA = 0.8
MESH = pl.DeviceIdType.MESH
F32 = jnp.float32


def velocity(i):
    return (i // 9 - 1, (i // 3) % 3 - 1, i % 3 - 1)


def crow(i, yh1, x8):
    return (i * 6 + yh1) * 48 + x8


def grow(i, yh, x):
    return (i * 4 + yh) * 32 + x


DIRS = range(27)
FACES_X = [(i, yhi) for i in DIRS if velocity(i)[0] for yhi in range(2)]
FACES_Y = [(i, xh) for i in DIRS if velocity(i)[1] for xh in range(2)]
FACES_Z = [(i, yhi, xh) for i in DIRS if velocity(i)[2] for yhi in range(2) for xh in range(2)]
EDGE_PIECES = 8


def lanes(shape=(8, 128)):
    return lax.broadcasted_iota(jnp.int32, shape, 1)


def roll(value, shift):
    shift = shift % 128
    return value if shift == 0 else pltpu.roll(value, shift, 1)


def collide_tile(load, n, store):
    s, d = {}, {}
    g13 = load(13)
    for j in range(14, 27):
        up, down = load(j), load(26 - j)
        s[j] = up + down
        d[j] = up - down
    level = {1: [], 2: [], 3: []}
    for j in range(14, 27):
        level[sum(abs(c) for c in velocity(j))].append(j)

    def total(values):
        values = list(values)
        while len(values) > 1:
            values = [values[k] + values[k + 1] if k + 1 < len(values) else values[k] for k in range(0, len(values), 2)]
        return values[0]

    rho = W0 * g13 + W1 * total(s[j] for j in level[1]) + W2 * total(s[j] for j in level[2]) + W3 * total(s[j] for j in level[3])
    momentum = []
    for axis in range(3):
        acc = None
        for lev, w in ((1, W1), (2, W2), (3, W3)):
            plus = [d[j] for j in level[lev] if velocity(j)[axis] > 0]
            minus = [d[j] for j in level[lev] if velocity(j)[axis] < 0]
            term = total(plus)
            if minus:
                term = term - total(minus)
            term = w * term
            acc = term if acc is None else acc + term
        momentum.append(acc)
    mx, my, mz = momentum
    rinv = 1.0 / rho
    fluid = 1.0 - n
    a = (1.0 - OMEGA) * fluid
    b = OMEGA * fluid
    p = 0.5 * (a + n)
    q = 0.5 * (a - n)
    e0 = b * (rho - 1.5 * rinv * (mx * mx + my * my + mz * mz))
    k = 4.5 * b * rinv
    b3 = 3.0 * b
    store(13, (a + n) * g13 + e0)
    for j in range(14, 27):
        cx, cy, cz = velocity(j)
        proj = None
        for c, m in ((cx, mx), (cy, my), (cz, mz)):
            if c:
                if proj is None:
                    proj = m if c > 0 else -m
                else:
                    proj = proj + m if c > 0 else proj - m
        even = p * s[j] + (e0 + k * (proj * proj))
        odd = q * d[j] + b3 * proj
        store(j, even + odd)
        store(26 - j, even - odd)


def kernel(
    pops_in, solid_in, list_in, tgt_in, kept_out, got, edge_got,
    solid_ref, list_ref, tgt_ref, tgtv_ref, praw, coll, zhalo, fin, kept, leave, leave2, bnd, buf1, buf2, srcv, srcs,
    xs, ys, zs, es, xr, yr, zr, er,
    load_sem, src_sem, know_sem, send_sem, recv_sem, s1, r1, s2, r2, s3, r3, s4, r4,
):
    ix, iy, iz = lax.axis_index("gx"), lax.axis_index("gy"), lax.axis_index("gz")
    me = iy * GZ + iz
    device = ix * ROW + me
    ox, oy = 1 - ix, 1 - iy
    has_down = iz > 0
    has_up = iz < GZ - 1

    pairs = ((tgt_in, tgtv_ref), (tgt_in, tgt_ref), (list_in, list_ref), (solid_in, solid_ref), (pops_in, praw))
    loads = [pltpu.make_async_copy(src, dst, load_sem.at[k]) for k, (src, dst) in enumerate(pairs)]
    for load in loads:
        load.start()

    bar = pltpu.get_barrier_semaphore()

    def greet(*target):
        pl.semaphore_signal(bar, inc=1, device_id=target, device_id_type=MESH)

    @pl.when(has_down)
    def _():
        for x in (ix, ox):
            for y in (iy, oy):
                greet(x, y, iz - 1)

    @pl.when(has_up)
    def _():
        for x in (ix, ox):
            for y in (iy, oy):
                greet(x, y, iz + 1)

    greet(ix, oy, iz)
    greet(ox, oy, iz)
    greet(ox, iy, iz)

    def flipped(bits):
        return (ix, iy, lax.bitwise_xor(iz, bits))

    rounds = [
        [flipped(1), flipped(2), flipped(3)],
        [flipped(4), flipped(8), flipped(12)],
        [(ix, oy, iz), flipped(16), (ix, oy, lax.bitwise_xor(iz, 16))],
    ]
    for bits in (2, 3, 4, 8, 12, 16):
        greet(*flipped(bits))
    greet(*rounds[2][2])

    def know_signal(r):
        for target in rounds[r]:
            pl.semaphore_signal(know_sem.at[r], inc=1, device_id=target, device_id_type=MESH)

    def know_wait(r):
        pl.semaphore_wait(know_sem.at[r], 3)

    lane = lanes()

    none = jnp.full((8, 128), ABSENT, F32)

    def clear_coll(i, c):
        for yh1 in (0, 5):
            for x in range(0, 48, 8):
                coll[pl.ds(crow(i, yh1, x), 8), :] = none
        for yh1 in range(1, 5):
            for x in (0, 40):
                coll[pl.ds(crow(i, yh1, x), 8), :] = none
        return c

    lax.fori_loop(0, 27, clear_coll, 0)

    def clear_z(i, c):
        for yh1 in (0, 5):
            for x in range(0, 48, 8):
                zhalo[pl.ds(crow(i, yh1, x), 8), :] = none
        for yh1 in range(1, 5):
            for x in (0, 40):
                zhalo[pl.ds(crow(i, yh1, x), 8), :] = none
        return c

    lax.fori_loop(0, 18, clear_z, 0)
    for side, missing in ((0, iz == 0), (1, iz == GZ - 1)):

        @pl.when(missing)
        def _():
            for step in range(STEPS):
                for m in range(9):
                    zr[step, side, m] = none
                for m in (1, 3, 5):
                    er[step, m + side] = none

    loads[0].wait()
    tg = tgtv_ref[...]
    sender = lanes((4, 128))
    tdev = jnp.where(tg >= 0, lax.shift_right_arithmetic(tg, 2), -1)
    tdev = jnp.where(tdev == sender, -1, tdev) - ix * ROW
    table = jnp.full((8, 128), -1, jnp.int32)
    for t8 in range(8):
        rows = lax.broadcasted_iota(jnp.int32, (8, 128), 0) + 8 * t8
        best = jnp.full((8, 128), -1, jnp.int32)
        for s in range(4):
            best = jnp.where(tdev[s : s + 1] == rows, lane, best)
        for shift in (64, 32, 16, 8, 4, 2, 1):
            best = jnp.maximum(best, pltpu.roll(best, shift, 1))
        table = jnp.where(lane == t8, best, table)
    srcv[...] = table
    src_copy = pltpu.make_async_copy(srcv, srcs, src_sem)
    src_copy.start()

    def raw_row(i, slot, yhi, x):
        return (i * 32 + 2 * x + yhi) * 4 + slot

    def slot_of(p):
        slot, there = 0, 0
        for s in range(4):
            match = list_ref[s, device] == p
            slot = jnp.where(match, s, slot)
            there = jnp.where(match, 1, there)
        return slot, there

    def collide(step):
        def tile(t, c):
            p, yhi, xh = t // 4, lax.rem(t // 2, 2), lax.rem(t, 2)
            slot, there = slot_of(p)
            yh = 2 * lax.rem(p, 2) + yhi
            x0 = 16 * (p // 2) + 8 * xh
            inside = jnp.full((8, 128), there, jnp.int32) > 0
            n = solid_ref[pl.ds(raw_row(0, slot, yhi, 8 * xh), 8, stride=8), :]
            if step == 0:
                def load(i):
                    return praw[pl.ds(raw_row(i, slot, yhi, 8 * xh), 8, stride=8), :]
            else:
                def load(i):
                    return fin[pl.ds(grow(i, yh, x0), 8), :]

            def store(i, value):
                coll[pl.ds(pl.multiple_of(crow(i, yh + 1, 8 + x0), 8), 8), :] = jnp.where(inside, value, ABSENT)

            collide_tile(load, n, store)
            return c

        lax.fori_loop(0, 16, tile, 0, unroll=2)

    def messages(step):
        down, up = iz - 1, iz + 1
        edges, far = es.at[step], er.at[step]
        table = [
            (None, xs.at[step], xr.at[step], (ox, iy, iz)),
            (None, ys.at[step], yr.at[step], (ix, oy, iz)),
            (None, edges.at[0], far.at[0], (ox, oy, iz)),
            (has_up, zs.at[step, 0], zr.at[step, 0], (ix, iy, up)),
            (has_down, zs.at[step, 1], zr.at[step, 1], (ix, iy, down)),
            (has_up, edges.at[1], far.at[1], (ox, iy, up)),
            (has_down, edges.at[2], far.at[2], (ox, iy, down)),
            (has_up, edges.at[3], far.at[3], (ix, oy, up)),
            (has_down, edges.at[4], far.at[4], (ix, oy, down)),
            (has_up, edges.at[5], far.at[5], (ox, oy, up)),
            (has_down, edges.at[6], far.at[6], (ox, oy, down)),
        ]

        def copy(m):
            _, src, dst, target = table[m]
            return pltpu.make_async_remote_copy(
                src_ref=src, dst_ref=dst, send_sem=send_sem.at[step, m], recv_sem=recv_sem.at[step, m],
                device_id=target, device_id_type=MESH,
            )

        return [row[0] for row in table], copy

    def guarded(condition, action):
        if condition is None:
            action()
        else:
            pl.when(condition)(action)

    def start(step, which):
        conditions, copy = messages(step)
        for m in which:
            guarded(conditions[m], lambda: copy(m).start())

    def arrive(step, which):
        _, copy = messages(step)
        for m in which:
            condition = None if m < 3 else has_down if m % 2 == 1 else has_up
            guarded(condition, lambda: copy(m).wait_recv())

    def pack_and_send(step):
        row = jnp.where(ix == 0, 39, 8)
        yh1 = 1 + 3 * oy
        z = lax.bitwise_and(lane, 15)
        group = lax.shift_right_logical(lane, 4)
        slots = [group == lax.rem(7 * oy - xo + 8, 8) for xo in range(4)]
        own_half = jnp.logical_or(jnp.logical_or(slots[0], slots[1]), jnp.logical_or(slots[2], slots[3]))

        halves = []
        for d in range(9):
            cz, cx = d // 3, d % 3
            i = 9 * cx + 6 * oy + cz
            acc = None
            for xo in range(4):
                value = roll(coll[pl.ds(pl.multiple_of(crow(i, yh1, 8 + 8 * xo), 8), 8), :], -16 * xo)
                acc = value if acc is None else jnp.where(slots[xo], value, acc)
            halves.append(acc)

        def merge(values, step_of, home):
            acc = values[0]
            for k in (1, 2):
                acc = jnp.where(z == home + k * step_of, roll(values[k], k * step_of), acc)
            return acc

        es[step, 3] = merge(halves[6:9], -1, 15)
        es[step, 4] = merge(halves[0:3], 1, 0)
        start(step, (7, 8))
        for v in range(5):
            tile = halves[2 * v]
            if v < 4:
                tile = jnp.where(own_half, tile, roll(halves[2 * v + 1], -64))
            ys[step, v] = tile
        start(step, (1,))

        def pack_z(m, c):
            up, down = None, None
            for k in range(16):
                yh, xo = k // 4, k % 4
                high = coll[pl.ds(pl.multiple_of(crow(3 * m + 2, yh + 1, 8 + 8 * xo), 8), 8), :]
                low = coll[pl.ds(pl.multiple_of(crow(3 * m, yh + 1, 8 + 8 * xo), 8), 8), :]
                high, low = roll(high, -k), roll(low, k)
                z = lax.bitwise_and(lane, 15)
                up = high if up is None else jnp.where(z == 15 - k, high, up)
                down = low if down is None else jnp.where(z == k, low, down)
            zs[step, 0, m] = up
            zs[step, 1, m] = down
            return c

        lax.fori_loop(0, 9, pack_z, 0, unroll=3)
        start(step, (3, 4))

        for cz in range(3):
            es[step, 0, cz : cz + 1] = coll[pl.ds(crow(18 * ox + 6 * oy + cz, yh1, row), 1), :]
        for side in range(2):
            es[step, 5 + side, 0:1] = coll[pl.ds(crow(18 * ox + 6 * oy + 2 - 2 * side, yh1, row), 1), :]
        start(step, (9, 10, 2))
        for cz in range(3):
            for cy in range(3):
                xs[step, cz, cy, 0:4] = coll[pl.ds(crow(18 * ox + 3 * cy + cz, 1, row), 4, stride=48), :]
        es[step, 1] = merge([xs[step, 2, cy] for cy in range(3)], -1, 15)
        es[step, 2] = merge([xs[step, 0, cy] for cy in range(3)], 1, 0)
        start(step, (5, 6))

        start(step, (0,))

    def receive(step):
        rowx = jnp.where(ix == 0, 40, 7)
        edge = 5 * oy
        arrive(step, (0,))
        for cz in range(3):
            for cy in range(3):
                coll[pl.ds(crow(18 * ix + 3 * cy + cz, 1, rowx), 4, stride=48), :] = xr[step, cz, cy, 0:4]

        def take_z(m, c):
            below, above = zr[step, 0, m], zr[step, 1, m]
            for k in range(16):
                yh, xo = k // 4, k % 4
                zhalo[pl.ds(pl.multiple_of(crow(m, yh + 1, 8 + 8 * xo), 8), 8), :] = roll(below, k - 16)
                zhalo[pl.ds(pl.multiple_of(crow(9 + m, yh + 1, 8 + 8 * xo), 8), 8), :] = roll(above, 16 - k)
            return c

        if step == 0:
            know_wait(0)
            know_signal(1)
        arrive(step, (3, 4))
        lax.fori_loop(0, 9, take_z, 0, unroll=3)
        arrive(step, (1,))
        for d in range(9):
            cz, cx = d // 3, d % 3
            i = 9 * cx + 6 * iy + cz
            value = yr[step, d // 2]
            for xo in range(4):
                coll[pl.ds(pl.multiple_of(crow(i, edge, 8 + 8 * xo), 8), 8), :] = roll(value, 16 * xo + 64 * (d % 2))
        arrive(step, (2,))
        for cz in range(3):
            coll[pl.ds(crow(18 * ix + 6 * iy + cz, edge, rowx), 1), :] = er[step, 0, cz : cz + 1]
        arrive(step, (5, 6, 7, 8, 9, 10))
        for side in range(2):
            sign = 1 - 2 * side
            value = er[step, 3 + side]
            for cx in range(3):
                m = 9 * side + 3 * cx + 2 * iy
                for xo in range(4):
                    zhalo[pl.ds(pl.multiple_of(crow(m, edge, 8 + 8 * xo), 8), 8), :] = roll(
                        value, sign * (cx - 16) + 16 * xo
                    )
            value = er[step, 1 + side]
            for cy in range(3):
                m = 9 * side + 6 * ix + cy
                zhalo[pl.ds(crow(m, 1, rowx), 4, stride=48), :] = roll(value, sign * (cy - 16))[0:4]
            m = 9 * side + 6 * ix + 2 * iy
            zhalo[pl.ds(crow(m, edge, rowx), 1), :] = roll(er[step, 5 + side], -16 * sign)[0:1]

    def propagate_tile(yh, x0, store):
        z15 = lax.bitwise_and(lane, 15) == 15
        z0 = lax.bitwise_and(lane, 15) == 0
        for i in range(27):
            cx, cy, cz = velocity(i)
            here = 8 + x0 - cx
            value = coll[pl.ds(crow(i, yh + 1, here), 8), :]
            if cy:
                other = coll[pl.ds(crow(i, yh + 1 - cy, here), 8), :]
                value = jnp.where(lane >= 112 if cy > 0 else lane < 16, other, value)
            if cz:
                m = i // 3 + (0 if cz > 0 else 9)
                halo = zhalo[pl.ds(crow(m, yh + 1, here), 8), :]
                if cy:
                    other = zhalo[pl.ds(crow(m, yh + 1 - cy, here), 8), :]
                    if cz > 0:
                        at = 111 if cy > 0 else 127
                    else:
                        at = 0 if cy > 0 else 16
                    halo = jnp.where(lane == at, other, halo)
                value = jnp.where(z15 if cz > 0 else z0, halo, value)
            value = roll(value, 16 * cy + cz)
            if i != 13:
                back = coll[pl.ds(crow(26 - i, yh + 1, 8 + x0), 8), :]
                value = jnp.where(value > EDGE, value, back)
            store(i, value)

    def propagate():
        def tile(t, c):
            yh, x0 = t // 4, 8 * lax.rem(t, 4)

            def store(i, value):
                fin[pl.ds(pl.multiple_of(grow(i, yh, x0), 8), 8), :] = value

            propagate_tile(yh, x0, store)
            return c

        lax.fori_loop(0, 16, tile, 0, unroll=2)

    for load in loads[1:]:
        load.wait()
    collide(0)
    pl.semaphore_wait(bar, 10 + 4 * jnp.where(has_down, 1, 0) + 4 * jnp.where(has_up, 1, 0))
    know_signal(0)
    pack_and_send(0)
    receive(0)
    know_wait(1)
    know_signal(2)
    propagate()
    collide(1)
    pack_and_send(1)

    leaving = 0
    for s in range(4):
        target = tgt_ref[s, device]
        away = jnp.where(target >= 0, jnp.where(lax.shift_right_arithmetic(target, 2) == device, 0, 1), 0)
        leaving = jnp.where(away == 1, jnp.clip(list_ref[s, device], 0, 3), leaving)

    def leave_to(buffer):
        def tile(t, c):
            yhi, xh = t // 2, lax.rem(t, 2)
            yh = 2 * lax.rem(leaving, 2) + yhi
            x0 = 16 * (leaving // 2) + 8 * xh

            def store(i, value):
                buffer[2 * i + yhi, pl.ds(pl.multiple_of(8 * xh, 8), 8), :] = value

            propagate_tile(yh, x0, store)
            return c

        lax.fori_loop(0, 4, tile, 0, unroll=2)

    leave_to(leave)
    know_wait(2)

    def piece_of(t):
        return t - (t + ix) // 6, lax.rem(t + ix, 6) != 5

    def spread(k, c):
        t = lax.bitwise_xor(me, ROW - k)
        piece, used = piece_of(t)

        @pl.when(used)
        def _():
            pltpu.make_async_remote_copy(
                src_ref=leave.at[piece], dst_ref=buf1.at[me], send_sem=s1, recv_sem=r1,
                device_id=(ix, t // GZ, lax.rem(t, GZ)), device_id_type=MESH,
            ).start()

        return c

    lax.fori_loop(1, ROW, spread, 0)
    receive(1)

    leave_to(leave2)
    group = lax.shift_right_logical(lane, 4)
    z = lax.bitwise_and(lane, 15)

    def put(tile, value):
        bnd[tile // 2, 8 * (tile % 2) : 8 * (tile % 2) + 8] = value

    for q, (i, yhi) in enumerate(FACES_X):
        x = 0 if velocity(i)[0] > 0 else 15
        bnd[q // 16, q % 16 : q % 16 + 1] = leave2[2 * i + yhi, x : x + 1]
    for tile in range(5):
        acc = None
        for slot, (i, xh) in enumerate(FACES_Y[8 * tile : 8 * tile + 8]):
            home, yhi = (0, 0) if velocity(i)[1] > 0 else (7, 1)
            value = roll(leave2[2 * i + yhi, 8 * xh : 8 * xh + 8], 16 * (slot - home))
            acc = value if acc is None else jnp.where(group == slot, value, acc)
        put(5 + tile, acc)
    for tile in range(5):
        acc = None
        for slot, (i, yhi, xh) in enumerate(FACES_Z[16 * tile : 16 * tile + 16]):
            home = 0 if velocity(i)[2] > 0 else 15
            value = roll(leave2[2 * i + yhi, 8 * xh : 8 * xh + 8], slot - home)
            acc = value if acc is None else jnp.where(z == slot, value, acc)
        put(10 + tile, acc)
    put(15, acc)

    def edge_spread(b, c):
        t = 6 * b + 5 - ix

        @pl.when(t != me)
        def _():
            pltpu.make_async_remote_copy(
                src_ref=bnd.at[b], dst_ref=buf1.at[me], send_sem=s3, recv_sem=r3,
                device_id=(ix, t // GZ, lax.rem(t, GZ)), device_id_type=MESH,
            ).start()

        return c

    lax.fori_loop(0, EDGE_PIECES, edge_spread, 0)

    def keep_tile(t, c):
        s, yhi, xh = t // 4, lax.rem(t // 2, 2), lax.rem(t, 2)
        pos, stays = 0, 0
        for k in range(4):
            match = tgt_ref[k, device] == device * 4 + s
            pos = jnp.where(match, jnp.clip(list_ref[k, device], 0, 3), pos)
            stays = jnp.where(match, 1, stays)
        there = jnp.full((8, 128), stays, jnp.int32) > 0

        def store(i, value):
            kept[pl.ds(raw_row(i, s, yhi, 8 * xh), 8, stride=8), :] = jnp.where(there, value, 0.0)

        propagate_tile(2 * lax.rem(pos, 2) + yhi, 16 * (pos // 2) + 8 * xh, store)
        return c

    lax.fori_loop(0, 16, keep_tile, 0)
    keep_copy = pltpu.make_async_copy(kept, kept_out, load_sem.at[0])
    keep_copy.start()
    src_copy.wait()
    own, passes = piece_of(me)
    own_edge = (me + ix) // 6
    relays = jnp.logical_and(jnp.logical_not(passes), own_edge < EDGE_PIECES)

    def count(buffer, n, sem):
        pltpu.make_async_copy(buffer.at[pl.ds(0, n)], buffer.at[pl.ds(0, n)], sem).wait()

    def relay(dst, send, recv):
        def forward(k, c):
            t = lax.bitwise_xor(me, ROW - k)
            source = srcs[lax.rem(t, 8), t // 8]
            buf2[t] = buf1[jnp.clip(source - ix * ROW, 0, ROW - 1)]
            pltpu.make_async_remote_copy(
                src_ref=buf2.at[t], dst_ref=dst, send_sem=send, recv_sem=recv,
                device_id=(ix, t // GZ, lax.rem(t, GZ)), device_id_type=MESH,
            ).start()
            return c

        lax.fori_loop(1, ROW, forward, 0)
        buf2[me] = buf1[jnp.clip(srcs[lax.rem(me, 8), me // 8] - ix * ROW, 0, ROW - 1)]
        mine = pltpu.make_async_copy(buf2.at[me], dst, load_sem.at[1])
        mine.start()
        mine.wait()

    @pl.when(passes)
    def _():
        buf1[me] = leave[own]
        count(buf1, ROW - 1, r1)
        relay(got.at[own], s2, r2)
        count(got, PIECES - 1, r2)
        count(got, EDGE_PIECES, r4)
        count(buf2, ROW - 1, s2)
        count(leave, PIECES - 1, s1)
        count(leave, EDGE_PIECES, s3)

    @pl.when(relays)
    def _():
        buf1[me] = bnd[own_edge]
        count(buf1, ROW - 1, r3)
        relay(edge_got.at[own_edge], s4, r4)
        count(got, PIECES, r2)
        count(got, EDGE_PIECES - 1, r4)
        count(buf2, ROW - 1, s4)
        count(leave, PIECES, s1)
        count(leave, EDGE_PIECES - 1, s3)

    @pl.when(jnp.logical_not(jnp.logical_or(passes, relays)))
    def _():
        count(got, PIECES, r2)
        count(got, EDGE_PIECES, r4)
        count(leave, PIECES, s1)
        count(leave, EDGE_PIECES, s3)

    keep_copy.wait()
    for step in range(STEPS):
        conditions, copy = messages(step)
        for m, condition in enumerate(conditions):
            guarded(condition, lambda: copy(m).wait_send())


def finish_kernel(kept_in, got_in, edge_in, tgt_in, out_ref, rows, got, edge, tgt_ref, sem, out_sem):
    parts = 3
    size = 3456 // parts
    device = (lax.axis_index("gx") * 2 + lax.axis_index("gy")) * GZ + lax.axis_index("gz")
    table = pltpu.make_async_copy(tgt_in, tgt_ref, sem.at[5])
    table.start()
    a = pltpu.make_async_copy(edge_in, edge, sem.at[0])
    b = pltpu.make_async_copy(got_in, got, sem.at[1])
    a.start()
    b.start()
    reads = [
        pltpu.make_async_copy(kept_in.at[pl.ds(k * size, size)], rows.at[pl.ds(k * size, size)], sem.at[2 + k])
        for k in range(parts)
    ]
    writes = [
        pltpu.make_async_copy(rows.at[pl.ds(k * size, size)], out_ref.at[pl.ds(k * size, size)], out_sem.at[k])
        for k in range(parts)
    ]
    for read in reads:
        read.start()
    table.wait()
    tg = tgt_ref[...]
    comes = jnp.logical_and(lax.shift_right_arithmetic(tg, 2) == device, lanes((4, 128)) != device)
    slot = jnp.max(jnp.where(comes, lax.bitwise_and(tg, 3), -1).astype(F32)).astype(jnp.int32)
    at_slot = jnp.clip(slot, 0, 3)
    a.wait()
    b.wait()
    lane = lanes()
    group = lax.shift_right_logical(lane, 4)
    z = lax.bitwise_and(lane, 15)
    sub = lax.broadcasted_iota(jnp.int32, (8, 128), 0)

    def face(tile):
        return edge[tile // 2, 8 * (tile % 2) : 8 * (tile % 2) + 8]

    for k in range(parts):
        reads[k].wait()

        @pl.when(slot >= 0)
        def _():
            for i in range(9 * k, 9 * k + 9):
                cx, cy, cz = velocity(i)
                for yhi in range(2):
                    for xh in range(2):
                        value = got[2 * i + yhi, 8 * xh : 8 * xh + 8]
                        if cz:
                            q = FACES_Z.index((i, yhi, xh))
                            home = 0 if cz > 0 else 15
                            value = jnp.where(z == home, roll(face(10 + q // 16), home - q % 16), value)
                        if cy and yhi == (0 if cy > 0 else 1):
                            q = FACES_Y.index((i, xh))
                            home = 0 if cy > 0 else 7
                            value = jnp.where(group == home, roll(face(5 + q // 8), 16 * (home - q % 8)), value)
                        if cx and xh == (0 if cx > 0 else 1):
                            q = FACES_X.index((i, yhi))
                            line = jnp.broadcast_to(edge[q // 16, q % 16 : q % 16 + 1], (8, 128))
                            value = jnp.where(sub == (0 if cx > 0 else 7), line, value)
                        rows[pl.ds((i * 32 + 16 * xh + yhi) * 4 + at_slot, 8, stride=8), :] = value

        writes[k].start()
    for write in writes:
        write.wait()


def body(populations, solid, block_list, targets):
    vmem = pltpu.VMEM
    tile = (8, 128)
    rows = populations.reshape(4, 27, 32, 128).transpose(1, 2, 0, 3).reshape(27 * 32 * 4, 128)
    cells = solid.reshape(4, 32, 128).transpose(1, 0, 2).reshape(32 * 4, 128)
    kept, got, edge = pl.pallas_call(
        kernel,
        out_shape=[
            jax.ShapeDtypeStruct((27 * 32 * 4, 128), F32),
            jax.ShapeDtypeStruct((PIECES, 16, 128), F32),
            jax.ShapeDtypeStruct((EDGE_PIECES, 16, 128), F32),
        ],
        in_specs=[pl.BlockSpec(memory_space=pl.ANY)] * 4,
        out_specs=[pl.BlockSpec(memory_space=pl.ANY)] * 3,
        scratch_shapes=[
            vmem((128, 128), F32),
            pltpu.SMEM((4, 128), jnp.int32),
            pltpu.SMEM((4, 128), jnp.int32),
            vmem((4, 128), jnp.int32),
            vmem((27 * 32 * 4, 128), F32),
            vmem((27 * 6 * 48, 128), F32),
            vmem((18 * 6 * 48, 128), F32),
            vmem((27 * 4 * 32, 128), F32),
            vmem((27 * 4 * 32, 128), F32),
            vmem((PIECES, 16, 128), F32),
            vmem((PIECES, 16, 128), F32),
            vmem((EDGE_PIECES, 16, 128), F32),
            vmem((ROW, 16, 128), F32),
            vmem((ROW, 16, 128), F32),
            vmem(tile, jnp.int32),
            pltpu.SMEM(tile, jnp.int32),
            vmem((2, 3, 3) + tile, F32),
            vmem((2, 5) + tile, F32),
            vmem((2, 2, 9) + tile, F32),
            vmem((2, 7) + tile, F32),
            vmem((2, 3, 3) + tile, F32),
            vmem((2, 5) + tile, F32),
            vmem((2, 2, 9) + tile, F32),
            vmem((2, 7) + tile, F32),
            pltpu.SemaphoreType.DMA((5,)),
            pltpu.SemaphoreType.DMA,
            pltpu.SemaphoreType.REGULAR((3,)),
            pltpu.SemaphoreType.DMA((STEPS, 11)),
            pltpu.SemaphoreType.DMA((STEPS, 11)),
            pltpu.SemaphoreType.DMA,
            pltpu.SemaphoreType.DMA,
            pltpu.SemaphoreType.DMA,
            pltpu.SemaphoreType.DMA,
            pltpu.SemaphoreType.DMA,
            pltpu.SemaphoreType.DMA,
            pltpu.SemaphoreType.DMA,
            pltpu.SemaphoreType.DMA,
        ],
        compiler_params=pltpu.CompilerParams(
            collective_id=0, has_side_effects=True, vmem_limit_bytes=58 * 1024 * 1024
        ),
        name="lattice",
    )(rows, cells, block_list.T, targets.T)
    out = pl.pallas_call(
        finish_kernel,
        out_shape=jax.ShapeDtypeStruct((27 * 32 * 4, 128), F32),
        in_specs=[pl.BlockSpec(memory_space=pl.ANY)] * 4,
        out_specs=pl.BlockSpec(memory_space=pl.ANY),
        scratch_shapes=[
            vmem((27 * 32 * 4, 128), F32),
            vmem((PIECES, 16, 128), F32),
            vmem((EDGE_PIECES, 16, 128), F32),
            vmem((4, 128), jnp.int32),
            pltpu.SemaphoreType.DMA((6,)),
            pltpu.SemaphoreType.DMA((3,)),
        ],
        compiler_params=pltpu.CompilerParams(vmem_limit_bytes=58 * 1024 * 1024),
        name="finish",
    )(kept, got, edge, targets.T)
    return out.reshape(27, 32, 4, 128).transpose(2, 0, 1, 3).reshape(4, 27, 4096)


def solution(mesh):
    in_specs = (P(("gx", "gy", "gz"), None, None), P(("gx", "gy", "gz"), None), P(), P())
    out_specs = P(("gx", "gy", "gz"), None, None)
    return jax.shard_map(body, mesh=mesh, in_specs=in_specs, out_specs=out_specs, check_vma=False)
```

```python
import jax
import jax.numpy as jnp
from jax import lax
from jax.experimental import pallas as pl
from jax.experimental.pallas import tpu as pltpu
from jax.sharding import PartitionSpec as P

STEPS = 2
GZ = 32
ROW = 64
PIECES = 54
ABSENT = -1.0e30
EDGE = -1.0e29
W0, W1, W2, W3 = 8.0 / 27.0, 2.0 / 27.0, 1.0 / 54.0, 1.0 / 216.0
OMEGA = 0.8
MESH = pl.DeviceIdType.MESH
F32 = jnp.float32


def velocity(i):
    return (i // 9 - 1, (i // 3) % 3 - 1, i % 3 - 1)


def crow(i, yh1, x8):
    return (i * 6 + yh1) * 48 + x8


def grow(i, yh, x):
    return (i * 4 + yh) * 32 + x


DIRS = range(27)
FACES_X = [(i, yhi) for i in DIRS if velocity(i)[0] for yhi in range(2)]
FACES_Y = [(i, xh) for i in DIRS if velocity(i)[1] for xh in range(2)]
FACES_Z = [(i, yhi, xh) for i in DIRS if velocity(i)[2] for yhi in range(2) for xh in range(2)]
EDGE_PIECES = 8


def lanes(shape=(8, 128)):
    return lax.broadcasted_iota(jnp.int32, shape, 1)


def roll(value, shift):
    shift = shift % 128
    return value if shift == 0 else pltpu.roll(value, shift, 1)


def collide_tile(load, n, store):
    s, d = {}, {}
    g13 = load(13)
    for j in range(14, 27):
        up, down = load(j), load(26 - j)
        s[j] = up + down
        d[j] = up - down
    level = {1: [], 2: [], 3: []}
    for j in range(14, 27):
        level[sum(abs(c) for c in velocity(j))].append(j)

    def total(values):
        values = list(values)
        while len(values) > 1:
            values = [values[k] + values[k + 1] if k + 1 < len(values) else values[k] for k in range(0, len(values), 2)]
        return values[0]

    rho = W0 * g13 + W1 * total(s[j] for j in level[1]) + W2 * total(s[j] for j in level[2]) + W3 * total(s[j] for j in level[3])
    momentum = []
    for axis in range(3):
        acc = None
        for lev, w in ((1, W1), (2, W2), (3, W3)):
            plus = [d[j] for j in level[lev] if velocity(j)[axis] > 0]
            minus = [d[j] for j in level[lev] if velocity(j)[axis] < 0]
            term = total(plus)
            if minus:
                term = term - total(minus)
            term = w * term
            acc = term if acc is None else acc + term
        momentum.append(acc)
    mx, my, mz = momentum
    rinv = 1.0 / rho
    fluid = 1.0 - n
    a = (1.0 - OMEGA) * fluid
    b = OMEGA * fluid
    p = 0.5 * (a + n)
    q = 0.5 * (a - n)
    e0 = b * (rho - 1.5 * rinv * (mx * mx + my * my + mz * mz))
    k = 4.5 * b * rinv
    b3 = 3.0 * b
    store(13, (a + n) * g13 + e0)
    for j in range(14, 27):
        cx, cy, cz = velocity(j)
        proj = None
        for c, m in ((cx, mx), (cy, my), (cz, mz)):
            if c:
                if proj is None:
                    proj = m if c > 0 else -m
                else:
                    proj = proj + m if c > 0 else proj - m
        even = p * s[j] + (e0 + k * (proj * proj))
        odd = q * d[j] + b3 * proj
        store(j, even + odd)
        store(26 - j, even - odd)


def kernel(
    pops_in, solid_in, list_in, tgt_in, kept_out, got, edge_got,
    solid_ref, list_ref, tgt_ref, tgtv_ref, praw, coll, zhalo, fin, kept, leave, leave2, bnd, buf1, buf2, srcv, srcs,
    xs, ys, zs, es, xr, yr, zr, er,
    load_sem, src_sem, know_sem, send_sem, recv_sem, s1, r1, s2, r2, s3, r3, s4, r4,
):
    ix, iy, iz = lax.axis_index("gx"), lax.axis_index("gy"), lax.axis_index("gz")
    me = iy * GZ + iz
    device = ix * ROW + me
    ox, oy = 1 - ix, 1 - iy
    has_down = iz > 0
    has_up = iz < GZ - 1

    pairs = ((tgt_in, tgtv_ref), (tgt_in, tgt_ref), (list_in, list_ref), (solid_in, solid_ref), (pops_in, praw))
    loads = [pltpu.make_async_copy(src, dst, load_sem.at[k]) for k, (src, dst) in enumerate(pairs)]
    for load in loads:
        load.start()

    bar = pltpu.get_barrier_semaphore()

    def greet(*target):
        pl.semaphore_signal(bar, inc=1, device_id=target, device_id_type=MESH)

    @pl.when(has_down)
    def _():
        for x in (ix, ox):
            for y in (iy, oy):
                greet(x, y, iz - 1)

    @pl.when(has_up)
    def _():
        for x in (ix, ox):
            for y in (iy, oy):
                greet(x, y, iz + 1)

    greet(ix, oy, iz)
    greet(ox, oy, iz)
    greet(ox, iy, iz)

    def flipped(bits):
        return (ix, iy, lax.bitwise_xor(iz, bits))

    rounds = [
        [flipped(1), flipped(2), flipped(3)],
        [flipped(4), flipped(8), flipped(12)],
        [(ix, oy, iz), flipped(16), (ix, oy, lax.bitwise_xor(iz, 16))],
    ]
    for bits in (2, 3, 4, 8, 12, 16):
        greet(*flipped(bits))
    greet(*rounds[2][2])

    def know_signal(r):
        for target in rounds[r]:
            pl.semaphore_signal(know_sem.at[r], inc=1, device_id=target, device_id_type=MESH)

    def know_wait(r):
        pl.semaphore_wait(know_sem.at[r], 3)

    lane = lanes()

    none = jnp.full((8, 128), ABSENT, F32)

    def clear_coll(i, c):
        for yh1 in (0, 5):
            for x in range(0, 48, 8):
                coll[pl.ds(crow(i, yh1, x), 8), :] = none
        for yh1 in range(1, 5):
            for x in (0, 40):
                coll[pl.ds(crow(i, yh1, x), 8), :] = none
        return c

    lax.fori_loop(0, 27, clear_coll, 0)

    def clear_z(i, c):
        for yh1 in (0, 5):
            for x in range(0, 48, 8):
                zhalo[pl.ds(crow(i, yh1, x), 8), :] = none
        for yh1 in range(1, 5):
            for x in (0, 40):
                zhalo[pl.ds(crow(i, yh1, x), 8), :] = none
        return c

    lax.fori_loop(0, 18, clear_z, 0)
    for side, missing in ((0, iz == 0), (1, iz == GZ - 1)):

        @pl.when(missing)
        def _():
            for step in range(STEPS):
                for m in range(9):
                    zr[step, side, m] = none
                for m in (1, 3, 5):
                    er[step, m + side] = none

    loads[0].wait()
    tg = tgtv_ref[...]
    sender = lanes((4, 128))
    tdev = jnp.where(tg >= 0, lax.shift_right_arithmetic(tg, 2), -1)
    tdev = jnp.where(tdev == sender, -1, tdev) - ix * ROW
    table = jnp.full((8, 128), -1, jnp.int32)
    for t8 in range(8):
        rows = lax.broadcasted_iota(jnp.int32, (8, 128), 0) + 8 * t8
        best = jnp.full((8, 128), -1, jnp.int32)
        for s in range(4):
            best = jnp.where(tdev[s : s + 1] == rows, lane, best)
        for shift in (64, 32, 16, 8, 4, 2, 1):
            best = jnp.maximum(best, pltpu.roll(best, shift, 1))
        table = jnp.where(lane == t8, best, table)
    srcv[...] = table
    src_copy = pltpu.make_async_copy(srcv, srcs, src_sem)
    src_copy.start()

    def raw_row(i, slot, yhi, x):
        return (i * 32 + 2 * x + yhi) * 4 + slot

    def slot_of(p):
        slot, there = 0, 0
        for s in range(4):
            match = list_ref[s, device] == p
            slot = jnp.where(match, s, slot)
            there = jnp.where(match, 1, there)
        return slot, there

    def collide(step):
        def tile(t, c):
            p, yhi, xh = t // 4, lax.rem(t // 2, 2), lax.rem(t, 2)
            slot, there = slot_of(p)
            yh = 2 * lax.rem(p, 2) + yhi
            x0 = 16 * (p // 2) + 8 * xh
            inside = jnp.full((8, 128), there, jnp.int32) > 0
            n = solid_ref[pl.ds(raw_row(0, slot, yhi, 8 * xh), 8, stride=8), :]
            if step == 0:
                def load(i):
                    return praw[pl.ds(raw_row(i, slot, yhi, 8 * xh), 8, stride=8), :]
            else:
                def load(i):
                    return fin[pl.ds(grow(i, yh, x0), 8), :]

            def store(i, value):
                coll[pl.ds(pl.multiple_of(crow(i, yh + 1, 8 + x0), 8), 8), :] = jnp.where(inside, value, ABSENT)

            collide_tile(load, n, store)
            return c

        lax.fori_loop(0, 16, tile, 0, unroll=2)

    def messages(step):
        down, up = iz - 1, iz + 1
        edges, far = es.at[step], er.at[step]
        table = [
            (None, xs.at[step], xr.at[step], (ox, iy, iz)),
            (None, ys.at[step], yr.at[step], (ix, oy, iz)),
            (None, edges.at[0], far.at[0], (ox, oy, iz)),
            (has_up, zs.at[step, 0], zr.at[step, 0], (ix, iy, up)),
            (has_down, zs.at[step, 1], zr.at[step, 1], (ix, iy, down)),
            (has_up, edges.at[1], far.at[1], (ox, iy, up)),
            (has_down, edges.at[2], far.at[2], (ox, iy, down)),
            (has_up, edges.at[3], far.at[3], (ix, oy, up)),
            (has_down, edges.at[4], far.at[4], (ix, oy, down)),
            (has_up, edges.at[5], far.at[5], (ox, oy, up)),
            (has_down, edges.at[6], far.at[6], (ox, oy, down)),
        ]

        def copy(m):
            _, src, dst, target = table[m]
            return pltpu.make_async_remote_copy(
                src_ref=src, dst_ref=dst, send_sem=send_sem.at[step, m], recv_sem=recv_sem.at[step, m],
                device_id=target, device_id_type=MESH,
            )

        return [row[0] for row in table], copy

    def guarded(condition, action):
        if condition is None:
            action()
        else:
            pl.when(condition)(action)

    def start(step, which):
        conditions, copy = messages(step)
        for m in which:
            guarded(conditions[m], lambda: copy(m).start())

    def arrive(step, which):
        _, copy = messages(step)
        for m in which:
            condition = None if m < 3 else has_down if m % 2 == 1 else has_up
            guarded(condition, lambda: copy(m).wait_recv())

    def pack_and_send(step):
        row = jnp.where(ix == 0, 39, 8)
        yh1 = 1 + 3 * oy
        z = lax.bitwise_and(lane, 15)
        group = lax.shift_right_logical(lane, 4)
        slots = [group == lax.rem(7 * oy - xo + 8, 8) for xo in range(4)]
        own_half = jnp.logical_or(jnp.logical_or(slots[0], slots[1]), jnp.logical_or(slots[2], slots[3]))

        halves = []
        for d in range(9):
            cz, cx = d // 3, d % 3
            i = 9 * cx + 6 * oy + cz
            acc = None
            for xo in range(4):
                value = roll(coll[pl.ds(pl.multiple_of(crow(i, yh1, 8 + 8 * xo), 8), 8), :], -16 * xo)
                acc = value if acc is None else jnp.where(slots[xo], value, acc)
            halves.append(acc)

        def merge(values, step_of, home):
            acc = values[0]
            for k in (1, 2):
                acc = jnp.where(z == home + k * step_of, roll(values[k], k * step_of), acc)
            return acc

        es[step, 3] = merge(halves[6:9], -1, 15)
        es[step, 4] = merge(halves[0:3], 1, 0)
        start(step, (7, 8))
        for v in range(5):
            tile = halves[2 * v]
            if v < 4:
                tile = jnp.where(own_half, tile, roll(halves[2 * v + 1], -64))
            ys[step, v] = tile
        start(step, (1,))

        def pack_z(m, c):
            up, down = None, None
            for k in range(16):
                yh, xo = k // 4, k % 4
                high = coll[pl.ds(pl.multiple_of(crow(3 * m + 2, yh + 1, 8 + 8 * xo), 8), 8), :]
                low = coll[pl.ds(pl.multiple_of(crow(3 * m, yh + 1, 8 + 8 * xo), 8), 8), :]
                high, low = roll(high, -k), roll(low, k)
                z = lax.bitwise_and(lane, 15)
                up = high if up is None else jnp.where(z == 15 - k, high, up)
                down = low if down is None else jnp.where(z == k, low, down)
            zs[step, 0, m] = up
            zs[step, 1, m] = down
            return c

        lax.fori_loop(0, 9, pack_z, 0, unroll=3)
        start(step, (3, 4))

        for cz in range(3):
            es[step, 0, cz : cz + 1] = coll[pl.ds(crow(18 * ox + 6 * oy + cz, yh1, row), 1), :]
        for side in range(2):
            es[step, 5 + side, 0:1] = coll[pl.ds(crow(18 * ox + 6 * oy + 2 - 2 * side, yh1, row), 1), :]
        start(step, (9, 10, 2))
        for cz in range(3):
            for cy in range(3):
                xs[step, cz, cy, 0:4] = coll[pl.ds(crow(18 * ox + 3 * cy + cz, 1, row), 4, stride=48), :]
        es[step, 1] = merge([xs[step, 2, cy] for cy in range(3)], -1, 15)
        es[step, 2] = merge([xs[step, 0, cy] for cy in range(3)], 1, 0)
        start(step, (5, 6))

        start(step, (0,))

    def receive(step):
        rowx = jnp.where(ix == 0, 40, 7)
        edge = 5 * oy
        arrive(step, (0,))
        for cz in range(3):
            for cy in range(3):
                coll[pl.ds(crow(18 * ix + 3 * cy + cz, 1, rowx), 4, stride=48), :] = xr[step, cz, cy, 0:4]

        def take_z(m, c):
            below, above = zr[step, 0, m], zr[step, 1, m]
            for k in range(16):
                yh, xo = k // 4, k % 4
                zhalo[pl.ds(pl.multiple_of(crow(m, yh + 1, 8 + 8 * xo), 8), 8), :] = roll(below, k - 16)
                zhalo[pl.ds(pl.multiple_of(crow(9 + m, yh + 1, 8 + 8 * xo), 8), 8), :] = roll(above, 16 - k)
            return c

        if step == 0:
            know_wait(0)
            know_signal(1)
        arrive(step, (3, 4))
        lax.fori_loop(0, 9, take_z, 0, unroll=3)
        arrive(step, (1,))
        for d in range(9):
            cz, cx = d // 3, d % 3
            i = 9 * cx + 6 * iy + cz
            value = yr[step, d // 2]
            for xo in range(4):
                coll[pl.ds(pl.multiple_of(crow(i, edge, 8 + 8 * xo), 8), 8), :] = roll(value, 16 * xo + 64 * (d % 2))
        arrive(step, (2,))
        for cz in range(3):
            coll[pl.ds(crow(18 * ix + 6 * iy + cz, edge, rowx), 1), :] = er[step, 0, cz : cz + 1]
        arrive(step, (5, 6, 7, 8, 9, 10))
        for side in range(2):
            sign = 1 - 2 * side
            value = er[step, 3 + side]
            for cx in range(3):
                m = 9 * side + 3 * cx + 2 * iy
                for xo in range(4):
                    zhalo[pl.ds(pl.multiple_of(crow(m, edge, 8 + 8 * xo), 8), 8), :] = roll(
                        value, sign * (cx - 16) + 16 * xo
                    )
            value = er[step, 1 + side]
            for cy in range(3):
                m = 9 * side + 6 * ix + cy
                zhalo[pl.ds(crow(m, 1, rowx), 4, stride=48), :] = roll(value, sign * (cy - 16))[0:4]
            m = 9 * side + 6 * ix + 2 * iy
            zhalo[pl.ds(crow(m, edge, rowx), 1), :] = roll(er[step, 5 + side], -16 * sign)[0:1]

    def propagate_tile(yh, x0, store):
        z15 = lax.bitwise_and(lane, 15) == 15
        z0 = lax.bitwise_and(lane, 15) == 0
        for i in range(27):
            cx, cy, cz = velocity(i)
            here = 8 + x0 - cx
            value = coll[pl.ds(crow(i, yh + 1, here), 8), :]
            if cy:
                other = coll[pl.ds(crow(i, yh + 1 - cy, here), 8), :]
                value = jnp.where(lane >= 112 if cy > 0 else lane < 16, other, value)
            if cz:
                m = i // 3 + (0 if cz > 0 else 9)
                halo = zhalo[pl.ds(crow(m, yh + 1, here), 8), :]
                if cy:
                    other = zhalo[pl.ds(crow(m, yh + 1 - cy, here), 8), :]
                    if cz > 0:
                        at = 111 if cy > 0 else 127
                    else:
                        at = 0 if cy > 0 else 16
                    halo = jnp.where(lane == at, other, halo)
                value = jnp.where(z15 if cz > 0 else z0, halo, value)
            value = roll(value, 16 * cy + cz)
            if i != 13:
                back = coll[pl.ds(crow(26 - i, yh + 1, 8 + x0), 8), :]
                value = jnp.where(value > EDGE, value, back)
            store(i, value)

    def propagate():
        def tile(t, c):
            yh, x0 = t // 4, 8 * lax.rem(t, 4)

            def store(i, value):
                fin[pl.ds(pl.multiple_of(grow(i, yh, x0), 8), 8), :] = value

            propagate_tile(yh, x0, store)
            return c

        lax.fori_loop(0, 16, tile, 0, unroll=2)

    for load in loads[1:]:
        load.wait()
    collide(0)
    pl.semaphore_wait(bar, 10 + 4 * jnp.where(has_down, 1, 0) + 4 * jnp.where(has_up, 1, 0))
    know_signal(0)
    pack_and_send(0)
    receive(0)
    know_wait(1)
    know_signal(2)
    propagate()
    collide(1)
    pack_and_send(1)

    leaving = 0
    for s in range(4):
        target = tgt_ref[s, device]
        away = jnp.where(target >= 0, jnp.where(lax.shift_right_arithmetic(target, 2) == device, 0, 1), 0)
        leaving = jnp.where(away == 1, jnp.clip(list_ref[s, device], 0, 3), leaving)

    def leave_to(buffer):
        def tile(t, c):
            yhi, xh = t // 2, lax.rem(t, 2)
            yh = 2 * lax.rem(leaving, 2) + yhi
            x0 = 16 * (leaving // 2) + 8 * xh

            def store(i, value):
                buffer[2 * i + yhi, pl.ds(pl.multiple_of(8 * xh, 8), 8), :] = value

            propagate_tile(yh, x0, store)
            return c

        lax.fori_loop(0, 4, tile, 0, unroll=2)

    leave_to(leave)
    know_wait(2)

    def piece_of(t):
        return t - (t + ix) // 6, lax.rem(t + ix, 6) != 5

    def spread(k, c):
        t = lax.bitwise_xor(me, ROW - k)
        piece, used = piece_of(t)

        @pl.when(used)
        def _():
            pltpu.make_async_remote_copy(
                src_ref=leave.at[piece], dst_ref=buf1.at[me], send_sem=s1, recv_sem=r1,
                device_id=(ix, t // GZ, lax.rem(t, GZ)), device_id_type=MESH,
            ).start()

        return c

    lax.fori_loop(1, ROW, spread, 0)
    receive(1)

    leave_to(leave2)
    group = lax.shift_right_logical(lane, 4)
    z = lax.bitwise_and(lane, 15)

    def put(tile, value):
        bnd[tile // 2, 8 * (tile % 2) : 8 * (tile % 2) + 8] = value

    def edge_spread(b, c):
        t = 6 * b + 5 - ix

        @pl.when(t != me)
        def _():
            pltpu.make_async_remote_copy(
                src_ref=bnd.at[b], dst_ref=buf1.at[me], send_sem=s3, recv_sem=r3,
                device_id=(ix, t // GZ, lax.rem(t, GZ)), device_id_type=MESH,
            ).start()

        return c

    for q, (i, yhi) in enumerate(FACES_X):
        x = 0 if velocity(i)[0] > 0 else 15
        bnd[q // 16, q % 16 : q % 16 + 1] = leave2[2 * i + yhi, x : x + 1]
    lax.fori_loop(0, 2, edge_spread, 0)
    for tile in range(5):
        acc = None
        for slot, (i, xh) in enumerate(FACES_Y[8 * tile : 8 * tile + 8]):
            home, yhi = (0, 0) if velocity(i)[1] > 0 else (7, 1)
            value = roll(leave2[2 * i + yhi, 8 * xh : 8 * xh + 8], 16 * (slot - home))
            acc = value if acc is None else jnp.where(group == slot, value, acc)
        put(5 + tile, acc)
    lax.fori_loop(2, 5, edge_spread, 0)
    for tile in range(5):
        acc = None
        for slot, (i, yhi, xh) in enumerate(FACES_Z[16 * tile : 16 * tile + 16]):
            home = 0 if velocity(i)[2] > 0 else 15
            value = roll(leave2[2 * i + yhi, 8 * xh : 8 * xh + 8], slot - home)
            acc = value if acc is None else jnp.where(z == slot, value, acc)
        put(10 + tile, acc)
    put(15, acc)
    lax.fori_loop(5, EDGE_PIECES, edge_spread, 0)


    def keep_tile(t, c):
        s, yhi, xh = t // 4, lax.rem(t // 2, 2), lax.rem(t, 2)
        pos, stays = 0, 0
        for k in range(4):
            match = tgt_ref[k, device] == device * 4 + s
            pos = jnp.where(match, jnp.clip(list_ref[k, device], 0, 3), pos)
            stays = jnp.where(match, 1, stays)
        there = jnp.full((8, 128), stays, jnp.int32) > 0

        def store(i, value):
            kept[pl.ds(raw_row(i, s, yhi, 8 * xh), 8, stride=8), :] = jnp.where(there, value, 0.0)

        propagate_tile(2 * lax.rem(pos, 2) + yhi, 16 * (pos // 2) + 8 * xh, store)
        return c

    lax.fori_loop(0, 16, keep_tile, 0)
    keep_copy = pltpu.make_async_copy(kept, kept_out, load_sem.at[0])
    keep_copy.start()
    src_copy.wait()
    own, passes = piece_of(me)
    own_edge = (me + ix) // 6
    relays = jnp.logical_and(jnp.logical_not(passes), own_edge < EDGE_PIECES)

    def count(buffer, n, sem):
        pltpu.make_async_copy(buffer.at[pl.ds(0, n)], buffer.at[pl.ds(0, n)], sem).wait()

    def relay(dst, send, recv):
        def forward(k, c):
            t = lax.bitwise_xor(me, ROW - k)
            source = srcs[lax.rem(t, 8), t // 8]
            buf2[t] = buf1[jnp.clip(source - ix * ROW, 0, ROW - 1)]
            pltpu.make_async_remote_copy(
                src_ref=buf2.at[t], dst_ref=dst, send_sem=send, recv_sem=recv,
                device_id=(ix, t // GZ, lax.rem(t, GZ)), device_id_type=MESH,
            ).start()
            return c

        lax.fori_loop(1, ROW, forward, 0)
        buf2[me] = buf1[jnp.clip(srcs[lax.rem(me, 8), me // 8] - ix * ROW, 0, ROW - 1)]
        mine = pltpu.make_async_copy(buf2.at[me], dst, load_sem.at[1])
        mine.start()
        mine.wait()

    @pl.when(passes)
    def _():
        buf1[me] = leave[own]
        count(buf1, ROW - 1, r1)
        relay(got.at[own], s2, r2)
        count(got, PIECES - 1, r2)
        count(got, EDGE_PIECES, r4)
        count(buf2, ROW - 1, s2)
        count(leave, PIECES - 1, s1)
        count(leave, EDGE_PIECES, s3)

    @pl.when(relays)
    def _():
        buf1[me] = bnd[own_edge]
        count(buf1, ROW - 1, r3)
        relay(edge_got.at[own_edge], s4, r4)
        count(got, PIECES, r2)
        count(got, EDGE_PIECES - 1, r4)
        count(buf2, ROW - 1, s4)
        count(leave, PIECES, s1)
        count(leave, EDGE_PIECES - 1, s3)

    @pl.when(jnp.logical_not(jnp.logical_or(passes, relays)))
    def _():
        count(got, PIECES, r2)
        count(got, EDGE_PIECES, r4)
        count(leave, PIECES, s1)
        count(leave, EDGE_PIECES, s3)

    keep_copy.wait()
    for step in range(STEPS):
        conditions, copy = messages(step)
        for m, condition in enumerate(conditions):
            guarded(condition, lambda: copy(m).wait_send())


def finish_kernel(kept_in, got_in, edge_in, tgt_in, out_ref, rows, got, edge, tgt_ref, sem, out_sem):
    parts = 3
    size = 3456 // parts
    device = (lax.axis_index("gx") * 2 + lax.axis_index("gy")) * GZ + lax.axis_index("gz")
    table = pltpu.make_async_copy(tgt_in, tgt_ref, sem.at[5])
    table.start()
    a = pltpu.make_async_copy(edge_in, edge, sem.at[0])
    b = pltpu.make_async_copy(got_in, got, sem.at[1])
    a.start()
    b.start()
    reads = [
        pltpu.make_async_copy(kept_in.at[pl.ds(k * size, size)], rows.at[pl.ds(k * size, size)], sem.at[2 + k])
        for k in range(parts)
    ]
    writes = [
        pltpu.make_async_copy(rows.at[pl.ds(k * size, size)], out_ref.at[pl.ds(k * size, size)], out_sem.at[k])
        for k in range(parts)
    ]
    for read in reads:
        read.start()
    table.wait()
    tg = tgt_ref[...]
    comes = jnp.logical_and(lax.shift_right_arithmetic(tg, 2) == device, lanes((4, 128)) != device)
    slot = jnp.max(jnp.where(comes, lax.bitwise_and(tg, 3), -1).astype(F32)).astype(jnp.int32)
    at_slot = jnp.clip(slot, 0, 3)
    a.wait()
    b.wait()
    lane = lanes()
    group = lax.shift_right_logical(lane, 4)
    z = lax.bitwise_and(lane, 15)
    sub = lax.broadcasted_iota(jnp.int32, (8, 128), 0)

    def face(tile):
        return edge[tile // 2, 8 * (tile % 2) : 8 * (tile % 2) + 8]

    for k in range(parts):
        reads[k].wait()

        @pl.when(slot >= 0)
        def _():
            for i in range(9 * k, 9 * k + 9):
                cx, cy, cz = velocity(i)
                for yhi in range(2):
                    for xh in range(2):
                        value = got[2 * i + yhi, 8 * xh : 8 * xh + 8]
                        if cz:
                            q = FACES_Z.index((i, yhi, xh))
                            home = 0 if cz > 0 else 15
                            value = jnp.where(z == home, roll(face(10 + q // 16), home - q % 16), value)
                        if cy and yhi == (0 if cy > 0 else 1):
                            q = FACES_Y.index((i, xh))
                            home = 0 if cy > 0 else 7
                            value = jnp.where(group == home, roll(face(5 + q // 8), 16 * (home - q % 8)), value)
                        if cx and xh == (0 if cx > 0 else 1):
                            q = FACES_X.index((i, yhi))
                            line = jnp.broadcast_to(edge[q // 16, q % 16 : q % 16 + 1], (8, 128))
                            value = jnp.where(sub == (0 if cx > 0 else 7), line, value)
                        rows[pl.ds((i * 32 + 16 * xh + yhi) * 4 + at_slot, 8, stride=8), :] = value

        writes[k].start()
    for write in writes:
        write.wait()


def body(populations, solid, block_list, targets):
    vmem = pltpu.VMEM
    tile = (8, 128)
    rows = populations.reshape(4, 27, 32, 128).transpose(1, 2, 0, 3).reshape(27 * 32 * 4, 128)
    cells = solid.reshape(4, 32, 128).transpose(1, 0, 2).reshape(32 * 4, 128)
    kept, got, edge = pl.pallas_call(
        kernel,
        out_shape=[
            jax.ShapeDtypeStruct((27 * 32 * 4, 128), F32),
            jax.ShapeDtypeStruct((PIECES, 16, 128), F32),
            jax.ShapeDtypeStruct((EDGE_PIECES, 16, 128), F32),
        ],
        in_specs=[pl.BlockSpec(memory_space=pl.ANY)] * 4,
        out_specs=[pl.BlockSpec(memory_space=pl.ANY)] * 3,
        scratch_shapes=[
            vmem((128, 128), F32),
            pltpu.SMEM((4, 128), jnp.int32),
            pltpu.SMEM((4, 128), jnp.int32),
            vmem((4, 128), jnp.int32),
            vmem((27 * 32 * 4, 128), F32),
            vmem((27 * 6 * 48, 128), F32),
            vmem((18 * 6 * 48, 128), F32),
            vmem((27 * 4 * 32, 128), F32),
            vmem((27 * 4 * 32, 128), F32),
            vmem((PIECES, 16, 128), F32),
            vmem((PIECES, 16, 128), F32),
            vmem((EDGE_PIECES, 16, 128), F32),
            vmem((ROW, 16, 128), F32),
            vmem((ROW, 16, 128), F32),
            vmem(tile, jnp.int32),
            pltpu.SMEM(tile, jnp.int32),
            vmem((2, 3, 3) + tile, F32),
            vmem((2, 5) + tile, F32),
            vmem((2, 2, 9) + tile, F32),
            vmem((2, 7) + tile, F32),
            vmem((2, 3, 3) + tile, F32),
            vmem((2, 5) + tile, F32),
            vmem((2, 2, 9) + tile, F32),
            vmem((2, 7) + tile, F32),
            pltpu.SemaphoreType.DMA((5,)),
            pltpu.SemaphoreType.DMA,
            pltpu.SemaphoreType.REGULAR((3,)),
            pltpu.SemaphoreType.DMA((STEPS, 11)),
            pltpu.SemaphoreType.DMA((STEPS, 11)),
            pltpu.SemaphoreType.DMA,
            pltpu.SemaphoreType.DMA,
            pltpu.SemaphoreType.DMA,
            pltpu.SemaphoreType.DMA,
            pltpu.SemaphoreType.DMA,
            pltpu.SemaphoreType.DMA,
            pltpu.SemaphoreType.DMA,
            pltpu.SemaphoreType.DMA,
        ],
        compiler_params=pltpu.CompilerParams(
            collective_id=0, has_side_effects=True, vmem_limit_bytes=58 * 1024 * 1024
        ),
        name="lattice",
    )(rows, cells, block_list.T, targets.T)
    out = pl.pallas_call(
        finish_kernel,
        out_shape=jax.ShapeDtypeStruct((27 * 32 * 4, 128), F32),
        in_specs=[pl.BlockSpec(memory_space=pl.ANY)] * 4,
        out_specs=pl.BlockSpec(memory_space=pl.ANY),
        scratch_shapes=[
            vmem((27 * 32 * 4, 128), F32),
            vmem((PIECES, 16, 128), F32),
            vmem((EDGE_PIECES, 16, 128), F32),
            vmem((4, 128), jnp.int32),
            pltpu.SemaphoreType.DMA((6,)),
            pltpu.SemaphoreType.DMA((3,)),
        ],
        compiler_params=pltpu.CompilerParams(vmem_limit_bytes=58 * 1024 * 1024),
        name="finish",
    )(kept, got, edge, targets.T)
    return out.reshape(27, 32, 4, 128).transpose(2, 0, 1, 3).reshape(4, 27, 4096)


def solution(mesh):
    in_specs = (P(("gx", "gy", "gz"), None, None), P(("gx", "gy", "gz"), None), P(), P())
    out_specs = P(("gx", "gy", "gz"), None, None)
    return jax.shard_map(body, mesh=mesh, in_specs=in_specs, out_specs=out_specs, check_vma=False)
```
